32 devices in a mesh: dp: 8 (over z, core), fsdp: 4 (over y, x).
Axes of the slice: x: 2, y: 2, z: 4, core: 2. Of those that a mesh axis runs over, the one named last changes fastest.
Arguments:
- tokens: bfloat16 [32, 512, 2048], P(('dp', 'fsdp')), may hold values from -6 to 6
- cotangent: bfloat16 [32, 512, 2048], P(('dp', 'fsdp')), may hold values from -6 to 6
- doc_starts: int32 [32, 4], P(('dp', 'fsdp')), may hold values from 0 to 511, as said below
- valid_len: int32 [32], P(('dp', 'fsdp')), may hold values from 257 to 512, as said below
- w_in: float32 [2048, 8512], P('fsdp', 'dp'), may hold values from -0.125 to 0.125
- w_out: float32 [4096, 2048], P('fsdp', 'dp'), may hold values from -0.09375 to 0.09375
- norm_gain: float32 [2048], P('fsdp'), may hold values from 0.5 to 1.5
- gate_gain: float32 [4096], P('fsdp'), may hold values from 0.5 to 1.5
- conv_w: float32 [4, 4352], P(None, 'fsdp'), may hold values from -3 to 3
- conv_b: float32 [4352], P('fsdp'), may hold values from -3 to 3
- dt_bias: float32 [64], P('fsdp'), may hold values from -6.9 to -2.25
- a_log: float32 [64], P('fsdp'), may hold values from 0 to 2.77
- d_skip: float32 [64], P('fsdp'), may hold values from 0.5 to 1.5
- first_w_in: float32 [2048, 8512], P('fsdp', 'dp'), may hold values from -0.625 to 0.625
- second_w_in: float32 [2048, 8512], P('fsdp', 'dp'), may hold values from 0.01 to 0.3
- first_w_out: float32 [4096, 2048], P('fsdp', 'dp'), may hold values from -0.625 to 0.625
- second_w_out: float32 [4096, 2048], P('fsdp', 'dp'), may hold values from 0.01 to 0.3
- first_norm_gain: float32 [2048], P('fsdp'), may hold values from -0.625 to 0.625
- second_norm_gain: float32 [2048], P('fsdp'), may hold values from 0.01 to 0.3
- first_gate_gain: float32 [4096], P('fsdp'), may hold values from -0.625 to 0.625
- second_gate_gain: float32 [4096], P('fsdp'), may hold values from 0.01 to 0.3
- first_conv_w: float32 [4, 4352], P(None, 'fsdp'), may hold values from -0.625 to 0.625
- second_conv_w: float32 [4, 4352], P(None, 'fsdp'), may hold values from 0.01 to 0.3
- first_conv_b: float32 [4352], P('fsdp'), may hold values from -0.625 to 0.625
- second_conv_b: float32 [4352], P('fsdp'), may hold values from 0.01 to 0.3
- first_dt_bias: float32 [64], P('fsdp'), may hold values from -0.625 to 0.625
- second_dt_bias: float32 [64], P('fsdp'), may hold values from 0.01 to 0.3
- first_a_log: float32 [64], P('fsdp'), may hold values from -0.625 to 0.625
- second_a_log: float32 [64], P('fsdp'), may hold values from 0.01 to 0.3
- first_d_skip: float32 [64], P('fsdp'), may hold values from -0.625 to 0.625
- second_d_skip: float32 [64], P('fsdp'), may hold values from 0.01 to 0.3
Outputs:
- out_tokens: bfloat16 [32, 512, 2048], P(('dp', 'fsdp'))
- grad_tokens: float32 [32, 512, 2048], P(('dp', 'fsdp'))
- new_w_in: float32 [2048, 8512], P('fsdp', 'dp')
- new_first_w_in: float32 [2048, 8512], P('fsdp', 'dp')
- new_second_w_in: float32 [2048, 8512], P('fsdp', 'dp')
- new_w_out: float32 [4096, 2048], P('fsdp', 'dp')
- new_first_w_out: float32 [4096, 2048], P('fsdp', 'dp')
- new_second_w_out: float32 [4096, 2048], P('fsdp', 'dp')
- step_norm_gain: float32 [2048], P('fsdp')
- new_first_norm_gain: float32 [2048], P('fsdp')
- new_second_norm_gain: float32 [2048], P('fsdp')
- step_gate_gain: float32 [4096], P('fsdp')
- new_first_gate_gain: float32 [4096], P('fsdp')
- new_second_gate_gain: float32 [4096], P('fsdp')
- step_conv_w: float32 [4, 4352], P(None, 'fsdp')
- new_first_conv_w: float32 [4, 4352], P(None, 'fsdp')
- new_second_conv_w: float32 [4, 4352], P(None, 'fsdp')
- step_conv_b: float32 [4352], P('fsdp')
- new_first_conv_b: float32 [4352], P('fsdp')
- new_second_conv_b: float32 [4352], P('fsdp')
- step_dt_bias: float32 [64], P('fsdp')
- new_first_dt_bias: float32 [64], P('fsdp')
- new_second_dt_bias: float32 [64], P('fsdp')
- step_a_log: float32 [64], P('fsdp')
- new_first_a_log: float32 [64], P('fsdp')
- new_second_a_log: float32 [64], P('fsdp')
- step_d_skip: float32 [64], P('fsdp')
- new_first_d_skip: float32 [64], P('fsdp')
- new_second_d_skip: float32 [64], P('fsdp')
The draws below stay inside these ranges and needn't reach their ends.
Inputs may be any that keep to these rules, and one draw needn't show every extreme that they name: `doc_starts`: in every row the first start is 0 and the starts rise strictly; a document runs from its start to the next start or to the row's end. Tokens of a row at positions from valid_len on are padding. Some row is full and some row has the least length in every draw.
All inputs are finite; a program needn't handle non-finite values.
Results may differ from the reference program's by a relative error of at most 0.024.
The reference program's roundings to bfloat16 on the way count: a program that leaves them out, or rounds other values in their place, can miss the bound.
Values may be sent and summed in bfloat16 or wider, within the bound.
No kernel may reach another device: no remote copies, remote signals or barrier semaphores. Data moves between devices by JAX's collectives and lax.ppermute only.
A program may use at most 320 MiB of HBM per device.

```python
import math
import jax
import jax.numpy as jnp
from jax import lax

D = 2048
NH = 64
HP = 64
NS = 128
CONVW = 4
SPAN = 256
NDOC = 4
TOK_DEV = 512
DI = 4096
CONV = 4352
DPROJ = 8512
ROWS = 32
TOKENS = 16384


def draw_doc_starts(key, part):
    key = jax.random.fold_in(key, 11)
    row_keys = jax.random.split(jax.random.fold_in(key, 1), ROWS)

    def one_row(row_key):
        picks = jax.random.permutation(row_key, TOK_DEV - 1)[:NDOC - 1] + 1
        ordered = jnp.sort(picks.astype(jnp.int32))
        return jnp.concatenate([jnp.zeros((1,), jnp.int32), ordered]).astype(jnp.int32)
    starts = jax.vmap(one_row)(row_keys)
    chosen = jax.random.randint(jax.random.fold_in(key, 2), (), 0, ROWS)
    column_index = jnp.arange(NDOC, dtype=jnp.int32)[None, :]
    row_index = jnp.arange(ROWS, dtype=jnp.int32)[:, None]
    forced = (row_index == chosen) & (column_index == NDOC - 1)
    return jnp.where(forced, TOK_DEV - 1, starts).astype(jnp.int32)


def draw_valid_len(key, part):
    key = jax.random.fold_in(key, 23)
    least = TOK_DEV - TOK_DEV // 2 + 1
    shortfall = jax.random.randint(jax.random.fold_in(key, 1), (ROWS,), 0, TOK_DEV // 2 - 1)
    full_row = jax.random.randint(jax.random.fold_in(key, 2), (), 0, ROWS)
    offset = jax.random.randint(jax.random.fold_in(key, 3), (), 0, ROWS - 1)
    short_row = (full_row + 1 + offset) % ROWS
    row_index = jnp.arange(ROWS, dtype=jnp.int32)
    lengths = jnp.where(row_index == full_row, TOK_DEV, TOK_DEV - shortfall)
    return jnp.where(row_index == short_row, least, lengths).astype(jnp.int32)


def strengthened(values, stream_key, source, target, shards_of, factor):
    def block_of(dim):
        return (jnp.arange(values.shape[dim]) // (values.shape[dim] // shards_of)).reshape((-1,) + (1,) * (values.ndim - 1 - dim))

    near = jax.random.permutation(stream_key, shards_of)[block_of(target)]
    second = (block_of(target) + shards_of // 2) % shards_of
    return jnp.where((block_of(source) == near) | (block_of(source) == second), factor * values, values)


def steps_of(rng, dims, pieces, smallest, top_value):
    factor_of, own = 1.0, jax.random.fold_in(rng, 6)
    for dim, blocks in pieces:
        draws = jnp.exp(jax.random.uniform(jax.random.fold_in(own, dim), (blocks,), jnp.float32, smallest / len(pieces), top_value / len(pieces)))
        factor_of = factor_of * jnp.repeat(draws, dims[dim] // blocks).reshape([-1 if axis == dim else 1 for axis in range(len(dims))])
    return factor_of


def normal_values(key, extent, scale, limit, cuts=(), kind=jnp.bfloat16):
    values = jax.random.normal(key, extent, jnp.float32) * scale
    if len(cuts) > 0:
        values = steps_of(key, extent, cuts, -0.22, 0.18) * values
    return jnp.clip(values, min=-limit, max=limit).astype(kind)


def bell_draw_with(stream_key, extent, scale, limit, shards, heavy, kind=jnp.bfloat16):
    drawn = scale * jax.random.normal(stream_key, extent, jnp.float32)
    if shards:
        drawn = drawn * steps_of(stream_key, extent, shards, -0.22, 0.18)
    return jnp.clip(strengthened(drawn, jax.random.fold_in(stream_key, 3), *heavy), -limit, limit).astype(kind)


def setup_inputs(seed: int = 0) -> dict:
    splits = jax.random.split(jax.random.key(seed), 32)
    return {
        "tokens": bell_draw_with(splits[0], (ROWS, TOK_DEV, D), 1.0, 6.0, ((0, 32),), (0, 2, 32, 2.75)),
        "cotangent": bell_draw_with(splits[1], (ROWS, TOK_DEV, D), 1.0, 6.0, ((0, 32),), (0, 2, 32, 2.75)),
        "doc_starts": draw_doc_starts(jax.random.fold_in(splits[31], 71), 0),
        "valid_len": draw_valid_len(jax.random.fold_in(splits[31], 71), 0),
        "w_in": normal_values(splits[4], (D, DPROJ), D ** -0.5, 0.125, ((0, 4), (1, 8)), jnp.float32),
        "w_out": normal_values(splits[5], (DI, D), DI ** -0.5, 0.09375, ((0, 4), (1, 8)), jnp.float32),
        "norm_gain": jnp.clip(1.0 + 0.1 * jax.random.normal(splits[6], (D,), jnp.float32), 0.5, 1.5),
        "gate_gain": jnp.clip(1.0 + 0.1 * jax.random.normal(splits[7], (DI,), jnp.float32), 0.5, 1.5),
        "conv_w": normal_values(splits[8], (CONVW, CONV), 0.5, 3.0, ((1, 4),), jnp.float32),
        "conv_b": normal_values(splits[9], (CONV,), 0.3, 3.0, ((0, 4),), jnp.float32),
        "dt_bias": jnp.clip(-6.9 + 4.65 * jax.random.uniform(splits[10], (NH,), jnp.float32) ** steps_of(splits[10], (NH,), ((0, 4),), -0.2, 0.2), -6.9, -2.25),
        "a_log": jnp.clip(2.77 * jax.random.uniform(splits[11], (NH,), jnp.float32) ** steps_of(splits[11], (NH,), ((0, 4),), -0.2, 0.2), 0.0, 2.77),
        "d_skip": jnp.clip(0.5 + 1.0 * jax.random.uniform(splits[12], (NH,), jnp.float32) ** steps_of(splits[12], (NH,), ((0, 4),), -0.2, 0.2), 0.5, 1.5),
        "first_w_in": normal_values(splits[13], (D, DPROJ), 0.1, 0.625, ((0, 4), (1, 8)), jnp.float32),
        "second_w_in": jnp.clip(jnp.exp(math.log(0.3) - 3.4011974 * jax.random.uniform(splits[14], (D, DPROJ), jnp.float32) ** steps_of(splits[14], (D, DPROJ), ((0, 4), (1, 8)), -0.2, 0.2)), 0.01, 0.3),
        "first_w_out": normal_values(splits[15], (DI, D), 0.1, 0.625, ((0, 4), (1, 8)), jnp.float32),
        "second_w_out": jnp.clip(jnp.exp(math.log(0.3) - 3.4011974 * jax.random.uniform(splits[16], (DI, D), jnp.float32) ** steps_of(splits[16], (DI, D), ((0, 4), (1, 8)), -0.2, 0.2)), 0.01, 0.3),
        "first_norm_gain": normal_values(splits[17], (D,), 0.1, 0.625, ((0, 4),), jnp.float32),
        "second_norm_gain": jnp.clip(jnp.exp(math.log(0.3) - 3.4011974 * jax.random.uniform(splits[18], (D,), jnp.float32) ** steps_of(splits[18], (D,), ((0, 4),), -0.2, 0.2)), 0.01, 0.3),
        "first_gate_gain": normal_values(splits[19], (DI,), 0.1, 0.625, ((0, 4),), jnp.float32),
        "second_gate_gain": jnp.clip(jnp.exp(math.log(0.3) - 3.4011974 * jax.random.uniform(splits[20], (DI,), jnp.float32) ** steps_of(splits[20], (DI,), ((0, 4),), -0.2, 0.2)), 0.01, 0.3),
        "first_conv_w": normal_values(splits[21], (CONVW, CONV), 0.1, 0.625, ((1, 4),), jnp.float32),
        "second_conv_w": jnp.clip(jnp.exp(math.log(0.3) - 3.4011974 * jax.random.uniform(splits[22], (CONVW, CONV), jnp.float32) ** steps_of(splits[22], (CONVW, CONV), ((1, 4),), -0.2, 0.2)), 0.01, 0.3),
        "first_conv_b": normal_values(splits[23], (CONV,), 0.1, 0.625, ((0, 4),), jnp.float32),
        "second_conv_b": jnp.clip(jnp.exp(math.log(0.3) - 3.4011974 * jax.random.uniform(splits[24], (CONV,), jnp.float32) ** steps_of(splits[24], (CONV,), ((0, 4),), -0.2, 0.2)), 0.01, 0.3),
        "first_dt_bias": normal_values(splits[25], (NH,), 0.1, 0.625, ((0, 4),), jnp.float32),
        "second_dt_bias": jnp.clip(jnp.exp(math.log(0.3) - 3.4011974 * jax.random.uniform(splits[26], (NH,), jnp.float32) ** steps_of(splits[26], (NH,), ((0, 4),), -0.2, 0.2)), 0.01, 0.3),
        "first_a_log": normal_values(splits[27], (NH,), 0.1, 0.625, ((0, 4),), jnp.float32),
        "second_a_log": jnp.clip(jnp.exp(math.log(0.3) - 3.4011974 * jax.random.uniform(splits[28], (NH,), jnp.float32) ** steps_of(splits[28], (NH,), ((0, 4),), -0.2, 0.2)), 0.01, 0.3),
        "first_d_skip": normal_values(splits[29], (NH,), 0.1, 0.625, ((0, 4),), jnp.float32),
        "second_d_skip": jnp.clip(jnp.exp(math.log(0.3) - 3.4011974 * jax.random.uniform(splits[30], (NH,), jnp.float32) ** steps_of(splits[30], (NH,), ((0, 4),), -0.2, 0.2)), 0.01, 0.3),
    }


@jax.custom_vjp
def low(v):
    return lax.optimization_barrier(v.astype(jnp.bfloat16)).astype(jnp.float32)

@jax.custom_vjp
def low_back(v):
    return v

def low_keep(v):
    return (low(v), None)

def low_pass(kept, grad):
    return (grad,)

def back_keep(v):
    return (v, None)

def back_low(kept, grad):
    return (low(grad),)
low.defvjp(low_keep, low_pass)
low_back.defvjp(back_keep, back_low)
EPSILON = 1e-05
BETA_ONE = 0.9
BETA_TWO = 0.95
ADAM_EPS = 1e-08
LEARN_RATE = 0.01
DECAY_RATE = 0.1
adam_step = 10
highest = lax.Precision.HIGHEST

def block_state(carry, inputs):
    carried_state, prev_segment = carry
    x_block, b_block, c_block, rate_block, step_block, seg_block = inputs
    block_len = seg_block.shape[0]
    row_index = jnp.arange(block_len, dtype=jnp.int32)
    lower_mask = row_index[:, None] >= row_index[None, :]
    cumulated = jnp.dot(lower_mask.astype(jnp.float32), rate_block, precision=highest)
    scores = jnp.dot(c_block, b_block.T, precision=highest)
    keep_mask = lower_mask & (seg_block[:, None] == seg_block[None, :])
    spread = cumulated[:, None, :] - cumulated[None, :, :]
    keep_float = keep_mask.astype(jnp.float32)[:, :, None]
    decay_table = jnp.exp(jnp.where(keep_mask[:, :, None], spread, 0.0)) * keep_float
    weights = scores[:, :, None] * decay_table * step_block[None, :, :]
    inside_part = jnp.einsum('tsh,shp->thp', weights, x_block, precision=highest)
    entering = (seg_block == prev_segment).astype(jnp.float32)
    reach = jnp.exp(cumulated) * entering[:, None]
    outside_part = jnp.einsum('tn,hpn->thp', c_block, carried_state, precision=highest) * reach[:, :, None]
    last_seg = seg_block[block_len - 1]
    same_last = (seg_block == last_seg).astype(jnp.float32)
    tail_weight = jnp.exp(cumulated[block_len - 1][None, :] - cumulated) * same_last[:, None] * step_block
    carried = jnp.exp(cumulated[block_len - 1]) * (last_seg == prev_segment).astype(jnp.float32)
    new_state = carried[:, None, None] * carried_state + jnp.einsum('sh,shp,sn->hpn', tail_weight, x_block, b_block, precision=highest)
    return ((new_state, last_seg), inside_part + outside_part)

def mixer(projected, starts, gate_g, conv_weight, conv_bias, dt_shift, log_decay, skip_gain):
    length = projected.shape[0]
    gate_part = projected[:, :DI]
    conv_in = projected[:, DI:DI + CONV]
    raw_dt = projected[:, DI + CONV:]
    position = jnp.arange(length, dtype=jnp.int32)
    counted = lax.optimization_barrier(jnp.sum((starts[None, :] <= position[:, None]).astype(jnp.int32), axis=1))
    segment = (counted - 1).astype(jnp.int32)
    convolved = jnp.zeros_like(conv_in) + conv_bias[None, :]
    for offset_k in range(CONVW):
        lag_rows = CONVW - 1 - offset_k
        moved = jnp.pad(conv_in, ((lag_rows, 0), (0, 0)))[:length]
        moved_seg = jnp.pad(segment, (lag_rows, 0), constant_values=-1)[:length]
        same_doc = (moved_seg == segment).astype(jnp.float32)
        convolved = convolved + conv_weight[offset_k][None, :] * moved * same_doc[:, None]
    activated = jax.nn.silu(convolved)
    x_heads = activated[:, :DI].reshape(length, NH, HP)
    b_input = activated[:, DI:DI + NS]
    c_input = activated[:, DI + NS:]
    step_size = jax.nn.softplus(raw_dt + dt_shift[None, :])
    decay_rates = step_size * (-jnp.exp(log_decay))[None, :]
    blocks = length // SPAN
    start_carry = (jnp.zeros((NH, HP, NS), jnp.float32), jnp.array(-1, dtype=jnp.int32))
    scan_inputs = (x_heads.reshape(blocks, SPAN, NH, HP), b_input.reshape(blocks, SPAN, NS), c_input.reshape(blocks, SPAN, NS), decay_rates.reshape(blocks, SPAN, NH), step_size.reshape(blocks, SPAN, NH), segment.reshape(blocks, SPAN))
    unused, outputs = lax.scan(jax.checkpoint(block_state), start_carry, scan_inputs)
    scanned = outputs.reshape(length, NH, HP) + skip_gain[None, :, None] * x_heads
    gated_out = scanned.reshape(length, DI) * jax.nn.silu(gate_part)
    return gated_out * lax.rsqrt(lax.optimization_barrier(jnp.mean(gated_out * gated_out, axis=-1, keepdims=True)) + EPSILON) * gate_g[None, :]

def forward(hidden, starts, valid, weight_in, weight_out, gain_norm, gain_gate, taps, tap_bias, shift_dt, log_decay, skip_gain):
    win = low(weight_in)
    wout = low(weight_out)
    ngain = low(gain_norm)
    ggain = low(gain_gate)
    conv_weight = low(taps)
    conv_bias = low(tap_bias)
    dt_shift = low(shift_dt)
    decay_log = low(log_decay)
    skip_low = low(skip_gain)
    scale_rows = lax.rsqrt(lax.optimization_barrier(jnp.mean(hidden * hidden, axis=-1, keepdims=True)) + EPSILON)
    normed = low(hidden * scale_rows * ngain)
    projected = low_back(jnp.einsum('gld,de->gle', normed, win, precision=highest))
    mixed = low(jax.vmap(mixer, in_axes=(0, 0, None, None, None, None, None, None))(projected, starts, ggain, conv_weight, conv_bias, dt_shift, decay_log, skip_low))
    branch = jnp.einsum('gli,id->gld', mixed, wout, precision=highest)
    position = jnp.arange(hidden.shape[1], dtype=jnp.int32)
    live = (position[None, :] < valid[:, None]).astype(jnp.float32)
    return hidden + branch * live[:, :, None]

def adam_direction(weight, gradient, first, second, decayed):
    first_new = BETA_ONE * first + (1.0 - BETA_ONE) * gradient
    second_new = BETA_TWO * second + (1.0 - BETA_TWO) * gradient * gradient
    first_hat = first_new / (1.0 - BETA_ONE ** adam_step)
    second_hat = second_new / (1.0 - BETA_TWO ** adam_step)
    direction = first_hat / (jnp.sqrt(second_hat) + ADAM_EPS)
    if decayed:
        direction = direction + DECAY_RATE * weight
    return (direction, first_new, second_new)

def adamw(weight, gradient, first, second, decayed):
    direction, first_new, second_new = adam_direction(weight, gradient, first, second, decayed)
    return (weight - LEARN_RATE * direction, first_new, second_new)

def reference(tokens, cotangent, doc_starts, valid_len, w_in, w_out, norm_gain, gate_gain, conv_w, conv_b, dt_bias, a_log, d_skip, first_w_in, second_w_in, first_w_out, second_w_out, first_norm_gain, second_norm_gain, first_gate_gain, second_gate_gain, first_conv_w, second_conv_w, first_conv_b, second_conv_b, first_dt_bias, second_dt_bias, first_a_log, second_a_log, first_d_skip, second_d_skip):
    params = (w_in, w_out, norm_gain, gate_gain, conv_w, conv_b, dt_bias, a_log, d_skip)
    row_count = tokens.shape[0]
    group = min(row_count, max(1, 4096 // TOK_DEV))
    while row_count % group != 0:
        group = group - 1
    count_groups = row_count // group

    def one_group(totals, items):
        tok_group, cot_group, starts, valid = items

        def run_forward(hid, weight_in, weight_out, gain_norm, gain_gate, taps, tap_bias, shift_dt, log_decay, skip_gain):
            return forward(hid, starts, valid, weight_in, weight_out, gain_norm, gain_gate, taps, tap_bias, shift_dt, log_decay, skip_gain)
        result, pullback = jax.vjp(run_forward, tok_group.astype(jnp.float32), w_in, w_out, norm_gain, gate_gain, conv_w, conv_b, dt_bias, a_log, d_skip)
        gradients = pullback(cot_group.astype(jnp.float32))
        new_totals = tuple((total + grad_part for total, grad_part in zip(totals, gradients[1:])))
        return (new_totals, (result.astype(jnp.bfloat16), gradients[0]))
    initial = tuple((jnp.zeros_like(param) for param in params))
    scan_items = (tokens.reshape(count_groups, group, TOK_DEV, D), cotangent.reshape(count_groups, group, TOK_DEV, D), doc_starts.reshape(count_groups, group, NDOC), valid_len.reshape(count_groups, group))
    totals, (outs_grouped, grads_grouped) = lax.scan(one_group, initial, scan_items)
    out_tokens = outs_grouped.reshape(row_count, TOK_DEV, D)
    grad_tokens = grads_grouped.reshape(row_count, TOK_DEV, D)
    factor = 1.0 / math.sqrt(TOKENS)
    new_w_in, new_first_w_in, new_second_w_in = adamw(w_in, totals[0] * factor, first_w_in, second_w_in, True)
    new_w_out, new_first_w_out, new_second_w_out = adamw(w_out, totals[1] * factor, first_w_out, second_w_out, True)
    step_norm_gain, new_first_norm_gain, new_second_norm_gain = adam_direction(norm_gain, totals[2] * factor, first_norm_gain, second_norm_gain, False)
    step_gate_gain, new_first_gate_gain, new_second_gate_gain = adam_direction(gate_gain, totals[3] * factor, first_gate_gain, second_gate_gain, False)
    step_conv_w, new_first_conv_w, new_second_conv_w = adam_direction(conv_w, totals[4] * factor, first_conv_w, second_conv_w, True)
    step_conv_b, new_first_conv_b, new_second_conv_b = adam_direction(conv_b, totals[5] * factor, first_conv_b, second_conv_b, True)
    step_dt_bias, new_first_dt_bias, new_second_dt_bias = adam_direction(dt_bias, totals[6] * factor, first_dt_bias, second_dt_bias, False)
    step_a_log, new_first_a_log, new_second_a_log = adam_direction(a_log, totals[7] * factor, first_a_log, second_a_log, False)
    step_d_skip, new_first_d_skip, new_second_d_skip = adam_direction(d_skip, totals[8] * factor, first_d_skip, second_d_skip, False)
    return (out_tokens, grad_tokens, new_w_in, new_first_w_in, new_second_w_in, new_w_out, new_first_w_out, new_second_w_out, step_norm_gain, new_first_norm_gain, new_second_norm_gain, step_gate_gain, new_first_gate_gain, new_second_gate_gain, step_conv_w, new_first_conv_w, new_second_conv_w, step_conv_b, new_first_conv_b, new_second_conv_b, step_dt_bias, new_first_dt_bias, new_second_dt_bias, step_a_log, new_first_a_log, new_second_a_log, step_d_skip, new_first_d_skip, new_second_d_skip)
```

```python
import functools
import math

import jax
import jax.numpy as jnp
from jax import lax
from jax.experimental import pallas as pl
from jax.experimental.pallas import tpu as pltpu
from jax.sharding import PartitionSpec as P

NH = 64
HP = 64
NS = 128
CONVW = 4
DI = 4096
CONV = 4352

EPSILON = 1e-05
BETA_ONE = 0.9
BETA_TWO = 0.95
ADAM_EPS = 1e-08
LEARN_RATE = 0.01
DECAY_RATE = 0.1
adam_step = 10
highest = lax.Precision.HIGHEST

Q = 128
BC = 512
HB = BC // HP
PAIRS = BC // 128
F32 = jnp.float32
BF16 = jnp.bfloat16


def dot(a, b):
    return jnp.dot(a, b, preferred_element_type=F32)


def dot_nt(a, b):
    return lax.dot_general(a, b, (((1,), (1,)), ((), ())), preferred_element_type=F32)


def sigmoid(v):
    return 1.0 / (1.0 + jnp.exp(-v))


def segment_of(starts_ref, position):
    count = jnp.zeros_like(position)
    for k in range(starts_ref.shape[1]):
        count = count + (starts_ref[0, k] <= position).astype(jnp.int32)
    return count


def conv_forward(values, weights, bias, same_ref):
    total = values * weights[CONVW - 1 : CONVW] + bias
    for lag in range(1, CONVW):
        moved = pltpu.roll(values, lag, 0) * same_ref[lag - 1]
        total = total + moved * weights[CONVW - 1 - lag : CONVW - lag]
    return total


def conv_backward(d_conv, values, weights, same_ref):
    length = values.shape[0]
    d_in = d_conv * weights[CONVW - 1 : CONVW]
    sums = [jnp.sum(d_conv * values, axis=0, keepdims=True)]
    for lag in range(1, CONVW):
        masked = d_conv * same_ref[lag - 1]
        sums.append(jnp.sum(masked * pltpu.roll(values, lag, 0), axis=0, keepdims=True))
        d_in = d_in + pltpu.roll(masked, length - lag, 0) * weights[CONVW - 1 - lag : CONVW - lag]
    return d_in, jnp.concatenate(sums[::-1], axis=0), jnp.sum(d_conv, axis=0, keepdims=True)


def prepare_masks(starts_ref, length, same_ref, enter_ref, last_ref):
    col = lax.broadcasted_iota(jnp.int32, (length, 128), 0)
    seg = segment_of(starts_ref, col)
    for lag in range(1, CONVW):
        same_ref[lag - 1] = (segment_of(starts_ref, col - lag) == seg).astype(F32)
    begin = col - lax.rem(col, Q)
    enter_ref[...] = ((segment_of(starts_ref, begin - 1) == seg) & (begin > 0)).astype(F32)
    last_ref[...] = (segment_of(starts_ref, begin + (Q - 1)) == seg).astype(F32)


def keep_mask(starts_ref, chunk):
    rows = lax.broadcasted_iota(jnp.int32, (Q, Q), 0) + chunk * Q
    cols = lax.broadcasted_iota(jnp.int32, (Q, Q), 1) + chunk * Q
    return (rows >= cols) & (segment_of(starts_ref, rows) == segment_of(starts_ref, cols))


def step_rows(dt_ref, shift_ref, logd_ref):
    pre = dt_ref[...] + shift_ref[...]
    step = jnp.maximum(pre, 0.0) + jnp.log1p(jnp.exp(-jnp.abs(pre)))
    decay = jnp.exp(logd_ref[...])
    return pre, step, -step * decay, decay


def cumulate(rate, chunks):
    rows = lax.broadcasted_iota(jnp.int32, (Q, Q), 0)
    cols = lax.broadcasted_iota(jnp.int32, (Q, Q), 1)
    upper = (rows <= cols).astype(F32)
    parts = [
        jnp.dot(rate[:, c * Q : (c + 1) * Q], upper, precision=highest, preferred_element_type=F32)
        for c in range(chunks)
    ]
    return jnp.concatenate(parts, axis=1)


def halves(lo, pair):
    zero = jnp.zeros_like(pair)
    return jnp.concatenate([jnp.where(lo, pair, zero), jnp.where(lo, zero, pair)], axis=0)


def forward_kernel(
    starts_ref, gate_ref, xin_ref, bc_ref, dt_ref, cw_ref, cb_ref, cwbc_ref, cbbc_ref,
    shift_ref, logd_ref, skip_ref, gain_ref,
    mixed_ref, y_ref, state_ref, q_ref,
    same_ref, enter_ref, last_ref, cmat_ref, bt_ref, score_ref, gated_ref, square_ref,
    x_ref, carry_ref, step_ref, cum_ref, cumt_ref,
):
    j = pl.program_id(0)
    length = gate_ref.shape[0]
    chunks = length // Q
    lo = lax.broadcasted_iota(jnp.int32, (Q, 128), 1) < HP

    @pl.when(j == 0)
    def _():
        prepare_masks(starts_ref, length, same_ref, enter_ref, last_ref)
        square_ref[...] = jnp.zeros_like(square_ref)
        both = []
        for part in range(2):
            cols = slice(part * NS, (part + 1) * NS)
            conv = conv_forward(bc_ref[:, cols].astype(F32), cwbc_ref[:, cols], cbbc_ref[:, cols], same_ref)
            both.append(conv * sigmoid(conv))
        bmat, cmat = both
        cmat_ref[...] = cmat.astype(BF16)
        bt = bmat.T
        bt_ref[...] = bt.astype(BF16)
        for c in range(chunks):
            rows = slice(c * Q, (c + 1) * Q)
            score = jnp.dot(cmat[rows].astype(BF16), bt[:, rows].astype(BF16), preferred_element_type=F32)
            score_ref[c] = jnp.where(keep_mask(starts_ref, c), score, 0.0)

    _, step, rate, _ = step_rows(dt_ref, shift_ref, logd_ref)
    cum = cumulate(rate, chunks)
    cumt_ref[...] = cum
    cum_ref[...] = cum.T
    step_ref[...] = step.T
    carry_ref[...] = jnp.zeros_like(carry_ref)
    for p in range(PAIRS):
        cols = slice(p * 128, (p + 1) * 128)
        conv = conv_forward(xin_ref[:, cols].astype(F32), cw_ref[:, cols], cb_ref[:, cols], same_ref)
        x_ref[:, cols] = conv * sigmoid(conv)
    for c in range(chunks):
        rows = slice(c * Q, (c + 1) * Q)
        entering_state = carry_ref[...].astype(BF16)
        state_ref[c] = entering_state
        if c > 0:
            outside = dot(cmat_ref[rows, :], entering_state)
        score = score_ref[c]
        for p in range(PAIRS):
            cols = slice(p * 128, (p + 1) * 128)
            cum_a = jnp.broadcast_to(cum_ref[rows, 2 * p : 2 * p + 1], (Q, Q))
            cum_b = jnp.broadcast_to(cum_ref[rows, 2 * p + 1 : 2 * p + 2], (Q, Q))
            low_a = (score * jnp.exp(jnp.minimum(cum_a - cumt_ref[2 * p : 2 * p + 1, rows], 0.0))).astype(BF16)
            low_b = (score * jnp.exp(jnp.minimum(cum_b - cumt_ref[2 * p + 1 : 2 * p + 2, rows], 0.0))).astype(BF16)
            cum_x = jnp.where(lo, cum_a, cum_b)
            step_x = jnp.where(lo, step_ref[rows, 2 * p : 2 * p + 1], step_ref[rows, 2 * p + 1 : 2 * p + 2])
            x = x_ref[rows, cols]
            xs = (x * step_x).astype(BF16)
            y = dot(jnp.concatenate([low_a, low_b], axis=1), halves(lo, xs))
            reach = jnp.exp(cum_x) * enter_ref[rows]
            if c > 0:
                y = y + reach * outside[:, cols]
            if c < chunks - 1:
                tail = jnp.exp(cum_x[Q - 1 : Q] - cum_x) * last_ref[rows]
                carry_ref[:, cols] = reach[Q - 1 : Q] * carry_ref[:, cols] + dot(
                    bt_ref[:, rows], (xs.astype(F32) * tail).astype(BF16)
                )
            y_ref[rows, cols] = y
            gate = gate_ref[rows, cols].astype(F32)
            gated = (y + skip_ref[:, cols] * x) * (gate * sigmoid(gate))
            square_ref[rows, :] += gated * gated
            gated_ref[rows, pl.ds(pl.multiple_of(j * BC + p * 128, 128), 128)] = gated

    @pl.when(j == pl.num_programs(0) - 1)
    def _():
        mean = jnp.sum(square_ref[...], axis=1, keepdims=True) * (1.0 / DI)
        q = lax.rsqrt(mean + EPSILON)
        q_ref[...] = q
        for c in range(DI // 512):
            cols = slice(c * 512, (c + 1) * 512)
            mixed_ref[:, cols] = (gated_ref[:, cols] * q * gain_ref[:, cols]).astype(BF16)


def backward_kernel(
    starts_ref, gate_ref, xin_ref, bc_ref, dt_ref, cw_ref, cb_ref, cwbc_ref, cbbc_ref,
    shift_ref, logd_ref, skip_ref, gain_ref, y_ref, state_ref, q_ref, mean_ref, dm_ref,
    dgate_ref, dxin_ref, dbc_ref, ddt_ref, sgain_ref, scw_ref, scb_ref, scwbc_ref, scbbc_ref,
    sshift_ref, slogd_ref, sskip_ref,
    same_ref, enter_ref, last_ref, bmat_ref, cmat_ref, ct_ref, score_ref, scoret_ref,
    x_ref, slope_ref, dy_ref, dxs_ref, carry_ref, step_ref, cum_ref, cumt_ref,
    dscore_ref, db_ref, dc_ref, v1_ref, v2_ref, v3_ref, v4_ref,
):
    j = pl.program_id(0)
    length = gate_ref.shape[0]
    chunks = length // Q
    lo = lax.broadcasted_iota(jnp.int32, (Q, 128), 1) < HP

    def activate_bc(part):
        cols = slice(part * NS, (part + 1) * NS)
        return conv_forward(bc_ref[:, cols].astype(F32), cwbc_ref[:, cols], cbbc_ref[:, cols], same_ref)

    @pl.when(j == 0)
    def _():
        prepare_masks(starts_ref, length, same_ref, enter_ref, last_ref)
        both = []
        for part in range(2):
            conv = activate_bc(part)
            both.append(conv * sigmoid(conv))
        bmat, cmat = both
        bmat_ref[...] = bmat.astype(BF16)
        cmat_ref[...] = cmat.astype(BF16)
        bt = bmat.T
        ct_ref[...] = cmat.T.astype(BF16)
        for c in range(chunks):
            rows = slice(c * Q, (c + 1) * Q)
            score = jnp.dot(cmat[rows].astype(BF16), bt[:, rows].astype(BF16), preferred_element_type=F32)
            score = jnp.where(keep_mask(starts_ref, c), score, 0.0)
            score_ref[c] = score
            scoret_ref[c] = score.T
        dscore_ref[...] = jnp.zeros_like(dscore_ref)
        db_ref[...] = jnp.zeros_like(db_ref)
        dc_ref[...] = jnp.zeros_like(dc_ref)

    pre, step, rate, decay = step_rows(dt_ref, shift_ref, logd_ref)
    cum = cumulate(rate, chunks)
    cumt_ref[...] = cum
    cum_ref[...] = cum.T
    step_ref[...] = step.T
    carry_ref[...] = jnp.zeros_like(carry_ref)
    q = q_ref[...]
    mean = mean_ref[...]
    for p in range(PAIRS):
        cols = slice(p * 128, (p + 1) * 128)
        conv = conv_forward(xin_ref[:, cols].astype(F32), cw_ref[:, cols], cb_ref[:, cols], same_ref)
        sig = sigmoid(conv)
        x = conv * sig
        x_ref[:, cols] = x
        slope_ref[:, cols] = sig * (1.0 + conv - x)
        gate = gate_ref[:, cols].astype(F32)
        gsig = sigmoid(gate)
        silu = gate * gsig
        scanned = y_ref[:, cols] + skip_ref[:, cols] * x
        gated = scanned * silu
        scaled = dm_ref[:, cols].astype(F32) * q
        sgain_ref[:, cols] = jnp.sum(gated * scaled, axis=0, keepdims=True)
        d_gated = scaled * gain_ref[:, cols] - gated * mean
        dgate_ref[:, cols] = (d_gated * scanned * (gsig * (1.0 + gate - silu))).astype(dgate_ref.dtype)
        d_scanned = d_gated * silu
        dy_ref[:, cols] = d_scanned
        sskip_ref[:, cols] = jnp.sum(d_scanned * x, axis=0, keepdims=True)

    for c in reversed(range(chunks)):
        rows = slice(c * Q, (c + 1) * Q)
        score = score_ref[c]
        scoret = scoret_ref[c]
        d_state = carry_ref[...]
        d_state_low = d_state.astype(BF16)
        if c < chunks - 1:
            from_state = dot(bmat_ref[rows, :], d_state_low)
        d_score = dscore_ref[c]
        for p in range(PAIRS):
            cols = slice(p * 128, (p + 1) * 128)
            cum_a = jnp.broadcast_to(cum_ref[rows, 2 * p : 2 * p + 1], (Q, Q))
            cum_b = jnp.broadcast_to(cum_ref[rows, 2 * p + 1 : 2 * p + 2], (Q, Q))
            row_a = cumt_ref[2 * p : 2 * p + 1, rows]
            row_b = cumt_ref[2 * p + 1 : 2 * p + 2, rows]
            cum_x = jnp.where(lo, cum_a, cum_b)
            step_x = jnp.where(lo, step_ref[rows, 2 * p : 2 * p + 1], step_ref[rows, 2 * p + 1 : 2 * p + 2])
            x = x_ref[rows, cols]
            xs = (x * step_x).astype(BF16)
            xs_wide = xs.astype(F32)
            d_y = dy_ref[rows, cols]
            d_y_low = d_y.astype(BF16)
            pair = dot_nt(d_y_low, halves(lo, xs))
            d_score = d_score + pair[:, :Q] * jnp.exp(jnp.minimum(cum_a - row_a, 0.0))
            d_score = d_score + pair[:, Q:] * jnp.exp(jnp.minimum(cum_b - row_b, 0.0))
            up_a = (scoret * jnp.exp(jnp.minimum(row_a - cum_a, 0.0))).astype(BF16)
            up_b = (scoret * jnp.exp(jnp.minimum(row_b - cum_b, 0.0))).astype(BF16)
            d_xs = dot(jnp.concatenate([up_a, up_b], axis=1), halves(lo, d_y_low))
            v1_ref[rows, cols] = d_y_low.astype(F32) * y_ref[rows, cols] - xs_wide * d_xs
            reach = jnp.exp(cum_x) * enter_ref[rows]
            if c < chunks - 1:
                tail = jnp.exp(cum_x[Q - 1 : Q] - cum_x) * last_ref[rows]
                d_tail = tail * from_state[:, cols]
                v3_ref[rows, cols] = xs_wide * d_tail
                d_xs = d_xs + d_tail
                db_ref[rows, :] += dot_nt((xs_wide * tail).astype(BF16), d_state_low[:, cols])
                entered = state_ref[c, :, cols]
                v4_ref[c : c + 1, cols] = reach[Q - 1 : Q] * jnp.sum(
                    d_state[:, cols] * entered.astype(F32), axis=0, keepdims=True
                )
            else:
                v3_ref[rows, cols] = jnp.zeros((Q, 128), F32)
                v4_ref[c : c + 1, cols] = jnp.zeros((1, 128), F32)
            if c > 0:
                reached = (reach * d_y).astype(BF16)
                dc_ref[rows, :] += dot_nt(reached, state_ref[c, :, cols])
                carry_ref[:, cols] = reach[Q - 1 : Q] * d_state[:, cols] + dot(ct_ref[:, rows], reached)
            v2_ref[rows, cols] = x * d_xs
            dxs_ref[rows, cols] = step_x * d_xs + skip_ref[:, cols] * d_y
        dscore_ref[c] = d_score

    head = lax.broadcasted_iota(jnp.int32, (HB, BC), 0)
    lane = lax.broadcasted_iota(jnp.int32, (HB, BC), 1)
    pick = ((lane >= head * HP) & (lane < (head + 1) * HP)).astype(BF16)

    def by_head(values):
        high = values.astype(BF16)
        rest = (values - high.astype(F32)).astype(BF16)
        return dot_nt(pick, high) + dot_nt(pick, rest)

    h1 = by_head(v1_ref[...])
    h2 = by_head(v2_ref[...])
    h3 = by_head(v3_ref[...])
    h4 = by_head(v4_ref[...])
    rows_i = lax.broadcasted_iota(jnp.int32, (Q, Q), 0)
    cols_i = lax.broadcasted_iota(jnp.int32, (Q, Q), 1)
    suffix = (rows_i >= cols_i).astype(F32)
    prefix = (rows_i < cols_i).astype(F32)
    parts = []
    for c in range(chunks):
        rows = slice(c * Q, (c + 1) * Q)
        parts.append(
            jnp.dot(h1[:, rows], suffix, precision=highest, preferred_element_type=F32)
            + jnp.dot(h3[:, rows], prefix, precision=highest, preferred_element_type=F32)
            + h4[:, c : c + 1]
        )
    d_rate = jnp.concatenate(parts, axis=1)
    d_step = h2 - d_rate * decay
    d_raw = d_step * sigmoid(pre)
    ddt_ref[...] = d_raw
    sshift_ref[...] = jnp.sum(d_raw, axis=1, keepdims=True)
    slogd_ref[...] = jnp.sum(d_rate * rate, axis=1, keepdims=True)

    for p in range(PAIRS):
        cols = slice(p * 128, (p + 1) * 128)
        d_conv = dxs_ref[:, cols] * slope_ref[:, cols]
        d_in, s_w, s_b = conv_backward(d_conv, xin_ref[:, cols].astype(F32), cw_ref[:, cols], same_ref)
        dxin_ref[:, cols] = d_in.astype(dxin_ref.dtype)
        scw_ref[:, cols] = s_w
        scb_ref[:, cols] = s_b

    @pl.when(j == pl.num_programs(0) - 1)
    def _():
        for c in range(chunks):
            rows = slice(c * Q, (c + 1) * Q)
            masked = jnp.where(keep_mask(starts_ref, c), dscore_ref[c], 0.0)
            dc_ref[rows, :] += dot(masked.astype(BF16), bmat_ref[rows, :])
            db_ref[rows, :] += dot(masked.T.astype(BF16), cmat_ref[rows, :])
        for part, grad_ref in ((0, db_ref), (1, dc_ref)):
            cols = slice(part * NS, (part + 1) * NS)
            conv = activate_bc(part)
            sig = sigmoid(conv)
            d_conv = grad_ref[...] * (sig * (1.0 + conv - conv * sig))
            d_in, s_w, s_b = conv_backward(d_conv, bc_ref[:, cols].astype(F32), cwbc_ref[:, cols], same_ref)
            dbc_ref[:, cols] = d_in.astype(dbc_ref.dtype)
            scwbc_ref[:, cols] = s_w
            scbbc_ref[:, cols] = s_b


def column_block(rows, offset=0):
    return pl.BlockSpec((rows, BC), lambda j: (0, j + offset))


def whole(*shape):
    return pl.BlockSpec(shape, lambda j: (0,) * len(shape))


def common_specs(length):
    heads = pl.BlockSpec((HB, 1), lambda j: (j, 0))
    return [
        pl.BlockSpec(memory_space=pltpu.SMEM),
        column_block(length),
        column_block(length, DI // BC),
        pl.BlockSpec((length, 2 * NS), lambda j: (0, 2 * DI // (2 * NS))),
        pl.BlockSpec((HB, length), lambda j: (j, 0)),
        column_block(CONVW),
        column_block(1),
        pl.BlockSpec((CONVW, 2 * NS), lambda j: (0, DI // (2 * NS))),
        pl.BlockSpec((1, 2 * NS), lambda j: (0, DI // (2 * NS))),
        heads,
        heads,
        column_block(1),
    ]


def mix_forward(starts, projected, dt_rows, conv_w, conv_b, shift, logd, skip_cols, gain):
    length = projected.shape[0]
    chunks = length // Q
    vmem = pltpu.VMEM
    return pl.pallas_call(
        forward_kernel,
        grid=(DI // BC,),
        in_specs=common_specs(length) + [whole(1, DI)],
        out_specs=[
            whole(length, DI),
            column_block(length),
            pl.BlockSpec((chunks, NS, BC), lambda j: (0, 0, j)),
            whole(length, 1),
        ],
        out_shape=[
            jax.ShapeDtypeStruct((length, DI), BF16),
            jax.ShapeDtypeStruct((length, DI), F32),
            jax.ShapeDtypeStruct((chunks, NS, DI), BF16),
            jax.ShapeDtypeStruct((length, 1), F32),
        ],
        scratch_shapes=[
            vmem((CONVW - 1, length, 128), F32),
            vmem((length, 128), F32),
            vmem((length, 128), F32),
            vmem((length, NS), BF16),
            vmem((NS, length), BF16),
            vmem((chunks, Q, Q), F32),
            vmem((length, DI), F32),
            vmem((length, 128), F32),
            vmem((length, BC), F32),
            vmem((NS, BC), F32),
            vmem((length, HB), F32),
            vmem((length, HB), F32),
            vmem((HB, length), F32),
        ],
        compiler_params=pltpu.CompilerParams(vmem_limit_bytes=56 * 1024 * 1024),
        name="mix_forward",
    )(starts, projected, projected, projected, dt_rows, conv_w, conv_b, conv_w, conv_b, shift, logd, skip_cols, gain)


def mix_backward(starts, projected, dt_rows, conv_w, conv_b, shift, logd, skip_cols, gain, y, states, q, mean, d_mixed):
    length = projected.shape[0]
    chunks = length // Q
    vmem = pltpu.VMEM
    heads = pl.BlockSpec((HB, 1), lambda j: (j, 0))
    col = whole(length, 1)
    shape = jax.ShapeDtypeStruct
    return pl.pallas_call(
        backward_kernel,
        grid=(DI // BC,),
        in_specs=common_specs(length)
        + [
            column_block(1),
            column_block(length),
            pl.BlockSpec((chunks, NS, BC), lambda j: (0, 0, j)),
            col,
            col,
            column_block(length),
        ],
        out_specs=[
            column_block(length),
            column_block(length),
            whole(length, 2 * NS),
            pl.BlockSpec((HB, length), lambda j: (j, 0)),
            column_block(1),
            column_block(CONVW),
            column_block(1),
            whole(CONVW, 2 * NS),
            whole(1, 2 * NS),
            heads,
            heads,
            column_block(1),
        ],
        out_shape=[
            shape((length, DI), BF16),
            shape((length, DI), BF16),
            shape((length, 2 * NS), BF16),
            shape((NH, length), F32),
            shape((1, DI), F32),
            shape((CONVW, DI), F32),
            shape((1, DI), F32),
            shape((CONVW, 2 * NS), F32),
            shape((1, 2 * NS), F32),
            shape((NH, 1), F32),
            shape((NH, 1), F32),
            shape((1, DI), F32),
        ],
        scratch_shapes=[
            vmem((CONVW - 1, length, 128), F32),
            vmem((length, 128), F32),
            vmem((length, 128), F32),
            vmem((length, NS), BF16),
            vmem((length, NS), BF16),
            vmem((NS, length), BF16),
            vmem((chunks, Q, Q), F32),
            vmem((chunks, Q, Q), F32),
            vmem((length, BC), F32),
            vmem((length, BC), F32),
            vmem((length, BC), F32),
            vmem((length, BC), F32),
            vmem((NS, BC), F32),
            vmem((length, HB), F32),
            vmem((length, HB), F32),
            vmem((HB, length), F32),
            vmem((chunks, Q, Q), F32),
            vmem((length, NS), F32),
            vmem((length, NS), F32),
            vmem((length, BC), F32),
            vmem((length, BC), F32),
            vmem((length, BC), F32),
            vmem((8, BC), F32),
        ],
        compiler_params=pltpu.CompilerParams(vmem_limit_bytes=56 * 1024 * 1024),
        name="mix_backward",
    )(
        starts, projected, projected, projected, dt_rows, conv_w, conv_b, conv_w, conv_b, shift, logd, skip_cols,
        gain, y, states, q, mean, d_mixed,
    )


def rms_scale(values, gain):
    return values * lax.rsqrt(jnp.mean(values * values, axis=-1, keepdims=True) + EPSILON) * gain


def adam_direction(weight, gradient, first, second, decayed):
    first_new = BETA_ONE * first + (1.0 - BETA_ONE) * gradient
    second_new = BETA_TWO * second + (1.0 - BETA_TWO) * gradient * gradient
    first_hat = first_new / (1.0 - BETA_ONE**adam_step)
    second_hat = second_new / (1.0 - BETA_TWO**adam_step)
    direction = first_hat / (jnp.sqrt(second_hat) + ADAM_EPS)
    if decayed:
        direction = direction + DECAY_RATE * weight
    return (direction, first_new, second_new)


def gather_small(values):
    flat = jnp.concatenate([v.astype(BF16).reshape(-1) for v in values])
    every = lax.all_gather(flat, "fsdp", axis=0, tiled=False)
    result, at = [], 0
    for v in values:
        size = v.size
        piece = every[:, at : at + size].astype(F32)
        at += size
        if v.ndim == 1:
            result.append(piece.reshape(1, -1))
        else:
            result.append(jnp.moveaxis(piece.reshape((-1,) + v.shape), 0, 1).reshape(v.shape[0], -1))
    return result


def shards(
    tokens, cotangent, doc_starts, valid_len,
    w_in, w_out, norm_gain, gate_gain, conv_w, conv_b, dt_bias, a_log, d_skip,
    first_w_in, second_w_in, first_w_out, second_w_out,
    first_norm_gain, second_norm_gain, first_gate_gain, second_gate_gain,
    first_conv_w, second_conv_w, first_conv_b, second_conv_b,
    first_dt_bias, second_dt_bias, first_a_log, second_a_log, first_d_skip, second_d_skip,
):
    length = tokens.shape[1]
    hidden = tokens[0].astype(F32)
    upstream = cotangent[0].astype(F32)
    small = (norm_gain, gate_gain, conv_w, conv_b, dt_bias, a_log, d_skip)
    norm_full, gate_full, convw_full, convb_full, shift_full, logd_full, skip_full = gather_small(small)
    in_full = lax.all_gather(
        lax.all_gather(w_in.astype(BF16), "dp", axis=1, tiled=True), "fsdp", axis=0, tiled=True
    )
    out_full = lax.all_gather(
        lax.all_gather(w_out.astype(BF16), "dp", axis=1, tiled=True), "fsdp", axis=0, tiled=True
    )
    scale = lax.rsqrt(jnp.mean(hidden * hidden, axis=-1, keepdims=True) + EPSILON)
    normed = (hidden * scale * norm_full).astype(BF16)
    projected = dot(normed, in_full)
    dt_rows = projected[:, DI + CONV :].T
    common = (
        doc_starts, projected, dt_rows, convw_full, convb_full, shift_full.T, logd_full.T,
        jnp.repeat(skip_full, HP, axis=1), gate_full,
    )
    mixed, y, states, q = mix_forward(*common)
    position = jnp.arange(length, dtype=jnp.int32)
    live = (position < valid_len[0]).astype(F32)[:, None]
    d_branch = (upstream * live).astype(BF16)
    branch = dot(mixed, out_full)
    out_tokens = (hidden + branch * live).astype(BF16)
    d_mixed = dot_nt(d_branch, out_full)
    mean = q * q * jnp.sum(mixed.astype(F32) * d_mixed, axis=1, keepdims=True) * (1.0 / DI)
    (
        d_gate_in, d_x_in, d_bc_in, d_dt, s_gain, s_cw, s_cb, s_cwbc, s_cbbc, s_shift, s_logd, s_skip,
    ) = mix_backward(*common, y, states, q, mean, d_mixed)
    d_low = jnp.concatenate([d_gate_in, d_x_in, d_bc_in, d_dt.T.astype(BF16)], axis=1)
    d_normed = dot_nt(d_low, in_full)
    weighted = norm_full * d_normed
    inner = jnp.mean(hidden * weighted, axis=-1, keepdims=True)
    grad_tokens = upstream + scale * weighted - hidden * (scale * scale * scale * inner)
    s_norm = jnp.sum(hidden * scale * d_normed, axis=0)
    contract = (((0,), (0,)), ((), ()))
    out_sum = lax.dot_general(mixed, d_branch, contract, preferred_element_type=F32).astype(BF16)
    in_sum = lax.dot_general(normed, d_low, contract, preferred_element_type=F32).astype(BF16)
    out_summed = lax.psum_scatter(out_sum, "fsdp", scatter_dimension=0, tiled=True)
    in_summed = lax.psum_scatter(in_sum, "fsdp", scatter_dimension=0, tiled=True)
    grad_in = lax.psum_scatter(in_summed, "dp", scatter_dimension=1, tiled=True).astype(F32)
    grad_out = lax.psum_scatter(out_summed, "dp", scatter_dimension=1, tiled=True).astype(F32)

    sums = (
        s_norm[None],
        s_gain,
        jnp.concatenate([s_cw, s_cwbc], axis=1),
        jnp.concatenate([s_cb, s_cbbc], axis=1),
        s_shift.T,
        s_logd.T,
        s_skip.reshape(1, NH, HP).sum(axis=2),
    )
    parts = lax.axis_size("fsdp")
    flat = jnp.concatenate(
        [jnp.moveaxis(s.reshape(s.shape[0], parts, -1), 1, 0).reshape(parts, -1) for s in sums], axis=1
    )
    total = lax.psum(flat, ("dp", "fsdp"))
    mine = lax.dynamic_index_in_dim(total, lax.axis_index("fsdp"), 0, keepdims=False)
    small_grads, at = [], 0
    for v in small:
        small_grads.append(mine[at : at + v.size].reshape(v.shape))
        at += v.size

    factor = 1.0 / math.sqrt(length * lax.axis_size("dp") * lax.axis_size("fsdp"))
    weights = (w_in, w_out) + small
    grads = (grad_in, grad_out) + tuple(small_grads)
    firsts = (
        first_w_in, first_w_out, first_norm_gain, first_gate_gain, first_conv_w, first_conv_b,
        first_dt_bias, first_a_log, first_d_skip,
    )
    seconds = (
        second_w_in, second_w_out, second_norm_gain, second_gate_gain, second_conv_w, second_conv_b,
        second_dt_bias, second_a_log, second_d_skip,
    )
    decay_flags = (True, True, False, False, True, True, False, False, False)
    results = []
    for i, (weight, gradient, first, second) in enumerate(zip(weights, grads, firsts, seconds)):
        direction, first_new, second_new = adam_direction(weight, gradient * factor, first, second, decay_flags[i])
        if i < 2:
            direction = weight - LEARN_RATE * direction
        results.extend((direction, first_new, second_new))
    return (out_tokens[None], grad_tokens[None]) + tuple(results)


def solution(mesh):
    rows3 = P(("dp", "fsdp"), None, None)
    both, split, last = P("fsdp", "dp"), P("fsdp"), P(None, "fsdp")
    small = (split, split, last, split, split, split, split)
    placed = (rows3, rows3, P(("dp", "fsdp"), None), P(("dp", "fsdp")), both, both) + small
    placed = placed + (both,) * 4 + tuple(s for s in small for _ in range(2))
    out = (rows3, rows3) + (both,) * 6 + tuple(s for s in small for _ in range(3))
    return jax.shard_map(shards, mesh=mesh, in_specs=placed, out_specs=out, check_vma=False)
```

```python
import functools
import math

import jax
import jax.numpy as jnp
from jax import lax
from jax.experimental import pallas as pl
from jax.experimental.layout import Layout, with_layout_constraint
from jax.experimental.pallas import tpu as pltpu
from jax.sharding import PartitionSpec as P

NH = 64
HP = 64
NS = 128
CONVW = 4
DI = 4096
CONV = 4352

EPSILON = 1e-05
BETA_ONE = 0.9
BETA_TWO = 0.95
ADAM_EPS = 1e-08
LEARN_RATE = 0.01
DECAY_RATE = 0.1
adam_step = 10
highest = lax.Precision.HIGHEST

Q = 128
BC = 512
HB = BC // HP
PAIRS = BC // 128
F32 = jnp.float32
BF16 = jnp.bfloat16


def dot(a, b):
    return jnp.dot(a, b, preferred_element_type=F32)


def dot_nt(a, b):
    return lax.dot_general(a, b, (((1,), (1,)), ((), ())), preferred_element_type=F32)


def sigmoid(v):
    return 1.0 / (1.0 + jnp.exp(-v))


def segment_of(starts_ref, position):
    row = pl.program_id(0)
    count = jnp.zeros_like(position)
    for k in range(starts_ref.shape[1]):
        count = count + (starts_ref[row, k] <= position).astype(jnp.int32)
    return count


def conv_forward(values, weights, bias, same_ref):
    total = values * weights[CONVW - 1 : CONVW] + bias
    for lag in range(1, CONVW):
        moved = pltpu.roll(values, lag, 0) * same_ref[lag - 1]
        total = total + moved * weights[CONVW - 1 - lag : CONVW - lag]
    return total


def conv_backward(d_conv, values, weights, same_ref):
    length = values.shape[0]
    d_in = d_conv * weights[CONVW - 1 : CONVW]
    sums = [jnp.sum(d_conv * values, axis=0, keepdims=True)]
    for lag in range(1, CONVW):
        masked = d_conv * same_ref[lag - 1]
        sums.append(jnp.sum(masked * pltpu.roll(values, lag, 0), axis=0, keepdims=True))
        d_in = d_in + pltpu.roll(masked, length - lag, 0) * weights[CONVW - 1 - lag : CONVW - lag]
    return d_in, jnp.concatenate(sums[::-1], axis=0), jnp.sum(d_conv, axis=0, keepdims=True)


def prepare_masks(starts_ref, length, same_ref, enter_ref, last_ref):
    col = lax.broadcasted_iota(jnp.int32, (length, 128), 0)
    seg = segment_of(starts_ref, col)
    for lag in range(1, CONVW):
        same_ref[lag - 1] = (segment_of(starts_ref, col - lag) == seg).astype(F32)
    begin = col - lax.rem(col, Q)
    enter_ref[...] = ((segment_of(starts_ref, begin - 1) == seg) & (begin > 0)).astype(F32)
    last_ref[...] = (segment_of(starts_ref, begin + (Q - 1)) == seg).astype(F32)


def keep_mask(starts_ref, chunk):
    rows = lax.broadcasted_iota(jnp.int32, (Q, Q), 0) + chunk * Q
    cols = lax.broadcasted_iota(jnp.int32, (Q, Q), 1) + chunk * Q
    return (rows >= cols) & (segment_of(starts_ref, rows) == segment_of(starts_ref, cols))


def step_rows(dt_ref, shift_ref, logd_ref):
    pre = dt_ref[...] + shift_ref[...]
    step = jnp.maximum(pre, 0.0) + jnp.log1p(jnp.exp(-jnp.abs(pre)))
    decay = jnp.exp(logd_ref[...])
    return pre, step, -step * decay, decay


def cumulate(rate, chunks):
    rows = lax.broadcasted_iota(jnp.int32, (Q, Q), 0)
    cols = lax.broadcasted_iota(jnp.int32, (Q, Q), 1)
    upper = (rows <= cols).astype(F32)
    parts = [
        jnp.dot(rate[:, c * Q : (c + 1) * Q], upper, precision=highest, preferred_element_type=F32)
        for c in range(chunks)
    ]
    return jnp.concatenate(parts, axis=1)


def halves(lo, pair):
    zero = jnp.zeros_like(pair)
    return jnp.concatenate([jnp.where(lo, pair, zero), jnp.where(lo, zero, pair)], axis=0)


def forward_kernel(
    starts_ref, gate_ref, xin_ref, bc_ref, dt_ref, cw_ref, cb_ref, cwbc_ref, cbbc_ref,
    shift_ref, logd_ref, skip_ref,
    gated_ref, y_ref, state_ref, total_ref,
    same_ref, enter_ref, last_ref, cmat_ref, bt_ref, score_ref, square_ref,
    x_ref, carry_ref, step_ref, cum_ref, cumt_ref,
):
    j = pl.program_id(1)
    length = gate_ref.shape[0]
    chunks = length // Q
    lo = lax.broadcasted_iota(jnp.int32, (Q, 128), 1) < HP

    @pl.when(j == 0)
    def _():
        prepare_masks(starts_ref, length, same_ref, enter_ref, last_ref)
        square_ref[...] = jnp.zeros_like(square_ref)
        both = []
        for part in range(2):
            cols = slice(part * NS, (part + 1) * NS)
            conv = conv_forward(bc_ref[:, cols].astype(F32), cwbc_ref[:, cols], cbbc_ref[:, cols], same_ref)
            both.append(conv * sigmoid(conv))
        bmat, cmat = both
        cmat_ref[...] = cmat.astype(BF16)
        bt = bmat.T
        bt_ref[...] = bt.astype(BF16)
        for c in range(chunks):
            rows = slice(c * Q, (c + 1) * Q)
            score = jnp.dot(cmat[rows].astype(BF16), bt[:, rows].astype(BF16), preferred_element_type=F32)
            score_ref[c] = jnp.where(keep_mask(starts_ref, c), score, 0.0)

    _, step, rate, _ = step_rows(dt_ref, shift_ref, logd_ref)
    cum = cumulate(rate, chunks)
    cumt_ref[...] = cum
    cum_ref[...] = cum.T
    step_ref[...] = step.T
    carry_ref[...] = jnp.zeros_like(carry_ref)
    for p in range(PAIRS):
        cols = slice(p * 128, (p + 1) * 128)
        conv = conv_forward(xin_ref[:, cols].astype(F32), cw_ref[:, cols], cb_ref[:, cols], same_ref)
        x_ref[:, cols] = conv * sigmoid(conv)
    for c in range(chunks):
        rows = slice(c * Q, (c + 1) * Q)
        entering_state = carry_ref[...].astype(BF16)
        state_ref[0, c] = entering_state
        if c > 0:
            outside = dot(cmat_ref[rows, :], entering_state)
        score = score_ref[c]
        for p in range(PAIRS):
            cols = slice(p * 128, (p + 1) * 128)
            cum_a = jnp.broadcast_to(cum_ref[rows, 2 * p : 2 * p + 1], (Q, Q))
            cum_b = jnp.broadcast_to(cum_ref[rows, 2 * p + 1 : 2 * p + 2], (Q, Q))
            low_a = (score * jnp.exp(jnp.minimum(cum_a - cumt_ref[2 * p : 2 * p + 1, rows], 0.0))).astype(BF16)
            low_b = (score * jnp.exp(jnp.minimum(cum_b - cumt_ref[2 * p + 1 : 2 * p + 2, rows], 0.0))).astype(BF16)
            cum_x = jnp.where(lo, cum_a, cum_b)
            step_x = jnp.where(lo, step_ref[rows, 2 * p : 2 * p + 1], step_ref[rows, 2 * p + 1 : 2 * p + 2])
            x = x_ref[rows, cols]
            xs = (x * step_x).astype(BF16)
            y = dot(jnp.concatenate([low_a, low_b], axis=1), halves(lo, xs))
            reach = jnp.exp(cum_x) * enter_ref[rows]
            if c > 0:
                y = y + reach * outside[:, cols]
            if c < chunks - 1:
                tail = jnp.exp(cum_x[Q - 1 : Q] - cum_x) * last_ref[rows]
                carry_ref[:, cols] = reach[Q - 1 : Q] * carry_ref[:, cols] + dot(
                    bt_ref[:, rows], (xs.astype(F32) * tail).astype(BF16)
                )
            y_ref[rows, cols] = y
            gate = gate_ref[rows, cols].astype(F32)
            gated = (y + skip_ref[:, cols] * x) * (gate * sigmoid(gate))
            square_ref[rows, :] += gated * gated
            gated_ref[rows, cols] = gated

    @pl.when(j == pl.num_programs(1) - 1)
    def _():
        total_ref[...] = jnp.sum(square_ref[...], axis=1, keepdims=True)


def backward_body(
    starts_ref, gate_ref, xin_ref, bc_ref, dt_ref, cw_ref, cb_ref, cwbc_ref, cbbc_ref,
    shift_ref, logd_ref, skip_ref, gain_ref, y_ref, state_ref, q_ref, mean_ref, dm_ref,
    before_ref, dgate_ref, dbc_ref, ddt_ref, sgain_ref, scw_ref, scb_ref, scwbc_ref, scbbc_ref,
    sshift_ref, slogd_ref, sskip_ref,
    same_ref, enter_ref, last_ref, bmat_ref, cmat_ref, ct_ref, score_ref, scoret_ref,
    x_ref, slope_ref, dy_ref, dxs_ref, carry_ref, step_ref, cum_ref, cumt_ref,
    dscore_ref, db_ref, dc_ref, v1_ref, v2_ref, v3_ref, v4_ref, dxin_ref,
):
    j = pl.program_id(1)
    length = gate_ref.shape[0]
    chunks = length // Q
    lo = lax.broadcasted_iota(jnp.int32, (Q, 128), 1) < HP

    def activate_bc(part):
        cols = slice(part * NS, (part + 1) * NS)
        return conv_forward(bc_ref[:, cols].astype(F32), cwbc_ref[:, cols], cbbc_ref[:, cols], same_ref)

    @pl.when(j == 0)
    def _():
        prepare_masks(starts_ref, length, same_ref, enter_ref, last_ref)
        both = []
        for part in range(2):
            conv = activate_bc(part)
            both.append(conv * sigmoid(conv))
        bmat, cmat = both
        bmat_ref[...] = bmat.astype(BF16)
        cmat_ref[...] = cmat.astype(BF16)
        bt = bmat.T
        ct_ref[...] = cmat.T.astype(BF16)
        for c in range(chunks):
            rows = slice(c * Q, (c + 1) * Q)
            score = jnp.dot(cmat[rows].astype(BF16), bt[:, rows].astype(BF16), preferred_element_type=F32)
            score = jnp.where(keep_mask(starts_ref, c), score, 0.0)
            score_ref[c] = score
            scoret_ref[c] = score.T
        dscore_ref[...] = jnp.zeros_like(dscore_ref)
        db_ref[...] = jnp.zeros_like(db_ref)
        dc_ref[...] = jnp.zeros_like(dc_ref)

    pre, step, rate, decay = step_rows(dt_ref, shift_ref, logd_ref)
    cum = cumulate(rate, chunks)
    cumt_ref[...] = cum
    cum_ref[...] = cum.T
    step_ref[...] = step.T
    carry_ref[...] = jnp.zeros_like(carry_ref)
    q = q_ref[...]
    mean = mean_ref[...]
    for p in range(PAIRS):
        cols = slice(p * 128, (p + 1) * 128)
        conv = conv_forward(xin_ref[:, cols].astype(F32), cw_ref[:, cols], cb_ref[:, cols], same_ref)
        sig = sigmoid(conv)
        x = conv * sig
        x_ref[:, cols] = x
        slope_ref[:, cols] = sig * (1.0 + conv - x)
        gate = gate_ref[:, cols].astype(F32)
        gsig = sigmoid(gate)
        silu = gate * gsig
        scanned = y_ref[:, cols] + skip_ref[:, cols] * x
        gated = scanned * silu
        scaled = dm_ref[:, cols].astype(F32) * q
        sgain_ref[0, :, cols] = jnp.sum(gated * scaled, axis=0, keepdims=True)
        d_gated = scaled * gain_ref[:, cols] - gated * mean
        dgate_ref[:, cols] = (d_gated * scanned * (gsig * (1.0 + gate - silu))).astype(dgate_ref.dtype)
        d_scanned = d_gated * silu
        dy_ref[:, cols] = d_scanned
        sskip_ref[0, :, cols] = jnp.sum(d_scanned * x, axis=0, keepdims=True)

    for c in reversed(range(chunks)):
        rows = slice(c * Q, (c + 1) * Q)
        score = score_ref[c]
        scoret = scoret_ref[c]
        d_state = carry_ref[...]
        d_state_low = d_state.astype(BF16)
        if c < chunks - 1:
            from_state = dot(bmat_ref[rows, :], d_state_low)
        d_score = dscore_ref[c]
        for p in range(PAIRS):
            cols = slice(p * 128, (p + 1) * 128)
            cum_a = jnp.broadcast_to(cum_ref[rows, 2 * p : 2 * p + 1], (Q, Q))
            cum_b = jnp.broadcast_to(cum_ref[rows, 2 * p + 1 : 2 * p + 2], (Q, Q))
            row_a = cumt_ref[2 * p : 2 * p + 1, rows]
            row_b = cumt_ref[2 * p + 1 : 2 * p + 2, rows]
            cum_x = jnp.where(lo, cum_a, cum_b)
            step_x = jnp.where(lo, step_ref[rows, 2 * p : 2 * p + 1], step_ref[rows, 2 * p + 1 : 2 * p + 2])
            x = x_ref[rows, cols]
            xs = (x * step_x).astype(BF16)
            xs_wide = xs.astype(F32)
            d_y = dy_ref[rows, cols]
            d_y_low = d_y.astype(BF16)
            pair = dot_nt(d_y_low, halves(lo, xs))
            d_score = d_score + pair[:, :Q] * jnp.exp(jnp.minimum(cum_a - row_a, 0.0))
            d_score = d_score + pair[:, Q:] * jnp.exp(jnp.minimum(cum_b - row_b, 0.0))
            up_a = (scoret * jnp.exp(jnp.minimum(row_a - cum_a, 0.0))).astype(BF16)
            up_b = (scoret * jnp.exp(jnp.minimum(row_b - cum_b, 0.0))).astype(BF16)
            d_xs = dot(jnp.concatenate([up_a, up_b], axis=1), halves(lo, d_y_low))
            v1_ref[rows, cols] = d_y_low.astype(F32) * y_ref[rows, cols] - xs_wide * d_xs
            reach = jnp.exp(cum_x) * enter_ref[rows]
            if c < chunks - 1:
                tail = jnp.exp(cum_x[Q - 1 : Q] - cum_x) * last_ref[rows]
                d_tail = tail * from_state[:, cols]
                v3_ref[rows, cols] = xs_wide * d_tail
                d_xs = d_xs + d_tail
                db_ref[rows, :] += dot_nt((xs_wide * tail).astype(BF16), d_state_low[:, cols])
                entered = state_ref[0, c, :, cols]
                v4_ref[c : c + 1, cols] = reach[Q - 1 : Q] * jnp.sum(
                    d_state[:, cols] * entered.astype(F32), axis=0, keepdims=True
                )
            else:
                v3_ref[rows, cols] = jnp.zeros((Q, 128), F32)
                v4_ref[c : c + 1, cols] = jnp.zeros((1, 128), F32)
            if c > 0:
                reached = (reach * d_y).astype(BF16)
                dc_ref[rows, :] += dot_nt(reached, state_ref[0, c, :, cols])
                carry_ref[:, cols] = reach[Q - 1 : Q] * d_state[:, cols] + dot(ct_ref[:, rows], reached)
            v2_ref[rows, cols] = x * d_xs
            dxs_ref[rows, cols] = step_x * d_xs + skip_ref[:, cols] * d_y
        dscore_ref[c] = d_score

    head = lax.broadcasted_iota(jnp.int32, (HB, BC), 0)
    lane = lax.broadcasted_iota(jnp.int32, (HB, BC), 1)
    pick = ((lane >= head * HP) & (lane < (head + 1) * HP)).astype(BF16)

    def by_head(values):
        high = values.astype(BF16)
        rest = (values - high.astype(F32)).astype(BF16)
        return dot_nt(pick, high) + dot_nt(pick, rest)

    h1 = by_head(v1_ref[...])
    h2 = by_head(v2_ref[...])
    h3 = by_head(v3_ref[...])
    h4 = by_head(v4_ref[...])
    rows_i = lax.broadcasted_iota(jnp.int32, (Q, Q), 0)
    cols_i = lax.broadcasted_iota(jnp.int32, (Q, Q), 1)
    suffix = (rows_i >= cols_i).astype(F32)
    prefix = (rows_i < cols_i).astype(F32)
    parts = []
    for c in range(chunks):
        rows = slice(c * Q, (c + 1) * Q)
        parts.append(
            jnp.dot(h1[:, rows], suffix, precision=highest, preferred_element_type=F32)
            + jnp.dot(h3[:, rows], prefix, precision=highest, preferred_element_type=F32)
            + h4[:, c : c + 1]
        )
    d_rate = jnp.concatenate(parts, axis=1)
    d_step = h2 - d_rate * decay
    d_raw = d_step * sigmoid(pre)
    ddt_ref[...] = d_raw
    sshift_ref[0] = jnp.sum(d_raw, axis=1, keepdims=True)
    slogd_ref[0] = jnp.sum(d_rate * rate, axis=1, keepdims=True)

    for p in range(PAIRS):
        cols = slice(p * 128, (p + 1) * 128)
        d_conv = dxs_ref[:, cols] * slope_ref[:, cols]
        d_in, s_w, s_b = conv_backward(d_conv, xin_ref[:, cols].astype(F32), cw_ref[:, cols], same_ref)
        dxin_ref[:, cols] = d_in.astype(dxin_ref.dtype)
        scw_ref[0, :, cols] = s_w
        scb_ref[0, :, cols] = s_b

    @pl.when(j == pl.num_programs(1) - 1)
    def _():
        for c in range(chunks):
            rows = slice(c * Q, (c + 1) * Q)
            masked = jnp.where(keep_mask(starts_ref, c), dscore_ref[c], 0.0)
            dc_ref[rows, :] += dot(masked.astype(BF16), bmat_ref[rows, :])
            db_ref[rows, :] += dot(masked.T.astype(BF16), cmat_ref[rows, :])
        for part, grad_ref in ((0, db_ref), (1, dc_ref)):
            cols = slice(part * NS, (part + 1) * NS)
            conv = activate_bc(part)
            sig = sigmoid(conv)
            d_conv = grad_ref[...] * (sig * (1.0 + conv - conv * sig))
            d_in, s_w, s_b = conv_backward(d_conv, bc_ref[:, cols].astype(F32), cwbc_ref[:, cols], same_ref)
            dbc_ref[:, cols] = d_in.astype(dbc_ref.dtype)
            scwbc_ref[0, :, cols] = s_w
            scbbc_ref[0, :, cols] = s_b


def backward_kernel(*refs):
    outputs_at = 18

    @pl.when(pl.program_id(2) == 0)
    def _():
        backward_body(*refs)

    @pl.when(pl.program_id(2) == 1)
    def _():
        refs[outputs_at + 1][...] = refs[-1][...]


def backward_first(*refs):
    backward_kernel(*refs[:18], None, *refs[18:])


def row_block(first, rows, offset=0):
    return pl.BlockSpec((rows, BC), lambda r, j, *s: (first + r, j + offset))


def columns(rows):
    return pl.BlockSpec((rows, BC), lambda r, j, *s: (0, j))


def whole(*shape):
    return pl.BlockSpec(shape, lambda r, j, *s: (0,) * len(shape))


def row_sums(rows):
    return pl.BlockSpec((1, rows, BC), lambda r, j, *s: (r, 0, j))


def common_specs(first, length, channels):
    heads = pl.BlockSpec((HB, 1), lambda r, j, *s: (j, 0))
    return [
        pl.BlockSpec(memory_space=pltpu.SMEM),
        row_block(first, length),
        row_block(first, length, channels // BC),
        pl.BlockSpec((length, 2 * NS), lambda r, j, *s: (first + r, 0)),
        pl.BlockSpec((HB, length), lambda r, j, *s: (j, first + r)),
        columns(CONVW),
        columns(1),
        whole(CONVW, 2 * NS),
        whole(1, 2 * NS),
        heads,
        heads,
        columns(1),
    ]


def mix_forward(first, length, starts, main, extra, dt_rows, conv_w, conv_b, cw_bc, cb_bc, shift, logd, skip_cols):
    rows = starts.shape[0]
    channels = main.shape[1] // 2
    chunks = length // Q
    vmem = pltpu.VMEM
    return pl.pallas_call(
        forward_kernel,
        grid=(rows, channels // BC),
        in_specs=common_specs(first, length, channels),
        out_specs=[
            row_block(0, length),
            row_block(0, length),
            pl.BlockSpec((1, chunks, NS, BC), lambda r, j: (r, 0, 0, j)),
            pl.BlockSpec((length, 1), lambda r, j: (r, 0)),
        ],
        out_shape=[
            jax.ShapeDtypeStruct((rows * length, channels), F32),
            jax.ShapeDtypeStruct((rows * length, channels), F32),
            jax.ShapeDtypeStruct((rows, chunks, NS, channels), BF16),
            jax.ShapeDtypeStruct((rows * length, 1), F32),
        ],
        scratch_shapes=[
            vmem((CONVW - 1, length, 128), F32),
            vmem((length, 128), F32),
            vmem((length, 128), F32),
            vmem((length, NS), BF16),
            vmem((NS, length), BF16),
            vmem((chunks, Q, Q), F32),
            vmem((length, 128), F32),
            vmem((length, BC), F32),
            vmem((NS, BC), F32),
            vmem((length, HB), F32),
            vmem((length, HB), F32),
            vmem((HB, length), F32),
        ],
        compiler_params=pltpu.CompilerParams(vmem_limit_bytes=48 * 1024 * 1024),
        name="mix_forward",
    )(starts, main, main, extra, dt_rows, conv_w, conv_b, cw_bc, cb_bc, shift, logd, skip_cols)


def mix_backward(
    first, total, length, before, starts, main, extra, dt_rows, conv_w, conv_b, cw_bc, cb_bc, shift, logd, skip_cols,
    gain, y, states, q, mean, d_mixed,
):
    rows = starts.shape[0]
    channels = main.shape[1] // 2
    heads = channels // HP
    blocks = channels // BC
    chunks = length // Q
    vmem = pltpu.VMEM
    per_head = pl.BlockSpec((1, HB, 1), lambda r, j, s: (r, j, 0))
    col = pl.BlockSpec((length, 1), lambda r, j, s: (first + r, 0))
    shape = jax.ShapeDtypeStruct
    operands = (
        starts, main, main, extra, dt_rows, conv_w, conv_b, cw_bc, cb_bc, shift, logd, skip_cols,
        gain, y, states, q, mean, d_mixed,
    )
    in_specs = common_specs(first, length, channels) + [
        columns(1),
        row_block(0, length),
        pl.BlockSpec((1, chunks, NS, BC), lambda r, j, s: (r, 0, 0, j)),
        col,
        col,
        row_block(first, length),
    ]
    aliases = {}
    if before is not None:
        aliases = {len(operands): 0}
        operands = operands + (before,)
        in_specs = in_specs + [pl.BlockSpec(memory_space=pl.ANY)]
    return pl.pallas_call(
        backward_first if before is None else backward_kernel,
        grid=(rows, blocks, 2),
        in_specs=in_specs,
        out_specs=[
            pl.BlockSpec((length, BC), lambda r, j, s: (first + r, j + blocks * s)),
            pl.BlockSpec((length, 2 * NS), lambda r, j, s: (r, 0)),
            pl.BlockSpec((HB, length), lambda r, j, s: (j, r)),
            row_sums(1),
            row_sums(CONVW),
            row_sums(1),
            pl.BlockSpec((1, CONVW, 2 * NS), lambda r, j, s: (r, 0, 0)),
            pl.BlockSpec((1, 1, 2 * NS), lambda r, j, s: (r, 0, 0)),
            per_head,
            per_head,
            row_sums(1),
        ],
        out_shape=[
            shape((total * length, 2 * channels), BF16),
            shape((rows * length, 2 * NS), BF16),
            shape((heads, rows * length), F32),
            shape((rows, 1, channels), F32),
            shape((rows, CONVW, channels), F32),
            shape((rows, 1, channels), F32),
            shape((rows, CONVW, 2 * NS), F32),
            shape((rows, 1, 2 * NS), F32),
            shape((rows, heads, 1), F32),
            shape((rows, heads, 1), F32),
            shape((rows, 1, channels), F32),
        ],
        scratch_shapes=[
            vmem((CONVW - 1, length, 128), F32),
            vmem((length, 128), F32),
            vmem((length, 128), F32),
            vmem((length, NS), BF16),
            vmem((length, NS), BF16),
            vmem((NS, length), BF16),
            vmem((chunks, Q, Q), F32),
            vmem((chunks, Q, Q), F32),
            vmem((length, BC), F32),
            vmem((length, BC), F32),
            vmem((length, BC), F32),
            vmem((length, BC), F32),
            vmem((NS, BC), F32),
            vmem((length, HB), F32),
            vmem((length, HB), F32),
            vmem((HB, length), F32),
            vmem((chunks, Q, Q), F32),
            vmem((length, NS), F32),
            vmem((length, NS), F32),
            vmem((length, BC), F32),
            vmem((length, BC), F32),
            vmem((length, BC), F32),
            vmem((8, BC), F32),
            vmem((length, BC), BF16),
        ],
        input_output_aliases=aliases,
        compiler_params=pltpu.CompilerParams(vmem_limit_bytes=48 * 1024 * 1024),
        name="mix_backward",
    )(*operands)


MAIN = 2 * DI
EXTRA = 2 * NS + NH


def adam_direction(weight, gradient, first, second, decayed):
    first_new = BETA_ONE * first + (1.0 - BETA_ONE) * gradient
    second_new = BETA_TWO * second + (1.0 - BETA_TWO) * gradient * gradient
    first_hat = first_new / (1.0 - BETA_ONE**adam_step)
    second_hat = second_new / (1.0 - BETA_TWO**adam_step)
    direction = first_hat / (jnp.sqrt(second_hat) + ADAM_EPS)
    if decayed:
        direction = direction + DECAY_RATE * weight
    return (direction, first_new, second_new)


def swap(value, axis, mask):
    size = lax.axis_size(axis)
    return lax.ppermute(value, axis, [(i, i ^ mask) for i in range(size)])


def bits_of(size):
    return [1 << b for b in reversed(range(size.bit_length() - 1))]


def place(buffer, shape, block, at, items):
    arrays, copies, table = [], [], [at[0], at[1]]
    for array, lead, row, col, valid, cuts in items:
        if not any(array is a for a in arrays):
            arrays.append(array)
        source = [array is a for a in arrays].index(True)
        for start, end in zip(cuts[:-1], cuts[1:]):
            copies.append((source, lead, start, end - start))
            table.extend([row, col, valid])
    table = jnp.stack([jnp.asarray(v, jnp.int32) for v in table])
    operands = [table] + arrays + ([] if buffer is None else [buffer])

    def kernel(table_ref, *refs):
        out_ref = refs[-1]
        for i, (source, lead, start, size) in enumerate(copies):
            piece = refs[source]
            row = pl.multiple_of(table_ref[3 * i + 2] + start, 16)
            col = pl.multiple_of(table_ref[3 * i + 3], 128)

            @pl.when(table_ref[3 * i + 4] > start)
            def _():
                rows = pl.ds(start, size)
                value = piece[rows, :] if lead is None else piece[lead, rows, :]
                out_ref[pl.ds(row, size), pl.ds(col, value.shape[1])] = value

    def all_of(a):
        return pl.BlockSpec(a.shape, lambda i, t: (0,) * a.ndim)

    return pl.pallas_call(
        kernel,
        grid_spec=pltpu.PrefetchScalarGridSpec(
            num_scalar_prefetch=1,
            grid=(1,),
            in_specs=[all_of(a) for a in arrays] + ([] if buffer is None else [pl.BlockSpec(memory_space=pl.ANY)]),
            out_specs=pl.BlockSpec(block, lambda i, t: (t[0], t[1])),
        ),
        out_shape=jax.ShapeDtypeStruct(shape, BF16),
        input_output_aliases={} if buffer is None else {len(operands) - 1: 0},
        compiler_params=pltpu.CompilerParams(vmem_limit_bytes=32 * 1024 * 1024),
        name="place",
    )(*operands)


def rows_into(buffer, row, rows, pieces, gain=None):
    size, width = sum(p.shape[0] for p in pieces), pieces[0].shape[1]
    operands = list(pieces) + ([] if gain is None else [gain]) + ([] if buffer is None else [buffer])

    def kernel(*refs):
        at = 0
        for i, piece in enumerate(pieces):
            for start in range(0, piece.shape[0], 128):
                value = refs[i][start : start + 128, :]
                if gain is not None:
                    value = value.astype(F32)
                    mean = jnp.mean(value * value, axis=1, keepdims=True)
                    value = (value * lax.rsqrt(mean + EPSILON) * refs[len(pieces)][...]).astype(BF16)
                refs[-1][at + start : at + start + 128, :] = value
            at += piece.shape[0]

    specs = [pl.BlockSpec(p.shape, lambda i: (0, 0)) for p in operands]
    if buffer is not None:
        specs[-1] = pl.BlockSpec(memory_space=pl.ANY)
    return pl.pallas_call(
        kernel,
        grid=(1,),
        in_specs=specs,
        out_specs=pl.BlockSpec((size, width), lambda i: (row, 0)),
        out_shape=jax.ShapeDtypeStruct((rows * size, width), BF16),
        input_output_aliases={} if buffer is None else {len(operands) - 1: 0},
        compiler_params=pltpu.CompilerParams(vmem_limit_bytes=32 * 1024 * 1024),
        name="rows_into",
    )(*operands)


def prefix_count(g, n, unit, period):
    return (n // period) * unit + jnp.clip(n % period - g * unit, 0, unit)


def static_count(g, n, unit, period):
    return (n // period) * unit + min(max(n % period - g * unit, 0), unit)


def then(value, *earlier):
    return lax.optimization_barrier((value,) + earlier)[0]


def spread_z(bundle, masks, late=()):
    have, order = bundle[None], [0]
    for i, mask in enumerate(masks):
        if i > 0:
            have = then(have, *late)
        have = jnp.concatenate([have, swap(have, "dp", 2 * mask)])
        order = order + [rel ^ mask for rel in order]
    return have, order


def grouped(tokens, cotangent, doc_starts, valid_len, weights, firsts, seconds):
    w_in, w_out, norm_gain, gate_gain, conv_w, conv_b, dt_bias, a_log, d_skip = weights
    small = weights[2:]
    dp, groups = lax.axis_size("dp"), lax.axis_size("fsdp")
    zs = dp // 2
    d, f = lax.axis_index("dp"), lax.axis_index("fsdp")
    z, c = d // 2, d % 2
    z_masks = bits_of(zs)
    length, width = tokens.shape[1], tokens.shape[2]
    local = DI // groups
    unit = local // groups
    k_rows, per_dev = w_in.shape
    k_half = k_rows // 2
    per_chip = 2 * per_dev
    out_cols = w_out.shape[1]
    sizes = {
        (zz, g): static_count(g, min(per_chip * (zz + 1), MAIN), unit, local)
        - static_count(g, min(per_chip * zz, MAIN), unit, local)
        for zz in range(zs)
        for g in range(groups)
    }
    cuts = [0] + sorted(set(sizes.values()) - {0})
    most = cuts[-1]

    def first_row(zz):
        return prefix_count(f, jnp.minimum(per_chip * zz, MAIN), unit, local)

    def rows_valid(zz):
        return first_row(zz + 1) - first_row(zz)

    def slice_row(row):
        return jnp.minimum(row, 2 * local - most)

    low = w_in.astype(BF16)
    mine = lax.dynamic_slice_in_dim(low, k_half * c, k_half, 0)
    other = swap(lax.dynamic_slice_in_dim(low, k_half * (1 - c), k_half, 0), "dp", 1)
    chip = jnp.concatenate([jnp.where(c == 0, mine, other), jnp.where(c == 0, other, mine)], axis=1)
    half = length // 2

    def neighbours(row, which):
        parts = (row[:half], row[half:])
        return [swap(parts[which], "fsdp", 1), swap(parts[1 - which], "fsdp", 2)]

    def corners(first):
        return [swap(first[0], "fsdp", 2), swap(first[1], "fsdp", 1)]

    def pieces_of(first, second, third):
        return [[first[0], second[0]], [second[1], first[1]], third]

    near = neighbours(tokens[0], 0)
    chip = then(chip, *near)
    column = per_chip * z + jnp.arange(per_chip, dtype=jnp.int32)
    owner = (column // unit) % groups
    begin = prefix_count(owner, per_chip * z, unit, local)
    rank = prefix_count(owner, column, unit, local) - begin
    moved = begin - slice_row(begin)
    extra_key = groups * most + column - MAIN
    places = jnp.arange(groups * most + EXTRA, dtype=jnp.int32)[:, None]

    def picks(ranks):
        key = jnp.where(column < MAIN, (owner ^ f) * most + ranks, extra_key)
        return (places == key[None, :]).astype(BF16)

    parts = dot_nt(picks(rank), chip).astype(BF16)

    def own_channels(v):
        v = v.reshape(v.shape[0], groups, groups, -1)
        return lax.dynamic_index_in_dim(v, f, 2, keepdims=False).reshape(v.shape[0], -1)

    blocks = [parts[m * most : (m + 1) * most] for m in range(groups)]
    blocks = blocks[:1] + [swap(blocks[m], "fsdp", m) for m in range(1, groups)]
    first = jnp.concatenate([blocks[0], parts[groups * most :]])[None]
    second = jnp.concatenate(blocks[1:])[None]
    got = swap(first, "dp", 2 * z_masks[0])
    first_2 = jnp.concatenate([first, got])
    sent_a = then(first_2, second)
    sent_b = then(second, first_2)
    got_a = swap(sent_a, "dp", 2 * z_masks[1])
    got_b = swap(sent_b, "dp", 2 * z_masks[0])
    far = corners([then(v, sent_a) for v in near])
    near_2 = neighbours(then(tokens[0], sent_a), 1)
    marks = jnp.concatenate([doc_starts[0], valid_len])
    marks = jnp.concatenate([(marks // 32).astype(BF16), (marks % 32).astype(BF16)])
    flat = then(jnp.concatenate([marks] + [v.astype(BF16).reshape(-1) for v in small])[None], first_2)
    rel_small = jnp.concatenate([flat] + [swap(flat, "fsdp", m) for m in range(1, groups)])
    count = marks.shape[0] // 2
    marks = rel_small[:, : 2 * count].astype(jnp.int32)
    marks = marks[:, :count] * 32 + marks[:, count:]
    rel_small = rel_small[:, 2 * count :]
    order = jnp.arange(groups, dtype=jnp.int32) ^ f
    every = jnp.sum(
        jnp.where((order[None, :] == jnp.arange(groups)[:, None])[:, :, None], rel_small[None], 0), axis=1
    ).astype(F32)
    full, at = [], 0
    for v in small:
        piece = every[:, at : at + v.size]
        at += v.size
        if v.ndim == 1:
            full.append(piece.reshape(1, -1))
        else:
            full.append(jnp.moveaxis(piece.reshape((-1,) + v.shape), 0, 1).reshape(v.shape[0], -1))
    norm_full, gate_full, convw_full, convb_full, shift_full, logd_full, skip_full = full

    hidden = tokens[0].astype(F32)
    upstream = cotangent[0].astype(F32)
    live = (jnp.arange(length, dtype=jnp.int32) < valid_len[0]).astype(F32)[:, None]
    starts = marks[:, :-1]
    live_all = jnp.concatenate([(jnp.arange(length) < marks[r, -1]).astype(F32)[:, None] for r in range(groups)])

    second_2 = then(jnp.concatenate([second, got_b]), got_a, *near_2)
    got_b2 = swap(second_2, "dp", 2 * z_masks[1])
    spread_a = jnp.concatenate([first_2, got_a])
    order_z = [0, z_masks[0]] + [z_masks[1], z_masks[0] ^ z_masks[1]]
    sibling_a = swap(then(spread_a, second_2), "dp", 1)
    sibling_b = swap(second_2, "dp", 1)
    near_pieces = pieces_of(near, near_2, far)
    normed_all = None
    for m in range(groups - 1):
        row = [then(tokens[0], second_2)] if m == 0 else near_pieces[m - 1]
        normed_all = rows_into(normed_all, m, groups, row, norm_full)
    extra_at = jnp.stack([jnp.int32(r) for r in order_z]) == (z ^ (zs - 1))
    extra_at = jnp.sum(jnp.where(extra_at, jnp.arange(zs, dtype=jnp.int32), 0))
    extra_own = lax.dynamic_index_in_dim(then(spread_a, second_2), extra_at, 0, keepdims=False)[most:]
    extra_got = jnp.stack([extra_own] + [swap(extra_own, "fsdp", m) for m in range(1, groups)])
    extra_got = then(extra_got, normed_all)
    extra_pair = [extra_got, swap(extra_got, "dp", 1)]
    up_near = neighbours(then(cotangent[0], second_2), 0)
    got_b2 = then(got_b2, normed_all, *far)
    sibling_b2 = swap(got_b2, "dp", 1)
    normed_all = rows_into(then(normed_all, got_b2), groups - 1, groups, near_pieces[-1], norm_full)
    bundles_in = [
        [(spread_a, range(zs))],
        [(second_2, range(2)), (got_b2, range(2, zs))],
        [(sibling_a, range(zs))],
        [(sibling_b, range(2)), (sibling_b2, range(2, zs))],
    ]
    w_main = None
    for rc in range(2):
        for m in range(groups):
            items, skip = [], 0 if m == 0 else most * (m - 1)
            for array, ranks in bundles_in[2 * rc + (m > 0)]:
                for at, i in enumerate(ranks):
                    zz = z ^ order_z[i]
                    valid = rows_valid(zz) + skip
                    items.append((array, at, first_row(zz) - skip, 0, valid, [e + skip for e in cuts]))
            w_main = place(w_main, (2 * local, width), (2 * local, k_half), (0, 2 * (f ^ m) + (c ^ rc)), items)
    extra_items = []
    for m in range(groups):
        for rc in range(2):
            extra_items.append((extra_pair[rc], m, 0, k_rows * (f ^ m) + k_half * (c ^ rc), EXTRA, (0, EXTRA)))
    w_extra = place(None, (EXTRA, width), (EXTRA, width), (0, 0), extra_items)

    out_low = w_out.astype(BF16).reshape(groups, unit, out_cols)
    blocks = [lax.dynamic_index_in_dim(out_low, f ^ m, 0, keepdims=False) for m in range(groups)]
    blocks = jnp.concatenate([blocks[0]] + [swap(blocks[m], "fsdp", m) for m in range(1, groups)])
    out_1 = then(blocks[None], w_main)
    out_2 = jnp.concatenate([out_1, swap(out_1, "dp", 2 * z_masks[0])])
    out_got = swap(out_2, "dp", 2 * z_masks[1])
    out_spread = jnp.concatenate([out_2, out_got])
    out_items = []
    for rc, array in enumerate((out_spread, swap(out_spread, "dp", 1))):
        for i, rel in enumerate(order_z):
            col = out_cols * (2 * (z ^ rel) + (c ^ rc))
            for m in range(groups):
                out_items.append((array, i, unit * (f ^ m) - unit * m, col, local, (unit * m, unit * (m + 1))))
    w_out_own = place(None, (local, width), (local, width), (0, 0), out_items)
    up_near_2 = neighbours(then(cotangent[0], w_main), 1)
    up_far = corners([then(v, w_main) for v in up_near])

    extra = dot_nt(normed_all, w_extra)
    main = dot_nt(then(normed_all, extra), w_main)
    raw_dt = extra[:, 2 * NS :].reshape(-1, groups, groups, NH // groups // groups)
    dt_rows = lax.dynamic_index_in_dim(raw_dt, f, 2, keepdims=False).reshape(groups * length, -1).T
    common = (
        main, extra, dt_rows,
        own_channels(convw_full[:, :DI]), own_channels(convb_full[:, :DI]), convw_full[:, DI:], convb_full[:, DI:],
        own_channels(shift_full).T, own_channels(logd_full).T, own_channels(jnp.repeat(skip_full, HP, axis=1)),
    )
    due = [[out_2, *up_near_2], [out_spread, *up_far]]
    up_pieces = pieces_of(up_near, up_near_2, up_far)
    half_rows = groups // 2
    results = []
    for i in range(2):
        begin = then(starts[i * half_rows : (i + 1) * half_rows], *due[i], *[v[3] for v in results])
        results.append(mix_forward(i * half_rows, length, begin, *common))
    gated, y, states, squares = zip(*results)
    gain = own_channels(gate_full)

    def group_sum(v):
        for mask in bits_of(groups):
            got = swap(v, "fsdp", mask)
            v = v + jnp.stack([got[r ^ mask] for r in range(groups)])
        return v

    squares = group_sum(jnp.concatenate(squares).reshape(groups, length))
    q = lax.rsqrt(squares.reshape(-1, 1) * (1.0 / DI) + EPSILON)
    mixed = jnp.concatenate(
        [(g * q[i * half_rows * length : (i + 1) * half_rows * length] * gain).astype(BF16) for i, g in enumerate(gated)]
    )
    upstream_all = None
    for m in range(groups):
        upstream_all = rows_into(upstream_all, m, groups, [cotangent[0]] if m == 0 else up_pieces[m - 1])
    mixed_live = mixed * live_all.astype(BF16)
    d_mixed = (dot_nt(upstream_all, w_out_own) * live_all).astype(BF16)
    inner = jnp.sum(mixed.astype(F32) * d_mixed.astype(F32), axis=1).reshape(groups, length)
    mean = q * q * group_sum(inner).reshape(-1, 1) * (1.0 / DI)

    def sum_low(a, b):
        return (a.astype(F32) + b.astype(F32)).astype(BF16)

    def rows_home(partial):
        pieces, sent = [], []
        for at, (one, two) in ((0, (1, 2)), (half, (2, 1))):
            rows = [partial[m * length + at : m * length + at + half] for m in range(groups)]
            got = swap(jnp.concatenate([rows[one], rows[3]]), "fsdp", one)
            passed = sum_low(rows[two], got[half:])
            sent.append(passed)
            pieces.append((rows[0], got[:half], swap(passed, "fsdp", two)))
        return pieces, sent

    def added(pieces):
        return jnp.concatenate([a.astype(F32) + b.astype(F32) + c.astype(F32) for a, b, c in pieces])

    contract = (((0,), (0,)), ((), ()))

    def sum_rows(a, b):
        return with_layout_constraint(
            lax.dot_general(a, b, contract, preferred_element_type=F32).astype(BF16), Layout((0, 1))
        )


    def out_columns(core):
        cols = [lax.dynamic_slice_in_dim(upstream_all, out_cols * (2 * i + core), out_cols, 1) for i in range(zs)]
        return jnp.concatenate(cols, axis=1)

    out_theirs = swap(sum_rows(mixed_live, out_columns(1 - c)), "dp", 1)
    out_ours = sum_rows(mixed_live, out_columns(c))
    branch_home, branch_sent = rows_home(dot(then(mixed, mean), w_out_own).astype(BF16))
    out_sum = sum_low(out_ours, out_theirs)
    flying = [lax.dynamic_slice_in_dim(out_sum, out_cols * (z ^ r), out_cols, 1) for r in range(zs)]
    d_main, backs = None, []
    operand = d_mixed
    for i in range(2):
        if i < len(z_masks):
            mask = z_masks[-1 - i]
            sent = jnp.stack(flying[1::2])
            operand = then(d_mixed, sent, *([] if i == 0 else branch_sent))
            got = swap(sent, "dp", 2 * mask)
            keep = flying[0::2]
        begin = starts[i * half_rows : (i + 1) * half_rows]
        result = mix_backward(
            i * half_rows, groups, length, d_main, begin, *common, gain, y[i], states[i], q, mean, operand
        )
        d_main = result[0]
        if i < len(z_masks):
            got = then(got, d_main)
            flying = [sum_low(k, got[j]) for j, k in enumerate(keep)]
        backs.append(result[1:])
    for mask in z_masks[::-1][2:]:
        got = swap(jnp.stack(flying[1::2]), "dp", 2 * mask)
        flying = [sum_low(k, got[j]) for j, k in enumerate(flying[0::2])]
    out_rows = [lax.dynamic_slice_in_dim(flying[0], unit * (f ^ m), unit, 0) for m in range(groups)]
    out_parts = jnp.stack([out_rows[0]] + [swap(out_rows[m], "fsdp", m) for m in range(1, groups)])
    d_bc_in = jnp.concatenate([b[0] for b in backs])
    d_dt = jnp.concatenate([b[1] for b in backs], axis=1)
    s_gain, s_cw, s_cb, s_cwbc, s_cbbc, s_shift, s_logd, s_skip = [
        sum(p.sum(axis=0) for p in v) for v in list(zip(*backs))[2:]
    ]
    here = (jnp.arange(groups, dtype=jnp.int32) == f).astype(F32)

    def all_channels(v):
        v = v.reshape(v.shape[0], groups, 1, -1)
        return (v * here[None, None, :, None]).reshape(v.shape[0], -1)

    d_extra = jnp.concatenate([d_bc_in, all_channels(d_dt.T).astype(BF16)], axis=1)

    bundles = [(groups - 2, groups - 1), (0, 1)]

    def bundle_sum(source, bundle, rc):
        block = [lax.dynamic_slice_in_dim(normed_all, k_rows * (f ^ m) + k_half * (c ^ rc), k_half, 1) for m in bundle]
        return sum_rows(source, jnp.concatenate(block, axis=1))

    def chip_blocks(ours, got):
        blocks = []
        for r in range(zs):
            row = slice_row(first_row(z ^ r))
            blocks.append(sum_low(*[lax.dynamic_slice_in_dim(v, row, most, 0) for v in (ours, got)]))
        return blocks

    def send_z(blocks, mask):
        sent = jnp.stack(blocks[1::2])
        return blocks[0::2], swap(sent, "dp", 2 * mask), sent

    def add_z(flying):
        keep, got, _ = flying
        return [sum_low(k, got[i]) for i, k in enumerate(keep)]

    extra_sum = sum_rows(d_extra, normed_all)
    halves_e = extra_sum.reshape(EXTRA, groups, 2, k_half)
    extra_theirs = swap(lax.dynamic_index_in_dim(halves_e, 1 - c, 2, keepdims=False), "dp", 1)
    extra_ours = lax.dynamic_index_in_dim(halves_e, c, 2, keepdims=False)
    theirs_a = bundle_sum(then(d_main, extra_sum), bundles[0], 1)
    got_a = swap(theirs_a, "dp", 1)
    ours_a = bundle_sum(then(d_main, theirs_a), bundles[0], 0)
    both = then(extra_ours.astype(F32) + extra_theirs.astype(F32), ours_a)
    flying_a = send_z(chip_blocks(ours_a, got_a), z_masks[-1])
    theirs_b = bundle_sum(then(d_main, flying_a[2]), bundles[1], 1)
    got_b = swap(theirs_b, "dp", 1)
    ours_b = bundle_sum(then(d_main, theirs_b), bundles[1], 0)
    total = lax.dynamic_index_in_dim(both, f, 1, keepdims=False)
    for m in range(1, groups):
        total = total + swap(
            lax.dynamic_index_in_dim(both, f ^ m, 1, keepdims=False).astype(BF16), "fsdp", m
        ).astype(F32)
    total = then(total.astype(BF16), ours_b)
    flying_b = send_z([then(v, total) for v in chip_blocks(ours_b, got_b)], z_masks[-1])
    partial = (dot(then(d_main, flying_b[2]), w_main) + dot(d_extra, w_extra)).astype(BF16)
    d_normed_home, d_normed_sent = rows_home(partial)
    held = [partial, *[v for piece in branch_home for v in piece]]
    flying_a = send_z([then(v, *held) for v in add_z(flying_a)], z_masks[0])
    total = sum_low(total, swap(then(total, flying_a[2]), "dp", 2 * z_masks[-1]))
    flying_b = send_z([then(v, flying_a[2]) for v in add_z(flying_b)], z_masks[0])
    total = sum_low(total, swap(then(total, flying_b[2]), "dp", 2 * z_masks[0]))
    flying_a = (flying_a[0], then(flying_a[1], flying_b[2]), None)
    flying_b = (flying_b[0], then(flying_b[1], *d_normed_sent), None)
    recv = [None] * groups
    for flying, bundle in ((flying_a, bundles[0]), (flying_b, bundles[1])):
        block = add_z(flying)[0]
        for i, m in enumerate(bundle):
            piece = block[:, i * k_half : (i + 1) * k_half]
            recv[m] = piece if m == 0 else swap(piece, "fsdp", m)


    out_parts = then(out_parts, flying_a[1])
    grad_out = jnp.concatenate(
        [lax.dynamic_index_in_dim(out_parts, f ^ g, 0, keepdims=False) for g in range(groups)]
    ).astype(F32)
    blocks = jnp.concatenate(recv + [total])
    grad_chip = lax.dot_general(blocks, picks(rank + moved), contract, preferred_element_type=F32).astype(BF16)
    left, right = grad_chip[:, :per_dev], grad_chip[:, per_dev:]
    own = jnp.where(c == 0, left, right)
    got = swap(jnp.where(c == 0, right, left), "dp", 1)
    grad_in = jnp.concatenate([jnp.where(c == 0, own, got), jnp.where(c == 0, got, own)]).astype(F32)

    out_tokens = (hidden + added(branch_home) * live).astype(BF16)
    d_normed = added(d_normed_home)
    scale = lax.rsqrt(jnp.mean(hidden * hidden, axis=-1, keepdims=True) + EPSILON)
    weighted = norm_full * d_normed
    average = jnp.mean(hidden * weighted, axis=-1, keepdims=True)
    grad_tokens = upstream + scale * weighted - hidden * (scale * scale * scale * average)
    s_norm = jnp.sum(hidden * scale * d_normed, axis=0)

    small_sums = (
        s_norm[None],
        all_channels(s_gain),
        jnp.concatenate([all_channels(s_cw), s_cwbc], axis=1),
        jnp.concatenate([all_channels(s_cb), s_cbbc], axis=1),
        all_channels(s_shift.T),
        all_channels(s_logd.T),
        all_channels(s_skip.reshape(1, -1, HP).sum(axis=2)),
    )
    flat = jnp.concatenate(
        [jnp.moveaxis(s.reshape(s.shape[0], groups, -1), 1, 0).reshape(groups, -1) for s in small_sums], axis=1
    )
    mine = lax.dynamic_index_in_dim(flat, f, 0, keepdims=True)
    for m in range(1, groups):
        mine = mine + swap(lax.dynamic_index_in_dim(flat, f ^ m, 0, keepdims=True), "fsdp", m)
    for mask in bits_of(dp):
        mine = mine + swap(mine, "dp", mask)
    return out_tokens, grad_tokens, (grad_in, grad_out) + split_small(mine[0], small)


def split_small(flat, small):
    result, at = [], 0
    for v in small:
        result.append(flat[at : at + v.size].reshape(v.shape))
        at += v.size
    return tuple(result)


def alone(tokens, cotangent, doc_starts, valid_len, weights, firsts, seconds):
    w_in, w_out = weights[:2]
    small = weights[2:]
    length = tokens.shape[1]
    hidden = tokens[0].astype(F32)
    upstream = cotangent[0].astype(F32)
    flat = jnp.concatenate([v.astype(BF16).reshape(-1) for v in small])
    every = lax.all_gather(flat, "fsdp", axis=0, tiled=False)
    full, at = [], 0
    for v in small:
        piece = every[:, at : at + v.size].astype(F32)
        at += v.size
        if v.ndim == 1:
            full.append(piece.reshape(1, -1))
        else:
            full.append(jnp.moveaxis(piece.reshape((-1,) + v.shape), 0, 1).reshape(v.shape[0], -1))
    norm_full, gate_full, convw_full, convb_full, shift_full, logd_full, skip_full = full
    in_full = lax.all_gather(
        lax.all_gather(w_in.astype(BF16), "dp", axis=1, tiled=True), "fsdp", axis=0, tiled=True
    )
    out_full = lax.all_gather(
        lax.all_gather(w_out.astype(BF16), "dp", axis=1, tiled=True), "fsdp", axis=0, tiled=True
    )
    scale = lax.rsqrt(jnp.mean(hidden * hidden, axis=-1, keepdims=True) + EPSILON)
    normed = (hidden * scale * norm_full).astype(BF16)
    projected = dot(normed, in_full)
    extra = projected[:, MAIN:]
    common = (
        projected[:, :MAIN], extra, extra[:, 2 * NS :].T, convw_full[:, :DI], convb_full[:, :DI],
        convw_full[:, DI:], convb_full[:, DI:], shift_full.T, logd_full.T, jnp.repeat(skip_full, HP, axis=1),
    )
    gated, y, states, squares = mix_forward(0, length, doc_starts, *common)
    q = lax.rsqrt(squares * (1.0 / DI) + EPSILON)
    mixed = (gated * q * gate_full).astype(BF16)
    live = (jnp.arange(length, dtype=jnp.int32) < valid_len[0]).astype(F32)[:, None]
    d_branch = (upstream * live).astype(BF16)
    out_tokens = (hidden + dot(mixed, out_full) * live).astype(BF16)
    d_mixed = dot_nt(d_branch, out_full)
    mean = q * q * jnp.sum(mixed.astype(F32) * d_mixed, axis=1, keepdims=True) * (1.0 / DI)
    d_main, d_bc_in, d_dt, *sums = mix_backward(
        0, 1, length, None, doc_starts, *common, gate_full, y, states, q, mean, d_mixed
    )
    s_gain, s_cw, s_cb, s_cwbc, s_cbbc, s_shift, s_logd, s_skip = [v[0] for v in sums]
    d_low = jnp.concatenate([d_main, d_bc_in, d_dt.T.astype(BF16)], axis=1)
    d_normed = dot_nt(d_low, in_full)
    weighted = norm_full * d_normed
    average = jnp.mean(hidden * weighted, axis=-1, keepdims=True)
    grad_tokens = upstream + scale * weighted - hidden * (scale * scale * scale * average)
    s_norm = jnp.sum(hidden * scale * d_normed, axis=0)
    contract = (((0,), (0,)), ((), ()))
    out_sum = lax.dot_general(mixed, d_branch, contract, preferred_element_type=F32).astype(BF16)
    in_sum = lax.dot_general(normed, d_low, contract, preferred_element_type=F32).astype(BF16)
    grads = []
    for total in (in_sum, out_sum):
        total = lax.psum_scatter(total, "fsdp", scatter_dimension=0, tiled=True)
        grads.append(lax.psum_scatter(total, "dp", scatter_dimension=1, tiled=True).astype(F32))
    sums = (
        s_norm[None],
        s_gain,
        jnp.concatenate([s_cw, s_cwbc], axis=1),
        jnp.concatenate([s_cb, s_cbbc], axis=1),
        s_shift.T,
        s_logd.T,
        s_skip.reshape(1, NH, HP).sum(axis=2),
    )
    parts = lax.axis_size("fsdp")
    flat = jnp.concatenate(
        [jnp.moveaxis(s.reshape(s.shape[0], parts, -1), 1, 0).reshape(parts, -1) for s in sums], axis=1
    )
    total = lax.psum(flat, ("dp", "fsdp"))
    mine = lax.dynamic_index_in_dim(total, lax.axis_index("fsdp"), 0, keepdims=False)
    return out_tokens, grad_tokens, tuple(grads) + split_small(mine, small)


def regular(w_in, dp, groups):
    zs = dp // 2
    if dp % 2 or zs & (zs - 1) or zs < 4 or groups & (groups - 1) or DI % (groups * groups * 128):
        return False
    local = DI // groups
    per_chip = 2 * w_in.shape[1]
    edges = [
        static_count(g, min(per_chip * zz, MAIN), local // groups, local) for zz in range(zs + 1) for g in range(groups)
    ]
    return local % BC == 0 and groups == 4 and zs == 4 and all(e % 16 == 0 for e in edges) and w_in.shape[0] % 256 == 0


def shards(tokens, cotangent, doc_starts, valid_len, *rest):
    weights, moments = rest[:9], rest[9:]
    firsts, seconds = moments[0::2], moments[1::2]
    dp, groups = lax.axis_size("dp"), lax.axis_size("fsdp")
    plan = grouped if regular(weights[0], dp, groups) else alone
    out_tokens, grad_tokens, grads = plan(tokens, cotangent, doc_starts, valid_len, weights, firsts, seconds)
    factor = 1.0 / math.sqrt(tokens.shape[0] * tokens.shape[1] * dp * groups)
    decay_flags = (True, True, False, False, True, True, False, False, False)
    results = []
    for i, (weight, gradient, first, second) in enumerate(zip(weights, grads, firsts, seconds)):
        direction, first_new, second_new = adam_direction(weight, gradient * factor, first, second, decay_flags[i])
        if i < 2:
            direction = weight - LEARN_RATE * direction
        results.extend((direction, first_new, second_new))
    return (out_tokens[None], grad_tokens[None]) + tuple(results)


def solution(mesh):
    rows3 = P(("dp", "fsdp"), None, None)
    both, split, last = P("fsdp", "dp"), P("fsdp"), P(None, "fsdp")
    small = (split, split, last, split, split, split, split)
    placed = (rows3, rows3, P(("dp", "fsdp"), None), P(("dp", "fsdp")), both, both) + small
    placed = placed + (both,) * 4 + tuple(s for s in small for _ in range(2))
    out = (rows3, rows3) + (both,) * 6 + tuple(s for s in small for _ in range(3))
    return jax.shard_map(shards, mesh=mesh, in_specs=placed, out_specs=out, check_vma=False)
```

```python
import functools
import math

import jax
import jax.numpy as jnp
from jax import lax
from jax.experimental import pallas as pl
from jax.experimental.layout import Layout, with_layout_constraint
from jax.experimental.pallas import tpu as pltpu
from jax.sharding import PartitionSpec as P

NH = 64
HP = 64
NS = 128
CONVW = 4
DI = 4096
CONV = 4352

EPSILON = 1e-05
BETA_ONE = 0.9
BETA_TWO = 0.95
ADAM_EPS = 1e-08
LEARN_RATE = 0.01
DECAY_RATE = 0.1
adam_step = 10
highest = lax.Precision.HIGHEST

Q = 128
BC = 512
HB = BC // HP
PAIRS = BC // 128
F32 = jnp.float32
BF16 = jnp.bfloat16


def dot(a, b):
    return jnp.dot(a, b, preferred_element_type=F32)


def dot_nt(a, b):
    return lax.dot_general(a, b, (((1,), (1,)), ((), ())), preferred_element_type=F32)


def sigmoid(v):
    return 1.0 / (1.0 + jnp.exp(-v))


def segment_of(starts_ref, position):
    row = pl.program_id(0)
    count = jnp.zeros_like(position)
    for k in range(starts_ref.shape[1]):
        count = count + (starts_ref[row, k] <= position).astype(jnp.int32)
    return count


def conv_forward(values, weights, bias, same_ref):
    total = values * weights[CONVW - 1 : CONVW] + bias
    for lag in range(1, CONVW):
        moved = pltpu.roll(values, lag, 0) * same_ref[lag - 1]
        total = total + moved * weights[CONVW - 1 - lag : CONVW - lag]
    return total


def conv_backward(d_conv, values, weights, same_ref):
    length = values.shape[0]
    d_in = d_conv * weights[CONVW - 1 : CONVW]
    sums = [jnp.sum(d_conv * values, axis=0, keepdims=True)]
    for lag in range(1, CONVW):
        masked = d_conv * same_ref[lag - 1]
        sums.append(jnp.sum(masked * pltpu.roll(values, lag, 0), axis=0, keepdims=True))
        d_in = d_in + pltpu.roll(masked, length - lag, 0) * weights[CONVW - 1 - lag : CONVW - lag]
    return d_in, jnp.concatenate(sums[::-1], axis=0), jnp.sum(d_conv, axis=0, keepdims=True)


def prepare_masks(starts_ref, length, same_ref, enter_ref, last_ref):
    col = lax.broadcasted_iota(jnp.int32, (length, 128), 0)
    seg = segment_of(starts_ref, col)
    for lag in range(1, CONVW):
        same_ref[lag - 1] = (segment_of(starts_ref, col - lag) == seg).astype(F32)
    begin = col - lax.rem(col, Q)
    enter_ref[...] = ((segment_of(starts_ref, begin - 1) == seg) & (begin > 0)).astype(F32)
    last_ref[...] = (segment_of(starts_ref, begin + (Q - 1)) == seg).astype(F32)


def keep_mask(starts_ref, chunk):
    rows = lax.broadcasted_iota(jnp.int32, (Q, Q), 0) + chunk * Q
    cols = lax.broadcasted_iota(jnp.int32, (Q, Q), 1) + chunk * Q
    return (rows >= cols) & (segment_of(starts_ref, rows) == segment_of(starts_ref, cols))


def step_rows(dt_ref, shift_ref, logd_ref):
    pre = dt_ref[...] + shift_ref[...]
    step = jnp.maximum(pre, 0.0) + jnp.log1p(jnp.exp(-jnp.abs(pre)))
    decay = jnp.exp(logd_ref[...])
    return pre, step, -step * decay, decay


def cumulate(rate, chunks):
    rows = lax.broadcasted_iota(jnp.int32, (Q, Q), 0)
    cols = lax.broadcasted_iota(jnp.int32, (Q, Q), 1)
    upper = (rows <= cols).astype(F32)
    parts = [
        jnp.dot(rate[:, c * Q : (c + 1) * Q], upper, precision=highest, preferred_element_type=F32)
        for c in range(chunks)
    ]
    return jnp.concatenate(parts, axis=1)


def halves(lo, pair):
    zero = jnp.zeros_like(pair)
    return jnp.concatenate([jnp.where(lo, pair, zero), jnp.where(lo, zero, pair)], axis=0)


def forward_kernel(
    starts_ref, gate_ref, xin_ref, bc_ref, dt_ref, cw_ref, cb_ref, cwbc_ref, cbbc_ref,
    shift_ref, logd_ref, skip_ref,
    gated_ref, y_ref, state_ref, total_ref,
    same_ref, enter_ref, last_ref, cmat_ref, bt_ref, score_ref, square_ref,
    x_ref, carry_ref, step_ref, cum_ref, cumt_ref, tailed_ref, decay_ref,
):
    j = pl.program_id(1)
    length = gate_ref.shape[0]
    chunks = length // Q
    lo = lax.broadcasted_iota(jnp.int32, (Q, 128), 1) < HP

    @pl.when(j == 0)
    def _():
        prepare_masks(starts_ref, length, same_ref, enter_ref, last_ref)
        square_ref[...] = jnp.zeros_like(square_ref)
        both = []
        for part in range(2):
            cols = slice(part * NS, (part + 1) * NS)
            conv = conv_forward(bc_ref[:, cols].astype(F32), cwbc_ref[:, cols], cbbc_ref[:, cols], same_ref)
            both.append(conv * sigmoid(conv))
        bmat, cmat = both
        cmat_ref[...] = cmat.astype(BF16)
        bt = bmat.T
        bt_ref[...] = bt.astype(BF16)
        for c in range(chunks):
            rows = slice(c * Q, (c + 1) * Q)
            score = jnp.dot(cmat[rows].astype(BF16), bt[:, rows].astype(BF16), preferred_element_type=F32)
            score_ref[c] = jnp.where(keep_mask(starts_ref, c), score, 0.0)

    _, step, rate, _ = step_rows(dt_ref, shift_ref, logd_ref)
    cum = cumulate(rate, chunks)
    cumt_ref[...] = cum
    cum_ref[...] = cum.T
    step_ref[...] = step.T
    carry_ref[...] = jnp.zeros_like(carry_ref)
    for p in range(PAIRS):
        cols = slice(p * 128, (p + 1) * 128)
        conv = conv_forward(xin_ref[:, cols].astype(F32), cw_ref[:, cols], cb_ref[:, cols], same_ref)
        x_ref[:, cols] = conv * sigmoid(conv)
    for c in range(chunks):
        rows = slice(c * Q, (c + 1) * Q)
        entering_state = carry_ref[...].astype(BF16)
        state_ref[0, c] = entering_state
        if c > 0:
            outside = dot(cmat_ref[rows, :], entering_state)
        score = score_ref[c]
        for p in range(PAIRS):
            cols = slice(p * 128, (p + 1) * 128)
            cum_a = jnp.broadcast_to(cum_ref[rows, 2 * p : 2 * p + 1], (Q, Q))
            cum_b = jnp.broadcast_to(cum_ref[rows, 2 * p + 1 : 2 * p + 2], (Q, Q))
            low_a = (score * jnp.exp(jnp.minimum(cum_a - cumt_ref[2 * p : 2 * p + 1, rows], 0.0))).astype(BF16)
            low_b = (score * jnp.exp(jnp.minimum(cum_b - cumt_ref[2 * p + 1 : 2 * p + 2, rows], 0.0))).astype(BF16)
            cum_x = jnp.where(lo, cum_a, cum_b)
            step_x = jnp.where(lo, step_ref[rows, 2 * p : 2 * p + 1], step_ref[rows, 2 * p + 1 : 2 * p + 2])
            x = x_ref[rows, cols]
            xs = (x * step_x).astype(BF16)
            y = dot(jnp.concatenate([low_a, low_b], axis=1), halves(lo, xs))
            reach = jnp.exp(cum_x) * enter_ref[rows]
            if c > 0:
                y = y + reach * outside[:, cols]
            if c < chunks - 1:
                tail = jnp.exp(cum_x[Q - 1 : Q] - cum_x) * last_ref[rows]
                tailed_ref[:, cols] = (xs.astype(F32) * tail).astype(BF16)
                decay_ref[0:1, cols] = reach[Q - 1 : Q]
            y_ref[rows, cols] = y
            gate = gate_ref[rows, cols].astype(F32)
            gated = (y + skip_ref[:, cols] * x) * (gate * sigmoid(gate))
            square_ref[rows, :] += gated * gated
            gated_ref[rows, cols] = gated
        if c < chunks - 1:
            carry_ref[...] = decay_ref[0:1, :] * carry_ref[...] + dot(bt_ref[:, rows], tailed_ref[...])

    @pl.when(j == pl.num_programs(1) - 1)
    def _():
        total_ref[...] = jnp.sum(square_ref[...], axis=1, keepdims=True)


def backward_body(
    starts_ref, gate_ref, xin_ref, bc_ref, dt_ref, cw_ref, cb_ref, cwbc_ref, cbbc_ref,
    shift_ref, logd_ref, skip_ref, gain_ref, y_ref, state_ref, q_ref, mean_ref, dm_ref,
    before_ref, dgate_ref, dbc_ref, ddt_ref, sgain_ref, scw_ref, scb_ref, scwbc_ref, scbbc_ref,
    sshift_ref, slogd_ref, sskip_ref,
    same_ref, enter_ref, last_ref, bmat_ref, cmat_ref, ct_ref, score_ref, scoret_ref,
    x_ref, slope_ref, dy_ref, dxs_ref, carry_ref, step_ref, cum_ref, cumt_ref,
    dscore_ref, db_ref, dc_ref, v1_ref, v2_ref, v3_ref, v4_ref, tailed_ref, reached_ref, decay_ref, held_ref,
):
    j = pl.program_id(2)
    length = gate_ref.shape[0]
    chunks = length // Q
    lo = lax.broadcasted_iota(jnp.int32, (Q, 128), 1) < HP

    def activate_bc(part):
        cols = slice(part * NS, (part + 1) * NS)
        return conv_forward(bc_ref[:, cols].astype(F32), cwbc_ref[:, cols], cbbc_ref[:, cols], same_ref)

    @pl.when(j == 0)
    def _():
        prepare_masks(starts_ref, length, same_ref, enter_ref, last_ref)
        both = []
        for part in range(2):
            conv = activate_bc(part)
            both.append(conv * sigmoid(conv))
        bmat, cmat = both
        bmat_ref[...] = bmat.astype(BF16)
        cmat_ref[...] = cmat.astype(BF16)
        bt = bmat.T
        ct_ref[...] = cmat.T.astype(BF16)
        for c in range(chunks):
            rows = slice(c * Q, (c + 1) * Q)
            score = jnp.dot(cmat[rows].astype(BF16), bt[:, rows].astype(BF16), preferred_element_type=F32)
            score = jnp.where(keep_mask(starts_ref, c), score, 0.0)
            score_ref[c] = score
            scoret_ref[c] = score.T
        dscore_ref[...] = jnp.zeros_like(dscore_ref)
        db_ref[...] = jnp.zeros_like(db_ref)
        dc_ref[...] = jnp.zeros_like(dc_ref)

    pre, step, rate, decay = step_rows(dt_ref, shift_ref, logd_ref)
    cum = cumulate(rate, chunks)
    cumt_ref[...] = cum
    cum_ref[...] = cum.T
    step_ref[...] = step.T
    carry_ref[...] = jnp.zeros_like(carry_ref)
    q = q_ref[...]
    mean = mean_ref[...]
    for p in range(PAIRS):
        cols = slice(p * 128, (p + 1) * 128)
        conv = conv_forward(xin_ref[:, cols].astype(F32), cw_ref[:, cols], cb_ref[:, cols], same_ref)
        sig = sigmoid(conv)
        x = conv * sig
        x_ref[:, cols] = x
        slope_ref[:, cols] = sig * (1.0 + conv - x)
        gate = gate_ref[:, cols].astype(F32)
        gsig = sigmoid(gate)
        silu = gate * gsig
        scanned = y_ref[:, cols] + skip_ref[:, cols] * x
        gated = scanned * silu
        scaled = dm_ref[:, cols].astype(F32) * q
        sgain_ref[0, :, cols] = jnp.sum(gated * scaled, axis=0, keepdims=True)
        d_gated = scaled * gain_ref[:, cols] - gated * mean
        dgate_ref[:, cols] = (d_gated * scanned * (gsig * (1.0 + gate - silu))).astype(dgate_ref.dtype)
        d_scanned = d_gated * silu
        dy_ref[:, cols] = d_scanned
        sskip_ref[0, :, cols] = jnp.sum(d_scanned * x, axis=0, keepdims=True)

    for c in reversed(range(chunks)):
        rows = slice(c * Q, (c + 1) * Q)
        score = score_ref[c]
        scoret = scoret_ref[c]
        d_state = carry_ref[...]
        d_state_low = d_state.astype(BF16)
        if c < chunks - 1:
            from_state = dot(bmat_ref[rows, :], d_state_low)
        d_score = dscore_ref[c]
        for p in range(PAIRS):
            cols = slice(p * 128, (p + 1) * 128)
            cum_a = jnp.broadcast_to(cum_ref[rows, 2 * p : 2 * p + 1], (Q, Q))
            cum_b = jnp.broadcast_to(cum_ref[rows, 2 * p + 1 : 2 * p + 2], (Q, Q))
            row_a = cumt_ref[2 * p : 2 * p + 1, rows]
            row_b = cumt_ref[2 * p + 1 : 2 * p + 2, rows]
            cum_x = jnp.where(lo, cum_a, cum_b)
            step_x = jnp.where(lo, step_ref[rows, 2 * p : 2 * p + 1], step_ref[rows, 2 * p + 1 : 2 * p + 2])
            x = x_ref[rows, cols]
            xs = (x * step_x).astype(BF16)
            xs_wide = xs.astype(F32)
            d_y = dy_ref[rows, cols]
            d_y_low = d_y.astype(BF16)
            pair = dot_nt(d_y_low, halves(lo, xs))
            d_score = d_score + pair[:, :Q] * jnp.exp(jnp.minimum(cum_a - row_a, 0.0))
            d_score = d_score + pair[:, Q:] * jnp.exp(jnp.minimum(cum_b - row_b, 0.0))
            up_a = (scoret * jnp.exp(jnp.minimum(row_a - cum_a, 0.0))).astype(BF16)
            up_b = (scoret * jnp.exp(jnp.minimum(row_b - cum_b, 0.0))).astype(BF16)
            d_xs = dot(jnp.concatenate([up_a, up_b], axis=1), halves(lo, d_y_low))
            v1_ref[rows, cols] = d_y_low.astype(F32) * y_ref[rows, cols] - xs_wide * d_xs
            reach = jnp.exp(cum_x) * enter_ref[rows]
            if c < chunks - 1:
                tail = jnp.exp(cum_x[Q - 1 : Q] - cum_x) * last_ref[rows]
                d_tail = tail * from_state[:, cols]
                v3_ref[rows, cols] = xs_wide * d_tail
                d_xs = d_xs + d_tail
                tailed_ref[:, cols] = (xs_wide * tail).astype(BF16)
                entered = state_ref[0, c, :, cols]
                v4_ref[c : c + 1, cols] = reach[Q - 1 : Q] * jnp.sum(
                    d_state[:, cols] * entered.astype(F32), axis=0, keepdims=True
                )
            else:
                v3_ref[rows, cols] = jnp.zeros((Q, 128), F32)
                v4_ref[c : c + 1, cols] = jnp.zeros((1, 128), F32)
            if c > 0:
                reached_ref[:, cols] = (reach * d_y).astype(BF16)
                decay_ref[0:1, cols] = reach[Q - 1 : Q]
            v2_ref[rows, cols] = x * d_xs
            dxs_ref[rows, cols] = step_x * d_xs + skip_ref[:, cols] * d_y
        dscore_ref[c] = d_score
        if c < chunks - 1:
            db_ref[rows, :] += dot_nt(tailed_ref[...], d_state_low)
        if c > 0:
            reached = reached_ref[...]
            dc_ref[rows, :] += dot_nt(reached, state_ref[0, c])
            carry_ref[...] = decay_ref[0:1, :] * d_state + dot(ct_ref[:, rows], reached)

    head = lax.broadcasted_iota(jnp.int32, (HB, BC), 0)
    lane = lax.broadcasted_iota(jnp.int32, (HB, BC), 1)
    pick = ((lane >= head * HP) & (lane < (head + 1) * HP)).astype(BF16)

    def by_head(values):
        high = values.astype(BF16)
        rest = (values - high.astype(F32)).astype(BF16)
        return dot_nt(pick, high) + dot_nt(pick, rest)

    h1 = by_head(v1_ref[...])
    h2 = by_head(v2_ref[...])
    h3 = by_head(v3_ref[...])
    h4 = by_head(v4_ref[...])
    rows_i = lax.broadcasted_iota(jnp.int32, (Q, Q), 0)
    cols_i = lax.broadcasted_iota(jnp.int32, (Q, Q), 1)
    suffix = (rows_i >= cols_i).astype(F32)
    prefix = (rows_i < cols_i).astype(F32)
    parts = []
    for c in range(chunks):
        rows = slice(c * Q, (c + 1) * Q)
        parts.append(
            jnp.dot(h1[:, rows], suffix, precision=highest, preferred_element_type=F32)
            + jnp.dot(h3[:, rows], prefix, precision=highest, preferred_element_type=F32)
            + h4[:, c : c + 1]
        )
    d_rate = jnp.concatenate(parts, axis=1)
    d_step = h2 - d_rate * decay
    d_raw = d_step * sigmoid(pre)
    ddt_ref[...] = d_raw
    sshift_ref[0] = jnp.sum(d_raw, axis=1, keepdims=True)
    slogd_ref[0] = jnp.sum(d_rate * rate, axis=1, keepdims=True)

    for p in range(PAIRS):
        cols = slice(p * 128, (p + 1) * 128)
        d_conv = dxs_ref[:, cols] * slope_ref[:, cols]
        d_in, s_w, s_b = conv_backward(d_conv, xin_ref[:, cols].astype(F32), cw_ref[:, cols], same_ref)
        held_ref[j, :, cols] = d_in.astype(BF16)
        scw_ref[0, :, cols] = s_w
        scb_ref[0, :, cols] = s_b

    @pl.when(j == pl.num_programs(2) - 1)
    def _():
        for c in range(chunks):
            rows = slice(c * Q, (c + 1) * Q)
            masked = jnp.where(keep_mask(starts_ref, c), dscore_ref[c], 0.0)
            dc_ref[rows, :] += dot(masked.astype(BF16), bmat_ref[rows, :])
            db_ref[rows, :] += dot(masked.T.astype(BF16), cmat_ref[rows, :])
        for part, grad_ref in ((0, db_ref), (1, dc_ref)):
            cols = slice(part * NS, (part + 1) * NS)
            conv = activate_bc(part)
            sig = sigmoid(conv)
            d_conv = grad_ref[...] * (sig * (1.0 + conv - conv * sig))
            d_in, s_w, s_b = conv_backward(d_conv, bc_ref[:, cols].astype(F32), cwbc_ref[:, cols], same_ref)
            dbc_ref[:, cols] = d_in.astype(dbc_ref.dtype)
            scwbc_ref[0, :, cols] = s_w
            scbbc_ref[0, :, cols] = s_b


def backward_kernel(*refs):
    outputs_at = 18

    @pl.when(pl.program_id(1) == 0)
    def _():
        backward_body(*refs)

    @pl.when(pl.program_id(1) == 1)
    def _():
        refs[outputs_at + 1][...] = refs[-1][pl.program_id(2)]


def backward_first(*refs):
    backward_kernel(*refs[:18], None, *refs[18:])


def forward_index(first, rows):
    return lambda r, j: (first + r, r, j)


def backward_index(first, rows):
    def index(r, s, j):
        r = jnp.minimum(r + s, rows - 1)
        return first + r, r, j * (1 - s)

    return index


def common_specs(index, length, channels):
    def at(shape, where):
        return pl.BlockSpec(shape, lambda *g: where(*index(*g)))

    blocks = channels // BC
    heads = at((HB, 1), lambda a, r, j: (j, 0))
    return at, [
        pl.BlockSpec(memory_space=pltpu.SMEM),
        at((length, BC), lambda a, r, j: (a, j)),
        at((length, BC), lambda a, r, j: (a, j + blocks)),
        at((length, 2 * NS), lambda a, r, j: (a, 0)),
        at((HB, length), lambda a, r, j: (j, a)),
        at((CONVW, BC), lambda a, r, j: (0, j)),
        at((1, BC), lambda a, r, j: (0, j)),
        at((CONVW, 2 * NS), lambda a, r, j: (0, 0)),
        at((1, 2 * NS), lambda a, r, j: (0, 0)),
        heads,
        heads,
        at((1, BC), lambda a, r, j: (0, j)),
    ]


def row_cost(size, weight):
    return pl.CostEstimate(flops=1000 * weight * size, bytes_accessed=12 * size, transcendentals=0)


def mix_forward(first, length, starts, main, extra, dt_rows, conv_w, conv_b, cw_bc, cb_bc, shift, logd, skip_cols):
    rows = starts.shape[0]
    channels = main.shape[1] // 2
    chunks = length // Q
    vmem = pltpu.VMEM
    _, in_specs = common_specs(forward_index(first, rows), length, channels)
    return pl.pallas_call(
        forward_kernel,
        grid=(rows, channels // BC),
        in_specs=in_specs,
        out_specs=[
            pl.BlockSpec((length, BC), lambda r, j: (r, j)),
            pl.BlockSpec((length, BC), lambda r, j: (r, j)),
            pl.BlockSpec((1, chunks, NS, BC), lambda r, j: (r, 0, 0, j)),
            pl.BlockSpec((length, 1), lambda r, j: (r, 0)),
        ],
        out_shape=[
            jax.ShapeDtypeStruct((rows * length, channels), F32),
            jax.ShapeDtypeStruct((rows * length, channels), F32),
            jax.ShapeDtypeStruct((rows, chunks, NS, channels), BF16),
            jax.ShapeDtypeStruct((rows * length, 1), F32),
        ],
        scratch_shapes=[
            vmem((CONVW - 1, length, 128), F32),
            vmem((length, 128), F32),
            vmem((length, 128), F32),
            vmem((length, NS), BF16),
            vmem((NS, length), BF16),
            vmem((chunks, Q, Q), F32),
            vmem((length, 128), F32),
            vmem((length, BC), F32),
            vmem((NS, BC), F32),
            vmem((length, HB), F32),
            vmem((length, HB), F32),
            vmem((HB, length), F32),
            vmem((Q, BC), BF16),
            vmem((8, BC), F32),
        ],
        compiler_params=pltpu.CompilerParams(vmem_limit_bytes=48 * 1024 * 1024),
        cost_estimate=row_cost(rows * length * channels, 18),
        name="mix_forward",
    )(starts, main, main, extra, dt_rows, conv_w, conv_b, cw_bc, cb_bc, shift, logd, skip_cols)


def mix_backward(
    first, total, length, before, starts, main, extra, dt_rows, conv_w, conv_b, cw_bc, cb_bc, shift, logd, skip_cols,
    gain, y, states, q, mean, d_mixed,
):
    rows = starts.shape[0]
    channels = main.shape[1] // 2
    heads = channels // HP
    blocks = channels // BC
    chunks = length // Q
    vmem = pltpu.VMEM
    at, in_specs = common_specs(backward_index(first, rows), length, channels)
    col = at((length, 1), lambda a, r, j: (a, 0))

    def result(shape, where):
        return pl.BlockSpec(shape, lambda r, s, j: where(r, jnp.maximum(j, s * (blocks - 1))))

    def row_sums(count):
        return result((1, count, BC), lambda r, j: (r, 0, j))

    per_head = result((1, HB, 1), lambda r, j: (r, j, 0))
    shape = jax.ShapeDtypeStruct
    operands = (
        starts, main, main, extra, dt_rows, conv_w, conv_b, cw_bc, cb_bc, shift, logd, skip_cols,
        gain, y, states, q, mean, d_mixed,
    )
    in_specs = in_specs + [
        at((1, BC), lambda a, r, j: (0, j)),
        at((length, BC), lambda a, r, j: (r, j)),
        at((1, chunks, NS, BC), lambda a, r, j: (r, 0, 0, j)),
        col,
        col,
        at((length, BC), lambda a, r, j: (a, j)),
    ]
    aliases = {}
    if before is not None:
        aliases = {len(operands): 0}
        operands = operands + (before,)
        in_specs = in_specs + [pl.BlockSpec(memory_space=pl.ANY)]
    return pl.pallas_call(
        backward_first if before is None else backward_kernel,
        grid=(rows, 2, blocks),
        in_specs=in_specs,
        out_specs=[
            pl.BlockSpec((length, BC), lambda r, s, j: (first + r, j + blocks * s)),
            result((length, 2 * NS), lambda r, j: (r, 0)),
            result((HB, length), lambda r, j: (j, r)),
            row_sums(1),
            row_sums(CONVW),
            row_sums(1),
            result((1, CONVW, 2 * NS), lambda r, j: (r, 0, 0)),
            result((1, 1, 2 * NS), lambda r, j: (r, 0, 0)),
            per_head,
            per_head,
            row_sums(1),
        ],
        out_shape=[
            shape((total * length, 2 * channels), BF16),
            shape((rows * length, 2 * NS), BF16),
            shape((heads, rows * length), F32),
            shape((rows, 1, channels), F32),
            shape((rows, CONVW, channels), F32),
            shape((rows, 1, channels), F32),
            shape((rows, CONVW, 2 * NS), F32),
            shape((rows, 1, 2 * NS), F32),
            shape((rows, heads, 1), F32),
            shape((rows, heads, 1), F32),
            shape((rows, 1, channels), F32),
        ],
        scratch_shapes=[
            vmem((CONVW - 1, length, 128), F32),
            vmem((length, 128), F32),
            vmem((length, 128), F32),
            vmem((length, NS), BF16),
            vmem((length, NS), BF16),
            vmem((NS, length), BF16),
            vmem((chunks, Q, Q), F32),
            vmem((chunks, Q, Q), F32),
            vmem((length, BC), F32),
            vmem((length, BC), F32),
            vmem((length, BC), F32),
            vmem((length, BC), F32),
            vmem((NS, BC), F32),
            vmem((length, HB), F32),
            vmem((length, HB), F32),
            vmem((HB, length), F32),
            vmem((chunks, Q, Q), F32),
            vmem((length, NS), F32),
            vmem((length, NS), F32),
            vmem((length, BC), F32),
            vmem((length, BC), F32),
            vmem((length, BC), F32),
            vmem((8, BC), F32),
            vmem((Q, BC), BF16),
            vmem((Q, BC), BF16),
            vmem((8, BC), F32),
            vmem((blocks, length, BC), BF16),
        ],
        input_output_aliases=aliases,
        compiler_params=pltpu.CompilerParams(vmem_limit_bytes=48 * 1024 * 1024),
        cost_estimate=row_cost(rows * length * channels, 42),
        name="mix_backward",
    )(*operands)


MAIN = 2 * DI
EXTRA = 2 * NS + NH


def adam_direction(weight, gradient, first, second, decayed):
    first_new = BETA_ONE * first + (1.0 - BETA_ONE) * gradient
    second_new = BETA_TWO * second + (1.0 - BETA_TWO) * gradient * gradient
    first_hat = first_new / (1.0 - BETA_ONE**adam_step)
    second_hat = second_new / (1.0 - BETA_TWO**adam_step)
    direction = first_hat / (jnp.sqrt(second_hat) + ADAM_EPS)
    if decayed:
        direction = direction + DECAY_RATE * weight
    return (direction, first_new, second_new)


def swap(value, axis, mask):
    size = lax.axis_size(axis)
    return lax.ppermute(value, axis, [(i, i ^ mask) for i in range(size)])


def bits_of(size):
    return [1 << b for b in reversed(range(size.bit_length() - 1))]


def place(buffer, shape, block, at, items):
    arrays, copies, table = [], [], [at[0], at[1]]
    for array, lead, row, col, valid, cuts in items:
        if not any(array is a for a in arrays):
            arrays.append(array)
        source = [array is a for a in arrays].index(True)
        for start, end in zip(cuts[:-1], cuts[1:]):
            copies.append((source, lead, start, end - start))
            table.extend([row, col, valid])
    table = jnp.stack([jnp.asarray(v, jnp.int32) for v in table])
    operands = [table] + arrays + ([] if buffer is None else [buffer])

    def kernel(table_ref, *refs):
        out_ref = refs[-1]
        for i, (source, lead, start, size) in enumerate(copies):
            piece = refs[source]
            row = pl.multiple_of(table_ref[3 * i + 2] + start, 16)
            col = pl.multiple_of(table_ref[3 * i + 3], 128)

            @pl.when(table_ref[3 * i + 4] > start)
            def _():
                rows = pl.ds(start, size)
                value = piece[rows, :] if lead is None else piece[lead, rows, :]
                out_ref[pl.ds(row, size), pl.ds(col, value.shape[1])] = value

    def all_of(a):
        return pl.BlockSpec(a.shape, lambda i, t: (0,) * a.ndim)

    return pl.pallas_call(
        kernel,
        grid_spec=pltpu.PrefetchScalarGridSpec(
            num_scalar_prefetch=1,
            grid=(1,),
            in_specs=[all_of(a) for a in arrays] + ([] if buffer is None else [pl.BlockSpec(memory_space=pl.ANY)]),
            out_specs=pl.BlockSpec(block, lambda i, t: (t[0], t[1])),
        ),
        out_shape=jax.ShapeDtypeStruct(shape, BF16),
        input_output_aliases={} if buffer is None else {len(operands) - 1: 0},
        compiler_params=pltpu.CompilerParams(vmem_limit_bytes=60 * 1024 * 1024),
        name="place",
    )(*operands)


def place_blocks(buffer, shape, arrays, size, order, columns, first_rows, counts, cuts):
    width, steps = arrays[0].shape[2], len(columns)
    pieces = [(a, n) for a, array in enumerate(arrays) for n in range(array.shape[0])]
    table = [jnp.asarray(v, jnp.int32) for v in columns]
    for rel in order:
        table.extend([first_rows(rel), counts(rel)])
    operands = [jnp.stack(table)] + list(arrays) + ([] if buffer is None else [buffer])

    def kernel(table_ref, *refs):
        for i, (a, n) in enumerate(pieces):
            begin = pl.multiple_of(table_ref[steps + 2 * i], 16)
            for start, end in zip(cuts[:-1], cuts[1:]):

                @pl.when(table_ref[steps + 2 * i + 1] > start)
                def _():
                    refs[-1][pl.ds(pl.multiple_of(begin + start, 16), end - start), :] = refs[a][n, start:end, :]

    return pl.pallas_call(
        kernel,
        grid_spec=pltpu.PrefetchScalarGridSpec(
            num_scalar_prefetch=1,
            grid=(steps,),
            in_specs=[pl.BlockSpec((a.shape[0], size, width), lambda i, t: (0, i, 0)) for a in arrays]
            + ([] if buffer is None else [pl.BlockSpec(memory_space=pl.ANY)]),
            out_specs=pl.BlockSpec((shape[0], width), lambda i, t: (0, t[i])),
        ),
        out_shape=jax.ShapeDtypeStruct(shape, BF16),
        input_output_aliases={} if buffer is None else {len(operands) - 1: 0},
        compiler_params=pltpu.CompilerParams(vmem_limit_bytes=60 * 1024 * 1024),
        name="place_blocks",
    )(*operands)


def matmul(a, b, kind, out_dtype=BF16, scale=None):
    m = a.shape[1] if kind == "tn" else a.shape[0]
    k = a.shape[0] if kind == "tn" else a.shape[1]
    n = b.shape[0] if kind == "nt" else b.shape[1]
    tm, tn = min(m, 1024), min(n, 512)
    dims = {"nn": ((1,), (0,)), "nt": ((1,), (1,)), "tn": ((0,), (0,))}[kind]

    def kernel(*refs):
        first = refs[0][...]
        if scale is not None:
            first = first * refs[2][...]
        total = lax.dot_general(first, refs[1][...], (dims, ((), ())), preferred_element_type=F32)
        refs[-1][...] = total.astype(out_dtype)

    in_specs = [
        pl.BlockSpec((k, tm), lambda i, j: (0, i)) if kind == "tn" else pl.BlockSpec((tm, k), lambda i, j: (i, 0)),
        pl.BlockSpec((tn, k), lambda i, j: (j, 0)) if kind == "nt" else pl.BlockSpec((k, tn), lambda i, j: (0, j)),
    ]
    operands = [a, b]
    if scale is not None:
        in_specs.append(pl.BlockSpec((k, 1), lambda i, j: (0, 0)))
        operands.append(scale)
    return pl.pallas_call(
        kernel,
        grid=(m // tm, n // tn),
        in_specs=in_specs,
        out_specs=pl.BlockSpec((tm, tn), lambda i, j: (i, j)),
        out_shape=jax.ShapeDtypeStruct((m, n), out_dtype),
        compiler_params=pltpu.CompilerParams(vmem_limit_bytes=56 * 1024 * 1024),
        cost_estimate=pl.CostEstimate(flops=2 * m * n * k, bytes_accessed=2 * (m * k + n * k + m * n), transcendentals=0),
        name="matmul_" + kind,
    )(*operands)


def mixed_gradient(upstream, weights, live, mixed):
    rows, width = upstream.shape
    local = weights.shape[0]
    tm, tn = min(rows, 1024), min(local, 512)

    def kernel(up_ref, w_ref, live_ref, mixed_ref, out_ref, inner_ref):
        total = (dot_nt(up_ref[...], w_ref[...]) * live_ref[...]).astype(BF16)
        out_ref[...] = total
        part = jnp.sum(total.astype(F32) * mixed_ref[...].astype(F32), axis=1, keepdims=True)

        @pl.when(pl.program_id(1) == 0)
        def _():
            inner_ref[...] = part

        @pl.when(pl.program_id(1) > 0)
        def _():
            inner_ref[...] += part

    return pl.pallas_call(
        kernel,
        grid=(rows // tm, local // tn),
        in_specs=[
            pl.BlockSpec((tm, width), lambda i, j: (i, 0)),
            pl.BlockSpec((tn, width), lambda i, j: (j, 0)),
            pl.BlockSpec((tm, 1), lambda i, j: (i, 0)),
            pl.BlockSpec((tm, tn), lambda i, j: (i, j)),
        ],
        out_specs=[pl.BlockSpec((tm, tn), lambda i, j: (i, j)), pl.BlockSpec((tm, 1), lambda i, j: (i, 0))],
        out_shape=[jax.ShapeDtypeStruct((rows, local), BF16), jax.ShapeDtypeStruct((rows, 1), F32)],
        compiler_params=pltpu.CompilerParams(vmem_limit_bytes=56 * 1024 * 1024),
        name="mixed_gradient",
    )(upstream, weights, live, mixed)


def rows_into(buffer, row, rows, length, pieces, gain=None):
    tile = 128
    counts = [p.shape[0] // tile for p in pieces]
    starts = [sum(counts[:i]) for i in range(len(counts) + 1)]
    width = pieces[0].shape[1]
    operands = list(pieces) + ([] if gain is None else [gain]) + ([] if buffer is None else [buffer])

    def kernel(*refs):
        step = pl.program_id(0)
        for i in range(len(pieces)):

            @pl.when((step >= starts[i]) & (step < starts[i + 1]))
            def _():
                value = refs[i][...]
                if gain is not None:
                    value = value.astype(F32)
                    mean = jnp.mean(value * value, axis=1, keepdims=True)
                    value = (value * lax.rsqrt(mean + EPSILON) * refs[len(pieces)][...]).astype(BF16)
                refs[-1][...] = value

    def piece_spec(i):
        return pl.BlockSpec((tile, width), lambda s: (jnp.clip(s - starts[i], 0, counts[i] - 1), 0))

    specs = [piece_spec(i) for i in range(len(pieces))]
    if gain is not None:
        specs.append(pl.BlockSpec(gain.shape, lambda s: (0, 0)))
    if buffer is not None:
        specs.append(pl.BlockSpec(memory_space=pl.ANY))
    return pl.pallas_call(
        kernel,
        grid=(starts[-1],),
        in_specs=specs,
        out_specs=pl.BlockSpec((tile, width), lambda s: (row * length // tile + s, 0)),
        out_shape=jax.ShapeDtypeStruct((rows * length, width), BF16),
        input_output_aliases={} if buffer is None else {len(operands) - 1: 0},
        compiler_params=pltpu.CompilerParams(vmem_limit_bytes=60 * 1024 * 1024),
        name="rows_into",
    )(*operands)


def prefix_count(g, n, unit, period):
    return (n // period) * unit + jnp.clip(n % period - g * unit, 0, unit)


def static_count(g, n, unit, period):
    return (n // period) * unit + min(max(n % period - g * unit, 0), unit)


def then(value, *earlier):
    return lax.optimization_barrier((value,) + earlier)[0]


def spread_z(bundle, masks, late=()):
    have, order = bundle[None], [0]
    for i, mask in enumerate(masks):
        if i > 0:
            have = then(have, *late)
        have = jnp.concatenate([have, swap(have, "dp", 2 * mask)])
        order = order + [rel ^ mask for rel in order]
    return have, order


def grouped(tokens, cotangent, doc_starts, valid_len, weights, firsts, seconds):
    w_in, w_out, norm_gain, gate_gain, conv_w, conv_b, dt_bias, a_log, d_skip = weights
    small = weights[2:]
    dp, groups = lax.axis_size("dp"), lax.axis_size("fsdp")
    zs = dp // 2
    d, f = lax.axis_index("dp"), lax.axis_index("fsdp")
    z, c = d // 2, d % 2
    z_masks = bits_of(zs)
    length, width = tokens.shape[1], tokens.shape[2]
    local = DI // groups
    unit = local // groups
    k_rows, per_dev = w_in.shape
    k_half = k_rows // 2
    per_chip = 2 * per_dev
    out_cols = w_out.shape[1]
    sizes = {
        (zz, g): static_count(g, min(per_chip * (zz + 1), MAIN), unit, local)
        - static_count(g, min(per_chip * zz, MAIN), unit, local)
        for zz in range(zs)
        for g in range(groups)
    }
    cuts = [0] + sorted(set(sizes.values()) - {0})
    most = cuts[-1]

    def first_row(zz):
        return prefix_count(f, jnp.minimum(per_chip * zz, MAIN), unit, local)

    def rows_valid(zz):
        return first_row(zz + 1) - first_row(zz)

    def slice_row(row):
        return jnp.minimum(row, 2 * local - most)

    low = w_in.astype(BF16)
    mine = lax.dynamic_slice_in_dim(low, k_half * c, k_half, 0)
    other = swap(lax.dynamic_slice_in_dim(low, k_half * (1 - c), k_half, 0), "dp", 1)
    chip = jnp.concatenate([jnp.where(c == 0, mine, other), jnp.where(c == 0, other, mine)], axis=1)
    column = per_chip * z + jnp.arange(per_chip, dtype=jnp.int32)
    owner = (column // unit) % groups
    begin = prefix_count(owner, per_chip * z, unit, local)
    rank = prefix_count(owner, column, unit, local) - begin
    moved = begin - slice_row(begin)
    extra_key = groups * most + column - MAIN
    places = jnp.arange(groups * most + EXTRA, dtype=jnp.int32)[:, None]

    def picks(ranks):
        key = jnp.where(column < MAIN, (owner ^ f) * most + ranks, extra_key)
        return (places == key[None, :]).astype(BF16)

    parts = dot_nt(picks(rank), chip).astype(BF16)

    def own_channels(v):
        v = v.reshape(v.shape[0], groups, groups, -1)
        return lax.dynamic_index_in_dim(v, f, 2, keepdims=False).reshape(v.shape[0], -1)

    out_low = w_out.astype(BF16).reshape(groups, unit, out_cols)
    out_blocks = [lax.dynamic_index_in_dim(out_low, f ^ m, 0, keepdims=False) for m in range(groups)]
    blocks = [parts[m * most : (m + 1) * most] for m in range(groups)]
    pairs = [swap(jnp.concatenate([blocks[m], out_blocks[m]]), "fsdp", m) for m in range(1, groups)]
    blocks = blocks[:1] + [p[:most] for p in pairs]
    out_cat = jnp.stack(out_blocks[:1] + [p[most:] for p in pairs])
    out_cat = jnp.concatenate([lax.dynamic_index_in_dim(out_cat, f ^ m, 0, keepdims=False) for m in range(groups)])
    first = jnp.concatenate([blocks[0], parts[groups * most :]])[None]
    marks = jnp.concatenate([doc_starts[0], valid_len])
    marks = jnp.concatenate([(marks // 32).astype(BF16), (marks % 32).astype(BF16)])
    flat = then(jnp.concatenate([marks] + [v.astype(BF16).reshape(-1) for v in small])[None], mine)
    rel_small = jnp.concatenate([flat] + [swap(flat, "fsdp", m) for m in range(1, groups)])
    order = jnp.arange(groups, dtype=jnp.int32) ^ f
    every = jnp.sum(
        jnp.where((order[None, :] == jnp.arange(groups)[:, None])[:, :, None], rel_small[None], 0), axis=1
    ).astype(F32)
    count = marks.shape[0] // 2
    marks = every[:, : 2 * count].astype(jnp.int32)
    marks = marks[:, :count] * 32 + marks[:, count:]
    every = every[:, 2 * count :]
    second = then(jnp.concatenate(blocks[1:])[None], rel_small)
    token_rows = lax.all_gather(tokens[0], "fsdp", axis=0, tiled=True)
    upstream_all = lax.all_gather(cotangent[0], "fsdp", axis=0, tiled=True)
    got = swap(first, "dp", 2 * z_masks[0])
    first_2 = jnp.concatenate([first, got])
    sent_a = then(first_2, second)
    sent_b = then(second, first_2)
    got_a = swap(sent_a, "dp", 2 * z_masks[1])
    got_b = swap(sent_b, "dp", 2 * z_masks[0])
    full, at = [], 0
    for v in small:
        piece = every[:, at : at + v.size]
        at += v.size
        if v.ndim == 1:
            full.append(piece.reshape(1, -1))
        else:
            full.append(jnp.moveaxis(piece.reshape((-1,) + v.shape), 0, 1).reshape(v.shape[0], -1))
    norm_full, gate_full, convw_full, convb_full, shift_full, logd_full, skip_full = full

    hidden = tokens[0].astype(F32)
    upstream = cotangent[0].astype(F32)
    live = (jnp.arange(length, dtype=jnp.int32) < valid_len[0]).astype(F32)[:, None]
    starts = marks[:, :-1]
    live_all = jnp.concatenate([(jnp.arange(length) < marks[r, -1]).astype(F32)[:, None] for r in range(groups)])

    second_2 = then(jnp.concatenate([second, got_b]), got_a)
    got_b2 = swap(second_2, "dp", 2 * z_masks[1])
    spread_a = jnp.concatenate([first_2, got_a])
    order_z = [0, z_masks[0]] + [z_masks[1], z_masks[0] ^ z_masks[1]]
    sibling_a = swap(then(spread_a, second_2), "dp", 1)
    sibling_b = swap(second_2, "dp", 1)
    normed_all = rows_into(None, 0, groups, length, [token_rows], norm_full)
    extra_at = jnp.stack([jnp.int32(r) for r in order_z]) == (z ^ (zs - 1))
    extra_at = jnp.sum(jnp.where(extra_at, jnp.arange(zs, dtype=jnp.int32), 0))
    extra_own = lax.dynamic_index_in_dim(then(spread_a, second_2), extra_at, 0, keepdims=False)[most:]
    extra_got = jnp.stack([extra_own] + [swap(extra_own, "fsdp", m) for m in range(1, groups)])
    extra_pair = [extra_got, swap(extra_got, "dp", 1)]
    w_shape = (2 * local, width)

    def place_main(buffer, arrays, ms, rc):
        where = [2 * (f ^ m) + (c ^ rc) for m in ms]
        return place_blocks(
            buffer, w_shape, arrays, most, order_z, where, lambda r: first_row(z ^ r), lambda r: rows_valid(z ^ r), cuts
        )

    w_main = place_main(None, [spread_a], [0], 0)
    w_main = place_main(w_main, [sibling_a], [0], 1)
    got_b2 = then(got_b2, normed_all, w_main)
    sibling_b2 = swap(got_b2, "dp", 1)
    others = range(1, groups)
    w_main = place_main(w_main, [second_2, got_b2], others, 0)
    w_main = place_main(w_main, [sibling_b, sibling_b2], others, 1)
    extra_items = []
    for m in range(groups):
        for rc in range(2):
            extra_items.append((extra_pair[rc], m, 0, k_rows * (f ^ m) + k_half * (c ^ rc), EXTRA, (0, EXTRA)))
    w_extra = place(None, (EXTRA, width), (EXTRA, width), (0, 0), extra_items)

    out_1 = then(out_cat[None], got_b2)
    out_got = swap(out_1, "dp", 2 * z_masks[0])

    w_dt = w_extra[2 * NS :].reshape(groups, groups, -1, width)
    w_dt = lax.dynamic_index_in_dim(w_dt, f, 1, keepdims=False).reshape(-1, width)
    w_own = jnp.concatenate([w_extra[: 2 * NS], w_dt, jnp.zeros((128 - w_dt.shape[0], width), BF16)])
    extra = matmul(normed_all, w_own, "nt", F32)
    dt_rows = extra[:, 2 * NS : 2 * NS + w_dt.shape[0]].T
    main = matmul(then(normed_all, extra), w_main, "nt", F32)
    common = (
        main, extra, dt_rows,
        own_channels(convw_full[:, :DI]), own_channels(convb_full[:, :DI]), convw_full[:, DI:], convb_full[:, DI:],
        own_channels(shift_full).T, own_channels(logd_full).T, own_channels(jnp.repeat(skip_full, HP, axis=1)),
    )
    half_rows = groups // 2
    out_2 = jnp.concatenate([out_1, then(out_got, main)])
    out_got = swap(out_2, "dp", 2 * z_masks[1])
    results = [mix_forward(0, length, then(starts[:half_rows], out_2), *common)]
    out_4 = jnp.concatenate([out_2, then(out_got, results[0][3])])
    out_sibling = swap(out_4, "dp", 1)
    results.append(mix_forward(half_rows, length, then(starts[half_rows:], out_4), *common))
    out_sibling = then(out_sibling, results[1][3])
    gated, y, states, squares = zip(*results)
    out_items = []
    for rc, array in enumerate((out_4, out_sibling)):
        for i, rel in enumerate(order_z):
            out_items.append((array, i, 0, out_cols * (2 * (z ^ rel) + (c ^ rc)), local, (0, local)))
    w_out_own = place(None, (local, width), (local, width), (0, 0), out_items)
    gain = own_channels(gate_full)

    def group_sum(v):
        return v, [swap(v, "fsdp", m) for m in range(1, groups)]

    def summed(parts, *late):
        v, got = parts
        for other in got:
            v = v + then(other, *late)
        return v

    squares = group_sum(jnp.concatenate(squares).reshape(groups, length))
    squares = summed(squares, w_out_own)
    q = lax.rsqrt(squares.reshape(-1, 1) * (1.0 / DI) + EPSILON)
    mixed = jnp.concatenate(
        [(g * q[i * half_rows * length : (i + 1) * half_rows * length] * gain).astype(BF16) for i, g in enumerate(gated)]
    )
    d_mixed, inner = mixed_gradient(upstream_all, w_out_own, live_all, mixed)
    inner = group_sum(inner.reshape(groups, length))
    out_full = matmul(then(mixed, inner[0]), upstream_all, "tn", scale=live_all.astype(BF16))
    branch = matmul(then(mixed, out_full), w_out_own, "nn")
    mean = q * q * summed(inner, out_full).reshape(-1, 1) * (1.0 / DI)

    def sum_low(a, b):
        return (a.astype(F32) + b.astype(F32)).astype(BF16)

    contract = (((0,), (0,)), ((), ()))


    out_own = lax.psum_scatter(out_full, "dp", scatter_dimension=1, tiled=True)
    d_mixed = then(d_mixed, branch)
    branch = lax.psum_scatter(branch, "fsdp", scatter_dimension=0, tiled=True)
    d_main, backs = None, []
    for i in range(2):
        begin = starts[i * half_rows : (i + 1) * half_rows]
        operand = d_mixed
        if i == 1:
            own = then(out_own, d_main)
            out_rows = [lax.dynamic_slice_in_dim(own, unit * (f ^ m), unit, 0) for m in range(groups)]
            operand = then(d_mixed, *out_rows)
            out_parts = [swap(out_rows[m], "fsdp", m) for m in range(1, groups)]
        result = mix_backward(
            i * half_rows, groups, length, d_main, begin, *common, gain, y[i], states[i], q, mean, operand
        )
        d_main = result[0]
        backs.append(result[1:])
    d_bc_in = jnp.concatenate([b[0] for b in backs])
    d_dt = jnp.concatenate([b[1] for b in backs], axis=1)
    s_gain, s_cw, s_cb, s_cwbc, s_cbbc, s_shift, s_logd, s_skip = [
        sum(p.sum(axis=0) for p in v) for v in list(zip(*backs))[2:]
    ]
    here = (jnp.arange(groups, dtype=jnp.int32) == f).astype(F32)

    def all_channels(v):
        v = v.reshape(v.shape[0], groups, 1, -1)
        return (v * here[None, None, :, None]).reshape(v.shape[0], -1)

    d_extra = jnp.concatenate([d_bc_in, all_channels(d_dt.T).astype(BF16)], axis=1)

    bundles = [(groups - 2, groups - 1), (0, 1)]

    def bundle_columns(value, bundle, core):
        return [lax.dynamic_slice_in_dim(value, k_rows * (f ^ m) + k_half * core, k_half, 1) for m in bundle]

    def chip_blocks(bundle, got):
        blocks = []
        for r in range(zs):
            row = slice_row(first_row(z ^ r))
            ours = [lax.dynamic_slice(main_sum, (row, k_rows * (f ^ m) + k_half * c), (most, k_half)) for m in bundle]
            theirs = lax.dynamic_slice_in_dim(got, row, most, 0)
            blocks.append(sum_low(jnp.concatenate(ours, axis=1), theirs))
        return blocks

    main_sum = matmul(then(d_main, *out_parts), normed_all, "tn")
    out_parts = jnp.stack(out_rows[:1] + out_parts)
    got_a = swap(jnp.concatenate(bundle_columns(main_sum, bundles[0], 1 - c), axis=1), "dp", 1)
    got_b = swap(jnp.concatenate(bundle_columns(main_sum, bundles[1], 1 - c), axis=1), "dp", 1)
    extra_sum = lax.dot_general(then(d_extra, main_sum), normed_all, contract, preferred_element_type=F32).astype(BF16)
    extra_sum = with_layout_constraint(extra_sum, Layout((0, 1)))
    halves_e = [jnp.stack(bundle_columns(extra_sum, range(groups), core)) for core in (c, 1 - c)]
    extra_theirs = swap(halves_e[1], "dp", 1)
    blocks_a = chip_blocks(bundles[0], then(got_a, extra_sum))
    blocks_b = chip_blocks(bundles[1], then(got_b, extra_sum))
    both = halves_e[0].astype(F32) + extra_theirs.astype(F32)
    total, both_low = both[0], both.astype(BF16)
    arriving = [swap(both_low[m], "fsdp", m) for m in range(1, groups)]
    sent_a, sent_b = jnp.stack(blocks_a[1::2]), jnp.stack(blocks_b[1::2])
    flying_a = swap(sent_a, "dp", 2 * z_masks[-1])
    flying_b = swap(sent_b, "dp", 2 * z_masks[-1])
    source = then(d_main, sent_a, sent_b, both_low, branch, *blocks_a[0::2], *blocks_b[0::2])
    middle = width // 2

    def to_normed(source, cols):
        return (dot(source, w_main[:, cols]) + dot(d_extra, w_extra[:, cols])).astype(BF16)

    partial = to_normed(source, slice(0, middle))
    d_normed = [lax.psum_scatter(partial, "fsdp", scatter_dimension=0, tiled=True)]
    flying_a = then(flying_a, partial)
    keep_a, sent_a = [sum_low(k, flying_a[i]) for i, k in enumerate(blocks_a[0::2])]
    flying_a = swap(sent_a, "dp", 2 * z_masks[0])
    partial = to_normed(then(d_main, keep_a, sent_a), slice(middle, width))
    d_normed.append(lax.psum_scatter(partial, "fsdp", scatter_dimension=0, tiled=True))
    flying_b, flying_a, _ = lax.optimization_barrier((flying_b, flying_a, partial))
    keep_b, sent_b = [sum_low(k, flying_b[i]) for i, k in enumerate(blocks_b[0::2])]
    done_a = sum_low(keep_a, flying_a)
    flying_b = swap(sent_b, "dp", 2 * z_masks[0])
    d_normed = jnp.concatenate(d_normed, axis=1).astype(F32)

    hidden = tokens[0].astype(F32)
    live = (jnp.arange(length, dtype=jnp.int32) < valid_len[0]).astype(F32)[:, None]
    scale = lax.rsqrt(jnp.mean(hidden * hidden, axis=-1, keepdims=True) + EPSILON)
    weighted = norm_full * d_normed
    average = jnp.mean(hidden * weighted, axis=-1, keepdims=True)
    grad_tokens = cotangent[0].astype(F32) + scale * weighted - hidden * (scale * scale * scale * average)
    s_norm = jnp.sum(hidden * scale * d_normed, axis=0)
    for got in arriving:
        total = total + then(got, sent_b).astype(F32)
    total = total.astype(BF16)
    total = sum_low(total, swap(total, "dp", 2 * z_masks[-1]))
    total = sum_low(total, swap(total, "dp", 2 * z_masks[0]))
    out_parts = then(out_parts, sent_b)
    s_gain, s_cw, s_cb, s_cwbc, s_cbbc, s_shift, s_logd, s_skip = [
        then(v, sent_b) for v in (s_gain, s_cw, s_cb, s_cwbc, s_cbbc, s_shift, s_logd, s_skip)
    ]
    done_b = sum_low(keep_b, then(flying_b, s_norm))
    recv = [None] * groups
    for block, bundle in ((done_a, bundles[0]), (done_b, bundles[1])):
        for i, m in enumerate(bundle):
            piece = block[:, i * k_half : (i + 1) * k_half]
            recv[m] = piece if m == 0 else swap(piece, "fsdp", m)


    grad_out = jnp.concatenate(
        [lax.dynamic_index_in_dim(out_parts, f ^ g, 0, keepdims=False) for g in range(groups)]
    ).astype(F32)
    blocks = jnp.concatenate(recv + [total])
    grad_chip = lax.dot_general(blocks, picks(rank + moved), contract, preferred_element_type=F32).astype(BF16)
    left, right = grad_chip[:, :per_dev], grad_chip[:, per_dev:]
    own = jnp.where(c == 0, left, right)
    got = swap(jnp.where(c == 0, right, left), "dp", 1)
    grad_in = jnp.concatenate([jnp.where(c == 0, own, got), jnp.where(c == 0, got, own)]).astype(F32)

    out_tokens = (hidden + branch.astype(F32) * live).astype(BF16)

    small_sums = (
        s_norm[None],
        all_channels(s_gain),
        jnp.concatenate([all_channels(s_cw), s_cwbc], axis=1),
        jnp.concatenate([all_channels(s_cb), s_cbbc], axis=1),
        all_channels(s_shift.T),
        all_channels(s_logd.T),
        all_channels(s_skip.reshape(1, -1, HP).sum(axis=2)),
    )
    flat = jnp.concatenate(
        [jnp.moveaxis(s.reshape(s.shape[0], groups, -1), 1, 0).reshape(groups, -1) for s in small_sums], axis=1
    )
    mine = lax.dynamic_index_in_dim(flat, f, 0, keepdims=True)
    for m in range(1, groups):
        mine = mine + swap(lax.dynamic_index_in_dim(flat, f ^ m, 0, keepdims=True), "fsdp", m)
    for mask in bits_of(dp):
        mine = mine + swap(mine, "dp", mask)
    return out_tokens, grad_tokens, (grad_in, grad_out) + split_small(mine[0], small)


def split_small(flat, small):
    result, at = [], 0
    for v in small:
        result.append(flat[at : at + v.size].reshape(v.shape))
        at += v.size
    return tuple(result)


def alone(tokens, cotangent, doc_starts, valid_len, weights, firsts, seconds):
    w_in, w_out = weights[:2]
    small = weights[2:]
    length = tokens.shape[1]
    hidden = tokens[0].astype(F32)
    upstream = cotangent[0].astype(F32)
    flat = jnp.concatenate([v.astype(BF16).reshape(-1) for v in small])
    every = lax.all_gather(flat, "fsdp", axis=0, tiled=False)
    full, at = [], 0
    for v in small:
        piece = every[:, at : at + v.size].astype(F32)
        at += v.size
        if v.ndim == 1:
            full.append(piece.reshape(1, -1))
        else:
            full.append(jnp.moveaxis(piece.reshape((-1,) + v.shape), 0, 1).reshape(v.shape[0], -1))
    norm_full, gate_full, convw_full, convb_full, shift_full, logd_full, skip_full = full
    in_full = lax.all_gather(
        lax.all_gather(w_in.astype(BF16), "dp", axis=1, tiled=True), "fsdp", axis=0, tiled=True
    )
    out_full = lax.all_gather(
        lax.all_gather(w_out.astype(BF16), "dp", axis=1, tiled=True), "fsdp", axis=0, tiled=True
    )
    scale = lax.rsqrt(jnp.mean(hidden * hidden, axis=-1, keepdims=True) + EPSILON)
    normed = (hidden * scale * norm_full).astype(BF16)
    projected = dot(normed, in_full)
    extra = projected[:, MAIN:]
    common = (
        projected[:, :MAIN], extra, extra[:, 2 * NS :].T, convw_full[:, :DI], convb_full[:, :DI],
        convw_full[:, DI:], convb_full[:, DI:], shift_full.T, logd_full.T, jnp.repeat(skip_full, HP, axis=1),
    )
    gated, y, states, squares = mix_forward(0, length, doc_starts, *common)
    q = lax.rsqrt(squares * (1.0 / DI) + EPSILON)
    mixed = (gated * q * gate_full).astype(BF16)
    live = (jnp.arange(length, dtype=jnp.int32) < valid_len[0]).astype(F32)[:, None]
    d_branch = (upstream * live).astype(BF16)
    out_tokens = (hidden + dot(mixed, out_full) * live).astype(BF16)
    d_mixed = dot_nt(d_branch, out_full)
    mean = q * q * jnp.sum(mixed.astype(F32) * d_mixed, axis=1, keepdims=True) * (1.0 / DI)
    d_main, d_bc_in, d_dt, *sums = mix_backward(
        0, 1, length, None, doc_starts, *common, gate_full, y, states, q, mean, d_mixed
    )
    s_gain, s_cw, s_cb, s_cwbc, s_cbbc, s_shift, s_logd, s_skip = [v[0] for v in sums]
    d_low = jnp.concatenate([d_main, d_bc_in, d_dt.T.astype(BF16)], axis=1)
    d_normed = dot_nt(d_low, in_full)
    weighted = norm_full * d_normed
    average = jnp.mean(hidden * weighted, axis=-1, keepdims=True)
    grad_tokens = upstream + scale * weighted - hidden * (scale * scale * scale * average)
    s_norm = jnp.sum(hidden * scale * d_normed, axis=0)
    contract = (((0,), (0,)), ((), ()))
    out_sum = lax.dot_general(mixed, d_branch, contract, preferred_element_type=F32).astype(BF16)
    in_sum = lax.dot_general(normed, d_low, contract, preferred_element_type=F32).astype(BF16)
    grads = []
    for total in (in_sum, out_sum):
        total = lax.psum_scatter(total, "fsdp", scatter_dimension=0, tiled=True)
        grads.append(lax.psum_scatter(total, "dp", scatter_dimension=1, tiled=True).astype(F32))
    sums = (
        s_norm[None],
        s_gain,
        jnp.concatenate([s_cw, s_cwbc], axis=1),
        jnp.concatenate([s_cb, s_cbbc], axis=1),
        s_shift.T,
        s_logd.T,
        s_skip.reshape(1, NH, HP).sum(axis=2),
    )
    parts = lax.axis_size("fsdp")
    flat = jnp.concatenate(
        [jnp.moveaxis(s.reshape(s.shape[0], parts, -1), 1, 0).reshape(parts, -1) for s in sums], axis=1
    )
    total = lax.psum(flat, ("dp", "fsdp"))
    mine = lax.dynamic_index_in_dim(total, lax.axis_index("fsdp"), 0, keepdims=False)
    return out_tokens, grad_tokens, tuple(grads) + split_small(mine, small)


def regular(w_in, dp, groups):
    zs = dp // 2
    if dp % 2 or zs & (zs - 1) or zs < 4 or groups & (groups - 1) or DI % (groups * groups * 128):
        return False
    local = DI // groups
    per_chip = 2 * w_in.shape[1]
    edges = [
        static_count(g, min(per_chip * zz, MAIN), local // groups, local) for zz in range(zs + 1) for g in range(groups)
    ]
    return local % BC == 0 and groups == 4 and zs == 4 and all(e % 16 == 0 for e in edges) and w_in.shape[0] % 256 == 0


def shards(tokens, cotangent, doc_starts, valid_len, *rest):
    weights, moments = rest[:9], rest[9:]
    firsts, seconds = moments[0::2], moments[1::2]
    dp, groups = lax.axis_size("dp"), lax.axis_size("fsdp")
    plan = grouped if regular(weights[0], dp, groups) else alone
    out_tokens, grad_tokens, grads = plan(tokens, cotangent, doc_starts, valid_len, weights, firsts, seconds)
    factor = 1.0 / math.sqrt(tokens.shape[0] * tokens.shape[1] * dp * groups)
    decay_flags = (True, True, False, False, True, True, False, False, False)
    results = []
    for i, (weight, gradient, first, second) in enumerate(zip(weights, grads, firsts, seconds)):
        direction, first_new, second_new = adam_direction(weight, gradient * factor, first, second, decay_flags[i])
        if i < 2:
            direction = weight - LEARN_RATE * direction
        results.extend((direction, first_new, second_new))
    return (out_tokens[None], grad_tokens[None]) + tuple(results)


def solution(mesh):
    rows3 = P(("dp", "fsdp"), None, None)
    both, split, last = P("fsdp", "dp"), P("fsdp"), P(None, "fsdp")
    small = (split, split, last, split, split, split, split)
    placed = (rows3, rows3, P(("dp", "fsdp"), None), P(("dp", "fsdp")), both, both) + small
    placed = placed + (both,) * 4 + tuple(s for s in small for _ in range(2))
    out = (rows3, rows3) + (both,) * 6 + tuple(s for s in small for _ in range(3))
    return jax.shard_map(shards, mesh=mesh, in_specs=placed, out_specs=out, check_vma=False)
```

```python
import functools
import math

import jax
import jax.numpy as jnp
from jax import lax
from jax.experimental import pallas as pl
from jax.experimental.layout import Layout, with_layout_constraint
from jax.experimental.pallas import tpu as pltpu
from jax.sharding import PartitionSpec as P

NH = 64
HP = 64
NS = 128
CONVW = 4
DI = 4096
CONV = 4352

EPSILON = 1e-05
BETA_ONE = 0.9
BETA_TWO = 0.95
ADAM_EPS = 1e-08
LEARN_RATE = 0.01
DECAY_RATE = 0.1
adam_step = 10
highest = lax.Precision.HIGHEST

Q = 128
BC = 512
HB = BC // HP
PAIRS = BC // 128
F32 = jnp.float32
BF16 = jnp.bfloat16


def dot(a, b):
    return jnp.dot(a, b, preferred_element_type=F32)


def dot_nt(a, b):
    return lax.dot_general(a, b, (((1,), (1,)), ((), ())), preferred_element_type=F32)


def sigmoid(v):
    return 1.0 / (1.0 + jnp.exp(-v))


def segment_of(starts_ref, position):
    row = pl.program_id(0)
    count = jnp.zeros_like(position)
    for k in range(starts_ref.shape[1]):
        count = count + (starts_ref[row, k] <= position).astype(jnp.int32)
    return count


def conv_forward(values, weights, bias, same_ref):
    total = values * weights[CONVW - 1 : CONVW] + bias
    for lag in range(1, CONVW):
        moved = pltpu.roll(values, lag, 0) * same_ref[lag - 1]
        total = total + moved * weights[CONVW - 1 - lag : CONVW - lag]
    return total


def conv_backward(d_conv, values, weights, same_ref):
    length = values.shape[0]
    d_in = d_conv * weights[CONVW - 1 : CONVW]
    sums = [jnp.sum(d_conv * values, axis=0, keepdims=True)]
    for lag in range(1, CONVW):
        masked = d_conv * same_ref[lag - 1]
        sums.append(jnp.sum(masked * pltpu.roll(values, lag, 0), axis=0, keepdims=True))
        d_in = d_in + pltpu.roll(masked, length - lag, 0) * weights[CONVW - 1 - lag : CONVW - lag]
    return d_in, jnp.concatenate(sums[::-1], axis=0), jnp.sum(d_conv, axis=0, keepdims=True)


def prepare_masks(starts_ref, length, same_ref, enter_ref, last_ref):
    col = lax.broadcasted_iota(jnp.int32, (length, 128), 0)
    seg = segment_of(starts_ref, col)
    for lag in range(1, CONVW):
        same_ref[lag - 1] = (segment_of(starts_ref, col - lag) == seg).astype(F32)
    begin = col - lax.rem(col, Q)
    enter_ref[...] = ((segment_of(starts_ref, begin - 1) == seg) & (begin > 0)).astype(F32)
    last_ref[...] = (segment_of(starts_ref, begin + (Q - 1)) == seg).astype(F32)


def keep_mask(starts_ref, chunk):
    rows = lax.broadcasted_iota(jnp.int32, (Q, Q), 0) + chunk * Q
    cols = lax.broadcasted_iota(jnp.int32, (Q, Q), 1) + chunk * Q
    return (rows >= cols) & (segment_of(starts_ref, rows) == segment_of(starts_ref, cols))


def step_rows(dt_ref, shift_ref, logd_ref):
    pre = dt_ref[...] + shift_ref[...]
    step = jnp.maximum(pre, 0.0) + jnp.log1p(jnp.exp(-jnp.abs(pre)))
    decay = jnp.exp(logd_ref[...])
    return pre, step, -step * decay, decay


def cumulate(rate, chunks):
    rows = lax.broadcasted_iota(jnp.int32, (Q, Q), 0)
    cols = lax.broadcasted_iota(jnp.int32, (Q, Q), 1)
    upper = (rows <= cols).astype(F32)
    parts = [
        jnp.dot(rate[:, c * Q : (c + 1) * Q], upper, precision=highest, preferred_element_type=F32)
        for c in range(chunks)
    ]
    return jnp.concatenate(parts, axis=1)


def halves(lo, pair):
    zero = jnp.zeros_like(pair)
    return jnp.concatenate([jnp.where(lo, pair, zero), jnp.where(lo, zero, pair)], axis=0)


def forward_kernel(
    starts_ref, gate_ref, xin_ref, bc_ref, dt_ref, cw_ref, cb_ref, cwbc_ref, cbbc_ref,
    shift_ref, logd_ref, skip_ref,
    gated_ref, y_ref, state_ref, total_ref,
    same_ref, enter_ref, last_ref, cmat_ref, bt_ref, score_ref, square_ref,
    x_ref, carry_ref, step_ref, cum_ref, cumt_ref, tailed_ref, decay_ref,
):
    j = pl.program_id(1)
    length = gate_ref.shape[0]
    chunks = length // Q
    lo = lax.broadcasted_iota(jnp.int32, (Q, 128), 1) < HP

    @pl.when(j == 0)
    def _():
        prepare_masks(starts_ref, length, same_ref, enter_ref, last_ref)
        square_ref[...] = jnp.zeros_like(square_ref)
        both = []
        for part in range(2):
            cols = slice(part * NS, (part + 1) * NS)
            conv = conv_forward(bc_ref[:, cols].astype(F32), cwbc_ref[:, cols], cbbc_ref[:, cols], same_ref)
            both.append(conv * sigmoid(conv))
        bmat, cmat = both
        cmat_ref[...] = cmat.astype(BF16)
        bt = bmat.T
        bt_ref[...] = bt.astype(BF16)
        for c in range(chunks):
            rows = slice(c * Q, (c + 1) * Q)
            score = jnp.dot(cmat[rows].astype(BF16), bt[:, rows].astype(BF16), preferred_element_type=F32)
            score_ref[c] = jnp.where(keep_mask(starts_ref, c), score, 0.0)

    _, step, rate, _ = step_rows(dt_ref, shift_ref, logd_ref)
    cum = cumulate(rate, chunks)
    cumt_ref[...] = cum
    cum_ref[...] = cum.T
    step_ref[...] = step.T
    carry_ref[...] = jnp.zeros_like(carry_ref)
    for p in range(PAIRS):
        cols = slice(p * 128, (p + 1) * 128)
        conv = conv_forward(xin_ref[:, cols].astype(F32), cw_ref[:, cols], cb_ref[:, cols], same_ref)
        x_ref[:, cols] = conv * sigmoid(conv)
    for c in range(chunks):
        rows = slice(c * Q, (c + 1) * Q)
        entering_state = carry_ref[...].astype(BF16)
        state_ref[0, c] = entering_state
        if c > 0:
            outside = dot(cmat_ref[rows, :], entering_state)
        score = score_ref[c]
        for p in range(PAIRS):
            cols = slice(p * 128, (p + 1) * 128)
            cum_a = jnp.broadcast_to(cum_ref[rows, 2 * p : 2 * p + 1], (Q, Q))
            cum_b = jnp.broadcast_to(cum_ref[rows, 2 * p + 1 : 2 * p + 2], (Q, Q))
            low_a = (score * jnp.exp(jnp.minimum(cum_a - cumt_ref[2 * p : 2 * p + 1, rows], 0.0))).astype(BF16)
            low_b = (score * jnp.exp(jnp.minimum(cum_b - cumt_ref[2 * p + 1 : 2 * p + 2, rows], 0.0))).astype(BF16)
            cum_x = jnp.where(lo, cum_a, cum_b)
            step_x = jnp.where(lo, step_ref[rows, 2 * p : 2 * p + 1], step_ref[rows, 2 * p + 1 : 2 * p + 2])
            x = x_ref[rows, cols]
            xs = (x * step_x).astype(BF16)
            y = dot(jnp.concatenate([low_a, low_b], axis=1), halves(lo, xs))
            reach = jnp.exp(cum_x) * enter_ref[rows]
            if c > 0:
                y = y + reach * outside[:, cols]
            if c < chunks - 1:
                tail = jnp.exp(cum_x[Q - 1 : Q] - cum_x) * last_ref[rows]
                tailed_ref[:, cols] = (xs.astype(F32) * tail).astype(BF16)
                decay_ref[0:1, cols] = reach[Q - 1 : Q]
            y_ref[rows, cols] = y
            gate = gate_ref[rows, cols].astype(F32)
            gated = (y + skip_ref[:, cols] * x) * (gate * sigmoid(gate))
            square_ref[rows, :] += gated * gated
            gated_ref[rows, cols] = gated
        if c < chunks - 1:
            carry_ref[...] = decay_ref[0:1, :] * carry_ref[...] + dot(bt_ref[:, rows], tailed_ref[...])

    @pl.when(j == pl.num_programs(1) - 1)
    def _():
        total_ref[...] = jnp.sum(square_ref[...], axis=1, keepdims=True)


def backward_body(
    starts_ref, gate_ref, xin_ref, bc_ref, dt_ref, cw_ref, cb_ref, cwbc_ref, cbbc_ref,
    shift_ref, logd_ref, skip_ref, gain_ref, y_ref, state_ref, q_ref, mean_ref, dm_ref,
    before_ref, dgate_ref, dbc_ref, ddt_ref, sgain_ref, scw_ref, scb_ref, scwbc_ref, scbbc_ref,
    sshift_ref, slogd_ref, sskip_ref,
    same_ref, enter_ref, last_ref, bmat_ref, cmat_ref, ct_ref, score_ref, scoret_ref,
    x_ref, slope_ref, dy_ref, dxs_ref, carry_ref, step_ref, cum_ref, cumt_ref,
    dscore_ref, db_ref, dc_ref, v1_ref, v2_ref, v3_ref, v4_ref, tailed_ref, reached_ref, decay_ref, held_ref,
):
    j = pl.program_id(2)
    length = gate_ref.shape[0]
    chunks = length // Q
    lo = lax.broadcasted_iota(jnp.int32, (Q, 128), 1) < HP

    def activate_bc(part):
        cols = slice(part * NS, (part + 1) * NS)
        return conv_forward(bc_ref[:, cols].astype(F32), cwbc_ref[:, cols], cbbc_ref[:, cols], same_ref)

    @pl.when(j == 0)
    def _():
        prepare_masks(starts_ref, length, same_ref, enter_ref, last_ref)
        both = []
        for part in range(2):
            conv = activate_bc(part)
            both.append(conv * sigmoid(conv))
        bmat, cmat = both
        bmat_ref[...] = bmat.astype(BF16)
        cmat_ref[...] = cmat.astype(BF16)
        bt = bmat.T
        ct_ref[...] = cmat.T.astype(BF16)
        for c in range(chunks):
            rows = slice(c * Q, (c + 1) * Q)
            score = jnp.dot(cmat[rows].astype(BF16), bt[:, rows].astype(BF16), preferred_element_type=F32)
            score = jnp.where(keep_mask(starts_ref, c), score, 0.0)
            score_ref[c] = score
            scoret_ref[c] = score.T
        dscore_ref[...] = jnp.zeros_like(dscore_ref)
        db_ref[...] = jnp.zeros_like(db_ref)
        dc_ref[...] = jnp.zeros_like(dc_ref)

    pre, step, rate, decay = step_rows(dt_ref, shift_ref, logd_ref)
    cum = cumulate(rate, chunks)
    cumt_ref[...] = cum
    cum_ref[...] = cum.T
    step_ref[...] = step.T
    carry_ref[...] = jnp.zeros_like(carry_ref)
    q = q_ref[...]
    mean = mean_ref[...]
    for p in range(PAIRS):
        cols = slice(p * 128, (p + 1) * 128)
        conv = conv_forward(xin_ref[:, cols].astype(F32), cw_ref[:, cols], cb_ref[:, cols], same_ref)
        sig = sigmoid(conv)
        x = conv * sig
        x_ref[:, cols] = x
        slope_ref[:, cols] = sig * (1.0 + conv - x)
        gate = gate_ref[:, cols].astype(F32)
        gsig = sigmoid(gate)
        silu = gate * gsig
        scanned = y_ref[:, cols] + skip_ref[:, cols] * x
        gated = scanned * silu
        scaled = dm_ref[:, cols].astype(F32) * q
        sgain_ref[0, :, cols] = jnp.sum(gated * scaled, axis=0, keepdims=True)
        d_gated = scaled * gain_ref[:, cols] - gated * mean
        dgate_ref[:, cols] = (d_gated * scanned * (gsig * (1.0 + gate - silu))).astype(dgate_ref.dtype)
        d_scanned = d_gated * silu
        dy_ref[:, cols] = d_scanned
        sskip_ref[0, :, cols] = jnp.sum(d_scanned * x, axis=0, keepdims=True)

    for c in reversed(range(chunks)):
        rows = slice(c * Q, (c + 1) * Q)
        score = score_ref[c]
        scoret = scoret_ref[c]
        d_state = carry_ref[...]
        d_state_low = d_state.astype(BF16)
        if c < chunks - 1:
            from_state = dot(bmat_ref[rows, :], d_state_low)
        d_score = dscore_ref[c]
        for p in range(PAIRS):
            cols = slice(p * 128, (p + 1) * 128)
            cum_a = jnp.broadcast_to(cum_ref[rows, 2 * p : 2 * p + 1], (Q, Q))
            cum_b = jnp.broadcast_to(cum_ref[rows, 2 * p + 1 : 2 * p + 2], (Q, Q))
            row_a = cumt_ref[2 * p : 2 * p + 1, rows]
            row_b = cumt_ref[2 * p + 1 : 2 * p + 2, rows]
            cum_x = jnp.where(lo, cum_a, cum_b)
            step_x = jnp.where(lo, step_ref[rows, 2 * p : 2 * p + 1], step_ref[rows, 2 * p + 1 : 2 * p + 2])
            x = x_ref[rows, cols]
            xs = (x * step_x).astype(BF16)
            xs_wide = xs.astype(F32)
            d_y = dy_ref[rows, cols]
            d_y_low = d_y.astype(BF16)
            pair = dot_nt(d_y_low, halves(lo, xs))
            d_score = d_score + pair[:, :Q] * jnp.exp(jnp.minimum(cum_a - row_a, 0.0))
            d_score = d_score + pair[:, Q:] * jnp.exp(jnp.minimum(cum_b - row_b, 0.0))
            up_a = (scoret * jnp.exp(jnp.minimum(row_a - cum_a, 0.0))).astype(BF16)
            up_b = (scoret * jnp.exp(jnp.minimum(row_b - cum_b, 0.0))).astype(BF16)
            d_xs = dot(jnp.concatenate([up_a, up_b], axis=1), halves(lo, d_y_low))
            v1_ref[rows, cols] = d_y_low.astype(F32) * y_ref[rows, cols] - xs_wide * d_xs
            reach = jnp.exp(cum_x) * enter_ref[rows]
            if c < chunks - 1:
                tail = jnp.exp(cum_x[Q - 1 : Q] - cum_x) * last_ref[rows]
                d_tail = tail * from_state[:, cols]
                v3_ref[rows, cols] = xs_wide * d_tail
                d_xs = d_xs + d_tail
                tailed_ref[:, cols] = (xs_wide * tail).astype(BF16)
                entered = state_ref[0, c, :, cols]
                v4_ref[c : c + 1, cols] = reach[Q - 1 : Q] * jnp.sum(
                    d_state[:, cols] * entered.astype(F32), axis=0, keepdims=True
                )
            else:
                v3_ref[rows, cols] = jnp.zeros((Q, 128), F32)
                v4_ref[c : c + 1, cols] = jnp.zeros((1, 128), F32)
            if c > 0:
                reached_ref[:, cols] = (reach * d_y).astype(BF16)
                decay_ref[0:1, cols] = reach[Q - 1 : Q]
            v2_ref[rows, cols] = x * d_xs
            dxs_ref[rows, cols] = step_x * d_xs + skip_ref[:, cols] * d_y
        dscore_ref[c] = d_score
        if c < chunks - 1:
            db_ref[rows, :] += dot_nt(tailed_ref[...], d_state_low)
        if c > 0:
            reached = reached_ref[...]
            dc_ref[rows, :] += dot_nt(reached, state_ref[0, c])
            carry_ref[...] = decay_ref[0:1, :] * d_state + dot(ct_ref[:, rows], reached)

    head = lax.broadcasted_iota(jnp.int32, (HB, BC), 0)
    lane = lax.broadcasted_iota(jnp.int32, (HB, BC), 1)
    pick = ((lane >= head * HP) & (lane < (head + 1) * HP)).astype(BF16)

    def by_head(values):
        high = values.astype(BF16)
        rest = (values - high.astype(F32)).astype(BF16)
        return dot_nt(pick, high) + dot_nt(pick, rest)

    h1 = by_head(v1_ref[...])
    h2 = by_head(v2_ref[...])
    h3 = by_head(v3_ref[...])
    h4 = by_head(v4_ref[...])
    rows_i = lax.broadcasted_iota(jnp.int32, (Q, Q), 0)
    cols_i = lax.broadcasted_iota(jnp.int32, (Q, Q), 1)
    suffix = (rows_i >= cols_i).astype(F32)
    prefix = (rows_i < cols_i).astype(F32)
    parts = []
    for c in range(chunks):
        rows = slice(c * Q, (c + 1) * Q)
        parts.append(
            jnp.dot(h1[:, rows], suffix, precision=highest, preferred_element_type=F32)
            + jnp.dot(h3[:, rows], prefix, precision=highest, preferred_element_type=F32)
            + h4[:, c : c + 1]
        )
    d_rate = jnp.concatenate(parts, axis=1)
    d_step = h2 - d_rate * decay
    d_raw = d_step * sigmoid(pre)
    ddt_ref[...] = d_raw
    sshift_ref[0] = jnp.sum(d_raw, axis=1, keepdims=True)
    slogd_ref[0] = jnp.sum(d_rate * rate, axis=1, keepdims=True)

    for p in range(PAIRS):
        cols = slice(p * 128, (p + 1) * 128)
        d_conv = dxs_ref[:, cols] * slope_ref[:, cols]
        d_in, s_w, s_b = conv_backward(d_conv, xin_ref[:, cols].astype(F32), cw_ref[:, cols], same_ref)
        held_ref[j, :, cols] = d_in.astype(BF16)
        scw_ref[0, :, cols] = s_w
        scb_ref[0, :, cols] = s_b

    @pl.when(j == pl.num_programs(2) - 1)
    def _():
        for c in range(chunks):
            rows = slice(c * Q, (c + 1) * Q)
            masked = jnp.where(keep_mask(starts_ref, c), dscore_ref[c], 0.0)
            dc_ref[rows, :] += dot(masked.astype(BF16), bmat_ref[rows, :])
            db_ref[rows, :] += dot(masked.T.astype(BF16), cmat_ref[rows, :])
        for part, grad_ref in ((0, db_ref), (1, dc_ref)):
            cols = slice(part * NS, (part + 1) * NS)
            conv = activate_bc(part)
            sig = sigmoid(conv)
            d_conv = grad_ref[...] * (sig * (1.0 + conv - conv * sig))
            d_in, s_w, s_b = conv_backward(d_conv, bc_ref[:, cols].astype(F32), cwbc_ref[:, cols], same_ref)
            dbc_ref[:, cols] = d_in.astype(dbc_ref.dtype)
            scwbc_ref[0, :, cols] = s_w
            scbbc_ref[0, :, cols] = s_b


def backward_kernel(*refs):
    outputs_at = 18

    @pl.when(pl.program_id(1) == 0)
    def _():
        backward_body(*refs)

    @pl.when(pl.program_id(1) == 1)
    def _():
        refs[outputs_at + 1][...] = refs[-1][pl.program_id(2)]


def backward_first(*refs):
    backward_kernel(*refs[:18], None, *refs[18:])


def forward_index(first, rows):
    return lambda r, j: (first + r, r, j)


def backward_index(first, rows):
    def index(r, s, j):
        r = jnp.minimum(r + s, rows - 1)
        return first + r, r, j * (1 - s)

    return index


def common_specs(index, length, channels):
    def at(shape, where):
        return pl.BlockSpec(shape, lambda *g: where(*index(*g)))

    blocks = channels // BC
    heads = at((HB, 1), lambda a, r, j: (j, 0))
    return at, [
        pl.BlockSpec(memory_space=pltpu.SMEM),
        at((length, BC), lambda a, r, j: (a, j)),
        at((length, BC), lambda a, r, j: (a, j + blocks)),
        at((length, 2 * NS), lambda a, r, j: (a, 0)),
        at((HB, length), lambda a, r, j: (j, a)),
        at((CONVW, BC), lambda a, r, j: (0, j)),
        at((1, BC), lambda a, r, j: (0, j)),
        at((CONVW, 2 * NS), lambda a, r, j: (0, 0)),
        at((1, 2 * NS), lambda a, r, j: (0, 0)),
        heads,
        heads,
        at((1, BC), lambda a, r, j: (0, j)),
    ]


def row_cost(size, weight):
    return pl.CostEstimate(flops=1000 * weight * size, bytes_accessed=12 * size, transcendentals=0)


def mix_forward(first, length, starts, main, extra, dt_rows, conv_w, conv_b, cw_bc, cb_bc, shift, logd, skip_cols):
    rows = starts.shape[0]
    channels = main.shape[1] // 2
    chunks = length // Q
    vmem = pltpu.VMEM
    _, in_specs = common_specs(forward_index(first, rows), length, channels)
    return pl.pallas_call(
        forward_kernel,
        grid=(rows, channels // BC),
        in_specs=in_specs,
        out_specs=[
            pl.BlockSpec((length, BC), lambda r, j: (r, j)),
            pl.BlockSpec((length, BC), lambda r, j: (r, j)),
            pl.BlockSpec((1, chunks, NS, BC), lambda r, j: (r, 0, 0, j)),
            pl.BlockSpec((length, 1), lambda r, j: (r, 0)),
        ],
        out_shape=[
            jax.ShapeDtypeStruct((rows * length, channels), F32),
            jax.ShapeDtypeStruct((rows * length, channels), F32),
            jax.ShapeDtypeStruct((rows, chunks, NS, channels), BF16),
            jax.ShapeDtypeStruct((rows * length, 1), F32),
        ],
        scratch_shapes=[
            vmem((CONVW - 1, length, 128), F32),
            vmem((length, 128), F32),
            vmem((length, 128), F32),
            vmem((length, NS), BF16),
            vmem((NS, length), BF16),
            vmem((chunks, Q, Q), F32),
            vmem((length, 128), F32),
            vmem((length, BC), F32),
            vmem((NS, BC), F32),
            vmem((length, HB), F32),
            vmem((length, HB), F32),
            vmem((HB, length), F32),
            vmem((Q, BC), BF16),
            vmem((8, BC), F32),
        ],
        compiler_params=pltpu.CompilerParams(vmem_limit_bytes=48 * 1024 * 1024),
        cost_estimate=row_cost(rows * length * channels, 18),
        name="mix_forward",
    )(starts, main, main, extra, dt_rows, conv_w, conv_b, cw_bc, cb_bc, shift, logd, skip_cols)


def mix_backward(
    first, total, length, before, starts, main, extra, dt_rows, conv_w, conv_b, cw_bc, cb_bc, shift, logd, skip_cols,
    gain, y, states, q, mean, d_mixed,
):
    rows = starts.shape[0]
    channels = main.shape[1] // 2
    heads = channels // HP
    blocks = channels // BC
    chunks = length // Q
    vmem = pltpu.VMEM
    at, in_specs = common_specs(backward_index(first, rows), length, channels)
    col = at((length, 1), lambda a, r, j: (a, 0))

    def result(shape, where):
        return pl.BlockSpec(shape, lambda r, s, j: where(r, jnp.maximum(j, s * (blocks - 1))))

    def row_sums(count):
        return result((1, count, BC), lambda r, j: (r, 0, j))

    per_head = result((1, HB, 1), lambda r, j: (r, j, 0))
    shape = jax.ShapeDtypeStruct
    operands = (
        starts, main, main, extra, dt_rows, conv_w, conv_b, cw_bc, cb_bc, shift, logd, skip_cols,
        gain, y, states, q, mean, d_mixed,
    )
    in_specs = in_specs + [
        at((1, BC), lambda a, r, j: (0, j)),
        at((length, BC), lambda a, r, j: (r, j)),
        at((1, chunks, NS, BC), lambda a, r, j: (r, 0, 0, j)),
        col,
        col,
        at((length, BC), lambda a, r, j: (a, j)),
    ]
    aliases = {}
    if before is not None:
        aliases = {len(operands): 0}
        operands = operands + (before,)
        in_specs = in_specs + [pl.BlockSpec(memory_space=pl.ANY)]
    return pl.pallas_call(
        backward_first if before is None else backward_kernel,
        grid=(rows, 2, blocks),
        in_specs=in_specs,
        out_specs=[
            pl.BlockSpec((length, BC), lambda r, s, j: (first + r, j + blocks * s)),
            result((length, 2 * NS), lambda r, j: (r, 0)),
            result((HB, length), lambda r, j: (j, r)),
            row_sums(1),
            row_sums(CONVW),
            row_sums(1),
            result((1, CONVW, 2 * NS), lambda r, j: (r, 0, 0)),
            result((1, 1, 2 * NS), lambda r, j: (r, 0, 0)),
            per_head,
            per_head,
            row_sums(1),
        ],
        out_shape=[
            shape((total * length, 2 * channels), BF16),
            shape((rows * length, 2 * NS), BF16),
            shape((heads, rows * length), F32),
            shape((rows, 1, channels), F32),
            shape((rows, CONVW, channels), F32),
            shape((rows, 1, channels), F32),
            shape((rows, CONVW, 2 * NS), F32),
            shape((rows, 1, 2 * NS), F32),
            shape((rows, heads, 1), F32),
            shape((rows, heads, 1), F32),
            shape((rows, 1, channels), F32),
        ],
        scratch_shapes=[
            vmem((CONVW - 1, length, 128), F32),
            vmem((length, 128), F32),
            vmem((length, 128), F32),
            vmem((length, NS), BF16),
            vmem((length, NS), BF16),
            vmem((NS, length), BF16),
            vmem((chunks, Q, Q), F32),
            vmem((chunks, Q, Q), F32),
            vmem((length, BC), F32),
            vmem((length, BC), F32),
            vmem((length, BC), F32),
            vmem((length, BC), F32),
            vmem((NS, BC), F32),
            vmem((length, HB), F32),
            vmem((length, HB), F32),
            vmem((HB, length), F32),
            vmem((chunks, Q, Q), F32),
            vmem((length, NS), F32),
            vmem((length, NS), F32),
            vmem((length, BC), F32),
            vmem((length, BC), F32),
            vmem((length, BC), F32),
            vmem((8, BC), F32),
            vmem((Q, BC), BF16),
            vmem((Q, BC), BF16),
            vmem((8, BC), F32),
            vmem((blocks, length, BC), BF16),
        ],
        input_output_aliases=aliases,
        compiler_params=pltpu.CompilerParams(vmem_limit_bytes=48 * 1024 * 1024),
        cost_estimate=row_cost(rows * length * channels, 42),
        name="mix_backward",
    )(*operands)


MAIN = 2 * DI
EXTRA = 2 * NS + NH


def adam_direction(weight, gradient, first, second, decayed):
    first_new = BETA_ONE * first + (1.0 - BETA_ONE) * gradient
    second_new = BETA_TWO * second + (1.0 - BETA_TWO) * gradient * gradient
    first_hat = first_new / (1.0 - BETA_ONE**adam_step)
    second_hat = second_new / (1.0 - BETA_TWO**adam_step)
    direction = first_hat / (jnp.sqrt(second_hat) + ADAM_EPS)
    if decayed:
        direction = direction + DECAY_RATE * weight
    return (direction, first_new, second_new)


def swap(value, axis, mask):
    size = lax.axis_size(axis)
    return lax.ppermute(value, axis, [(i, i ^ mask) for i in range(size)])


def bits_of(size):
    return [1 << b for b in reversed(range(size.bit_length() - 1))]


def place(buffer, shape, block, at, items):
    arrays, copies, table = [], [], [at[0], at[1]]
    for array, lead, row, col, valid, cuts in items:
        if not any(array is a for a in arrays):
            arrays.append(array)
        source = [array is a for a in arrays].index(True)
        for start, end in zip(cuts[:-1], cuts[1:]):
            copies.append((source, lead, start, end - start))
            table.extend([row, col, valid])
    table = jnp.stack([jnp.asarray(v, jnp.int32) for v in table])
    operands = [table] + arrays + ([] if buffer is None else [buffer])

    def kernel(table_ref, *refs):
        out_ref = refs[-1]
        for i, (source, lead, start, size) in enumerate(copies):
            piece = refs[source]
            row = pl.multiple_of(table_ref[3 * i + 2] + start, 16)
            col = pl.multiple_of(table_ref[3 * i + 3], 128)

            @pl.when(table_ref[3 * i + 4] > start)
            def _():
                rows = pl.ds(start, size)
                value = piece[rows, :] if lead is None else piece[lead, rows, :]
                out_ref[pl.ds(row, size), pl.ds(col, value.shape[1])] = value

    def all_of(a):
        return pl.BlockSpec(a.shape, lambda i, t: (0,) * a.ndim)

    return pl.pallas_call(
        kernel,
        grid_spec=pltpu.PrefetchScalarGridSpec(
            num_scalar_prefetch=1,
            grid=(1,),
            in_specs=[all_of(a) for a in arrays] + ([] if buffer is None else [pl.BlockSpec(memory_space=pl.ANY)]),
            out_specs=pl.BlockSpec(block, lambda i, t: (t[0], t[1])),
        ),
        out_shape=jax.ShapeDtypeStruct(shape, BF16),
        input_output_aliases={} if buffer is None else {len(operands) - 1: 0},
        compiler_params=pltpu.CompilerParams(vmem_limit_bytes=60 * 1024 * 1024),
        name="place",
    )(*operands)


def place_blocks(buffer, shape, arrays, size, order, columns, first_rows, counts, cuts):
    width, steps = arrays[0].shape[2], len(columns)
    pieces = [(a, n) for a, array in enumerate(arrays) for n in range(array.shape[0])]
    table = [jnp.asarray(v, jnp.int32) for v in columns]
    for rel in order:
        table.extend([first_rows(rel), counts(rel)])
    operands = [jnp.stack(table)] + list(arrays) + ([] if buffer is None else [buffer])

    def kernel(table_ref, *refs):
        for i, (a, n) in enumerate(pieces):
            begin = pl.multiple_of(table_ref[steps + 2 * i], 16)
            for start, end in zip(cuts[:-1], cuts[1:]):

                @pl.when(table_ref[steps + 2 * i + 1] > start)
                def _():
                    refs[-1][pl.ds(pl.multiple_of(begin + start, 16), end - start), :] = refs[a][n, start:end, :]

    return pl.pallas_call(
        kernel,
        grid_spec=pltpu.PrefetchScalarGridSpec(
            num_scalar_prefetch=1,
            grid=(steps,),
            in_specs=[pl.BlockSpec((a.shape[0], size, width), lambda i, t: (0, i, 0)) for a in arrays]
            + ([] if buffer is None else [pl.BlockSpec(memory_space=pl.ANY)]),
            out_specs=pl.BlockSpec((shape[0], width), lambda i, t: (0, t[i])),
        ),
        out_shape=jax.ShapeDtypeStruct(shape, BF16),
        input_output_aliases={} if buffer is None else {len(operands) - 1: 0},
        compiler_params=pltpu.CompilerParams(vmem_limit_bytes=60 * 1024 * 1024),
        name="place_blocks",
    )(*operands)


def matmul(a, b, kind, out_dtype=BF16, scale=None, more=None):
    m = a.shape[1] if kind == "tn" else a.shape[0]
    k = a.shape[0] if kind == "tn" else a.shape[1]
    n = b.shape[0] if kind == "nt" else b.shape[1]
    tm, tn = min(m, 1024), min(n, 512)
    dims = {"nn": ((1,), (0,)), "nt": ((1,), (1,)), "tn": ((0,), (0,))}[kind]

    def kernel(*refs):
        first = refs[0][...]
        if scale is not None:
            first = first * refs[2][...]
        total = lax.dot_general(first, refs[1][...], (dims, ((), ())), preferred_element_type=F32)
        if more is not None:
            total = total + dot(refs[2][...], refs[3][...])
        refs[-1][...] = total.astype(out_dtype)

    in_specs = [
        pl.BlockSpec((k, tm), lambda i, j: (0, i)) if kind == "tn" else pl.BlockSpec((tm, k), lambda i, j: (i, 0)),
        pl.BlockSpec((tn, k), lambda i, j: (j, 0)) if kind == "nt" else pl.BlockSpec((k, tn), lambda i, j: (0, j)),
    ]
    operands = [a, b]
    if more is not None:
        inner = more[0].shape[1]
        in_specs += [pl.BlockSpec((tm, inner), lambda i, j: (i, 0)), pl.BlockSpec((inner, tn), lambda i, j: (0, j))]
        operands += list(more)
    if scale is not None:
        in_specs.append(pl.BlockSpec((k, 1), lambda i, j: (0, 0)))
        operands.append(scale)
    return pl.pallas_call(
        kernel,
        grid=(m // tm, n // tn),
        in_specs=in_specs,
        out_specs=pl.BlockSpec((tm, tn), lambda i, j: (i, j)),
        out_shape=jax.ShapeDtypeStruct((m, n), out_dtype),
        compiler_params=pltpu.CompilerParams(vmem_limit_bytes=56 * 1024 * 1024),
        cost_estimate=pl.CostEstimate(flops=2 * m * n * k, bytes_accessed=2 * (m * k + n * k + m * n), transcendentals=0),
        name="matmul_" + kind,
    )(*operands)


def matmul_blocks(a, b, size, chosen):
    k, m = a.shape
    tm, count = min(m, 2048), len(chosen) // 2

    def kernel(chosen_ref, a_ref, b_ref, first_ref, second_ref):
        total = lax.dot_general(a_ref[...], b_ref[...], (((0,), (0,)), ((), ())), preferred_element_type=F32)

        @pl.when(pl.program_id(1) < count)
        def _():
            first_ref[...] = total.astype(BF16)

        @pl.when(pl.program_id(1) >= count)
        def _():
            second_ref[...] = total.astype(BF16)

    return pl.pallas_call(
        kernel,
        grid_spec=pltpu.PrefetchScalarGridSpec(
            num_scalar_prefetch=1,
            grid=(m // tm, 2 * count),
            in_specs=[
                pl.BlockSpec((k, tm), lambda i, j, t: (0, i)),
                pl.BlockSpec((k, size), lambda i, j, t: (0, t[j])),
            ],
            out_specs=[
                pl.BlockSpec((tm, size), lambda i, j, t: (i, jnp.minimum(j, count - 1))),
                pl.BlockSpec((tm, size), lambda i, j, t: (i, jnp.maximum(j - count, 0))),
            ],
        ),
        out_shape=[jax.ShapeDtypeStruct((m, size * count), BF16)] * 2,
        compiler_params=pltpu.CompilerParams(vmem_limit_bytes=56 * 1024 * 1024),
        name="matmul_blocks",
    )(jnp.stack([jnp.asarray(v, jnp.int32) for v in chosen]), a, b)


def mixed_gradient(upstream, weights, live, mixed):
    rows, width = upstream.shape
    local = weights.shape[0]
    tm, tn = min(rows, 1024), min(local, 512)

    def kernel(up_ref, w_ref, live_ref, mixed_ref, out_ref, inner_ref):
        total = (dot_nt(up_ref[...], w_ref[...]) * live_ref[...]).astype(BF16)
        out_ref[...] = total
        part = jnp.sum(total.astype(F32) * mixed_ref[...].astype(F32), axis=1, keepdims=True)

        @pl.when(pl.program_id(1) == 0)
        def _():
            inner_ref[...] = part

        @pl.when(pl.program_id(1) > 0)
        def _():
            inner_ref[...] += part

    return pl.pallas_call(
        kernel,
        grid=(rows // tm, local // tn),
        in_specs=[
            pl.BlockSpec((tm, width), lambda i, j: (i, 0)),
            pl.BlockSpec((tn, width), lambda i, j: (j, 0)),
            pl.BlockSpec((tm, 1), lambda i, j: (i, 0)),
            pl.BlockSpec((tm, tn), lambda i, j: (i, j)),
        ],
        out_specs=[pl.BlockSpec((tm, tn), lambda i, j: (i, j)), pl.BlockSpec((tm, 1), lambda i, j: (i, 0))],
        out_shape=[jax.ShapeDtypeStruct((rows, local), BF16), jax.ShapeDtypeStruct((rows, 1), F32)],
        compiler_params=pltpu.CompilerParams(vmem_limit_bytes=56 * 1024 * 1024),
        name="mixed_gradient",
    )(upstream, weights, live, mixed)


def rows_into(buffer, row, rows, length, pieces, gain=None):
    tile = 128
    counts = [p.shape[0] // tile for p in pieces]
    starts = [sum(counts[:i]) for i in range(len(counts) + 1)]
    width = pieces[0].shape[1]
    operands = list(pieces) + ([] if gain is None else [gain]) + ([] if buffer is None else [buffer])

    def kernel(*refs):
        step = pl.program_id(0)
        for i in range(len(pieces)):

            @pl.when((step >= starts[i]) & (step < starts[i + 1]))
            def _():
                value = refs[i][...]
                if gain is not None:
                    value = value.astype(F32)
                    mean = jnp.mean(value * value, axis=1, keepdims=True)
                    value = (value * lax.rsqrt(mean + EPSILON) * refs[len(pieces)][...]).astype(BF16)
                refs[-1][...] = value

    def piece_spec(i):
        return pl.BlockSpec((tile, width), lambda s: (jnp.clip(s - starts[i], 0, counts[i] - 1), 0))

    specs = [piece_spec(i) for i in range(len(pieces))]
    if gain is not None:
        specs.append(pl.BlockSpec(gain.shape, lambda s: (0, 0)))
    if buffer is not None:
        specs.append(pl.BlockSpec(memory_space=pl.ANY))
    return pl.pallas_call(
        kernel,
        grid=(starts[-1],),
        in_specs=specs,
        out_specs=pl.BlockSpec((tile, width), lambda s: (row * length // tile + s, 0)),
        out_shape=jax.ShapeDtypeStruct((rows * length, width), BF16),
        input_output_aliases={} if buffer is None else {len(operands) - 1: 0},
        compiler_params=pltpu.CompilerParams(vmem_limit_bytes=60 * 1024 * 1024),
        name="rows_into",
    )(*operands)


def prefix_count(g, n, unit, period):
    return (n // period) * unit + jnp.clip(n % period - g * unit, 0, unit)


def static_count(g, n, unit, period):
    return (n // period) * unit + min(max(n % period - g * unit, 0), unit)


def together(*values):
    return lax.optimization_barrier(values)


def then(value, *earlier):
    return lax.optimization_barrier((value,) + earlier)[0]


def spread_z(bundle, masks, late=()):
    have, order = bundle[None], [0]
    for i, mask in enumerate(masks):
        if i > 0:
            have = then(have, *late)
        have = jnp.concatenate([have, swap(have, "dp", 2 * mask)])
        order = order + [rel ^ mask for rel in order]
    return have, order


def grouped(tokens, cotangent, doc_starts, valid_len, weights, firsts, seconds):
    w_in, w_out, norm_gain, gate_gain, conv_w, conv_b, dt_bias, a_log, d_skip = weights
    small = weights[2:]
    dp, groups = lax.axis_size("dp"), lax.axis_size("fsdp")
    zs = dp // 2
    d, f = lax.axis_index("dp"), lax.axis_index("fsdp")
    z, c = d // 2, d % 2
    z_masks = bits_of(zs)
    length, width = tokens.shape[1], tokens.shape[2]
    local = DI // groups
    unit = local // groups
    k_rows, per_dev = w_in.shape
    k_half = k_rows // 2
    per_chip = 2 * per_dev
    out_cols = w_out.shape[1]
    sizes = {
        (zz, g): static_count(g, min(per_chip * (zz + 1), MAIN), unit, local)
        - static_count(g, min(per_chip * zz, MAIN), unit, local)
        for zz in range(zs)
        for g in range(groups)
    }
    cuts = [0] + sorted(set(sizes.values()) - {0})
    most = cuts[-1]

    def first_row(zz):
        return prefix_count(f, jnp.minimum(per_chip * zz, MAIN), unit, local)

    def rows_valid(zz):
        return first_row(zz + 1) - first_row(zz)

    def slice_row(row):
        return jnp.minimum(row, 2 * local - most)

    low = w_in.astype(BF16)
    mine = lax.dynamic_slice_in_dim(low, k_half * c, k_half, 0)
    other = swap(lax.dynamic_slice_in_dim(low, k_half * (1 - c), k_half, 0), "dp", 1)
    chip = jnp.concatenate([jnp.where(c == 0, mine, other), jnp.where(c == 0, other, mine)], axis=1)
    column = per_chip * z + jnp.arange(per_chip, dtype=jnp.int32)
    owner = (column // unit) % groups
    begin = prefix_count(owner, per_chip * z, unit, local)
    rank = prefix_count(owner, column, unit, local) - begin
    moved = begin - slice_row(begin)
    extra_key = groups * most + column - MAIN
    places = jnp.arange(groups * most + EXTRA, dtype=jnp.int32)[:, None]

    def picks(ranks):
        key = jnp.where(column < MAIN, (owner ^ f) * most + ranks, extra_key)
        return (places == key[None, :]).astype(BF16)

    parts = dot_nt(picks(rank), chip).astype(BF16)

    def own_channels(v):
        v = v.reshape(v.shape[0], groups, groups, -1)
        return lax.dynamic_index_in_dim(v, f, 2, keepdims=False).reshape(v.shape[0], -1)

    out_low = w_out.astype(BF16).reshape(groups, unit, out_cols)
    out_blocks = [lax.dynamic_index_in_dim(out_low, f ^ m, 0, keepdims=False) for m in range(groups)]
    blocks = [parts[m * most : (m + 1) * most] for m in range(groups)]
    blocks = blocks[:1] + [swap(blocks[m], "fsdp", m) for m in range(1, groups)]
    first = jnp.concatenate([blocks[0], parts[groups * most :]])[None]
    marks = jnp.concatenate([doc_starts[0], valid_len])
    marks = jnp.concatenate([(marks // 32).astype(BF16), (marks % 32).astype(BF16)])
    flat = then(jnp.concatenate([marks] + [v.astype(BF16).reshape(-1) for v in small])[None], mine)
    rel_small = jnp.concatenate([flat] + [swap(flat, "fsdp", m) for m in range(1, groups)])
    order = jnp.arange(groups, dtype=jnp.int32) ^ f
    every = jnp.sum(
        jnp.where((order[None, :] == jnp.arange(groups)[:, None])[:, :, None], rel_small[None], 0), axis=1
    ).astype(F32)
    count = marks.shape[0] // 2
    marks = every[:, : 2 * count].astype(jnp.int32)
    marks = marks[:, :count] * 32 + marks[:, count:]
    every = every[:, 2 * count :]
    second = then(jnp.concatenate(blocks[1:])[None], rel_small)
    token_rows = lax.all_gather(tokens[0], "fsdp", axis=0, tiled=True)
    upstream_all = lax.all_gather(cotangent[0], "fsdp", axis=0, tiled=True)
    got = swap(first, "dp", 2 * z_masks[0])
    first_2 = jnp.concatenate([first, got])
    sent_a = then(first_2, second)
    sent_b = then(second, first_2)
    got_a = swap(sent_a, "dp", 2 * z_masks[1])
    got_b = swap(sent_b, "dp", 2 * z_masks[0])
    full, at = [], 0
    for v in small:
        piece = every[:, at : at + v.size]
        at += v.size
        if v.ndim == 1:
            full.append(piece.reshape(1, -1))
        else:
            full.append(jnp.moveaxis(piece.reshape((-1,) + v.shape), 0, 1).reshape(v.shape[0], -1))
    norm_full, gate_full, convw_full, convb_full, shift_full, logd_full, skip_full = full

    hidden = tokens[0].astype(F32)
    upstream = cotangent[0].astype(F32)
    live = (jnp.arange(length, dtype=jnp.int32) < valid_len[0]).astype(F32)[:, None]
    starts = marks[:, :-1]
    live_all = jnp.concatenate([(jnp.arange(length) < marks[r, -1]).astype(F32)[:, None] for r in range(groups)])

    out_blocks = [then(v, sent_b) for v in out_blocks]
    out_cat = jnp.stack(out_blocks[:1] + [swap(out_blocks[m], "fsdp", m) for m in range(1, groups)])
    out_cat = jnp.concatenate([lax.dynamic_index_in_dim(out_cat, f ^ m, 0, keepdims=False) for m in range(groups)])
    second_2, got_a, out_cat = together(jnp.concatenate([second, got_b]), got_a, out_cat)
    got_b2 = swap(second_2, "dp", 2 * z_masks[1])
    spread_a = jnp.concatenate([first_2, got_a])
    order_z = [0, z_masks[0]] + [z_masks[1], z_masks[0] ^ z_masks[1]]
    sibling_a = swap(then(spread_a, second_2), "dp", 1)
    sibling_b = swap(second_2, "dp", 1)
    extra_at = jnp.stack([jnp.int32(r) for r in order_z]) == (z ^ (zs - 1))
    extra_at = jnp.sum(jnp.where(extra_at, jnp.arange(zs, dtype=jnp.int32), 0))
    extra_own = lax.dynamic_index_in_dim(then(spread_a, second_2), extra_at, 0, keepdims=False)[most:]
    extra_got = jnp.stack([extra_own] + [swap(extra_own, "fsdp", m) for m in range(1, groups)])
    w_shape = (2 * local, width)

    def place_main(buffer, arrays, ms, rc):
        where = [2 * (f ^ m) + (c ^ rc) for m in ms]
        return place_blocks(
            buffer, w_shape, arrays, most, order_z, where, lambda r: first_row(z ^ r), lambda r: rows_valid(z ^ r), cuts
        )

    w_main = place_main(None, [spread_a], [0], 0)
    w_main = place_main(w_main, [sibling_a], [0], 1)
    normed_all = rows_into(None, 0, groups, length, [then(token_rows, w_main)], norm_full)
    extra_got = then(extra_got, w_main)
    extra_pair = [extra_got, swap(extra_got, "dp", 1)]
    extra_pair[1] = then(extra_pair[1], normed_all)
    extra_items = []
    for m in range(groups):
        for rc in range(2):
            extra_items.append((extra_pair[rc], m, 0, k_rows * (f ^ m) + k_half * (c ^ rc), EXTRA, (0, EXTRA)))
    w_extra = place(None, (EXTRA, width), (EXTRA, width), (0, 0), extra_items)
    w_dt = w_extra[2 * NS :].reshape(groups, groups, -1, width)
    w_dt = lax.dynamic_index_in_dim(w_dt, f, 1, keepdims=False).reshape(-1, width)
    w_own = jnp.concatenate([w_extra[: 2 * NS], w_dt, jnp.zeros((128 - w_dt.shape[0], width), BF16)])
    extra = matmul(normed_all, w_own, "nt", F32)
    dt_rows = extra[:, 2 * NS : 2 * NS + w_dt.shape[0]].T
    got_b2 = then(got_b2, normed_all, w_main, extra)
    sibling_b2 = swap(got_b2, "dp", 1)
    others = range(1, groups)
    w_main = place_main(w_main, [second_2, got_b2], others, 0)
    w_main = place_main(w_main, [sibling_b, sibling_b2], others, 1)
    out_1 = then(out_cat[None], got_b2)
    out_got = swap(out_1, "dp", 2 * z_masks[0])

    main = matmul(then(normed_all, extra), w_main, "nt", F32)
    common = (
        main, extra, dt_rows,
        own_channels(convw_full[:, :DI]), own_channels(convb_full[:, :DI]), convw_full[:, DI:], convb_full[:, DI:],
        own_channels(shift_full).T, own_channels(logd_full).T, own_channels(jnp.repeat(skip_full, HP, axis=1)),
    )
    half_rows = groups // 2
    out_2 = jnp.concatenate([out_1, then(out_got, main)])
    out_got = swap(out_2, "dp", 2 * z_masks[1])
    results = [mix_forward(0, length, then(starts[:half_rows], out_2), *common)]
    out_4 = jnp.concatenate([out_2, then(out_got, results[0][3])])
    out_sibling = swap(out_4, "dp", 1)
    results.append(mix_forward(half_rows, length, then(starts[half_rows:], out_4), *common))
    out_sibling = then(out_sibling, results[1][3])
    gated, y, states, squares = zip(*results)
    out_items = []
    for rc, array in enumerate((out_4, out_sibling)):
        for i, rel in enumerate(order_z):
            out_items.append((array, i, 0, out_cols * (2 * (z ^ rel) + (c ^ rc)), local, (0, local)))
    w_out_own = place(None, (local, width), (local, width), (0, 0), out_items)
    gain = own_channels(gate_full)

    def group_sum(v):
        return v, [swap(v, "fsdp", m) for m in range(1, groups)]

    def summed(parts, *late):
        v, got = parts
        for other in got:
            v = v + then(other, *late)
        return v

    squares = group_sum(jnp.concatenate(squares).reshape(groups, length))
    squares = summed(squares, w_out_own)
    q = lax.rsqrt(squares.reshape(-1, 1) * (1.0 / DI) + EPSILON)
    mixed = jnp.concatenate(
        [(g * q[i * half_rows * length : (i + 1) * half_rows * length] * gain).astype(BF16) for i, g in enumerate(gated)]
    )
    d_mixed, inner = mixed_gradient(upstream_all, w_out_own, live_all, mixed)
    inner = group_sum(inner.reshape(groups, length))
    out_full = matmul(then(mixed, inner[0]), upstream_all, "tn", scale=live_all.astype(BF16))
    branch = matmul(then(mixed, out_full), w_out_own, "nn")
    mean = q * q * summed(inner, out_full).reshape(-1, 1) * (1.0 / DI)

    def sum_low(a, b):
        return (a.astype(F32) + b.astype(F32)).astype(BF16)

    contract = (((0,), (0,)), ((), ()))


    out_own = lax.psum_scatter(out_full, "dp", scatter_dimension=1, tiled=True)
    d_mixed = then(d_mixed, branch)
    branch = lax.psum_scatter(branch, "fsdp", scatter_dimension=0, tiled=True)
    d_main, backs = None, []
    for i in range(2):
        begin = starts[i * half_rows : (i + 1) * half_rows]
        d_main, *result = mix_backward(
            i * half_rows, groups, length, d_main, begin, *common, gain, y[i], states[i], q, mean, d_mixed
        )
        backs.append(result)
    d_bc_in = jnp.concatenate([b[0] for b in backs])
    d_dt = jnp.concatenate([b[1] for b in backs], axis=1)
    sums = [jnp.concatenate(v) for v in list(zip(*backs))[2:]]
    here = (jnp.arange(groups, dtype=jnp.int32) == f).astype(F32)

    def all_channels(v):
        v = v.reshape(v.shape[0], groups, 1, -1)
        return (v * here[None, None, :, None]).reshape(v.shape[0], -1)

    d_extra = jnp.concatenate([d_bc_in, all_channels(d_dt.T).astype(BF16)], axis=1)

    bundles = [(groups - 2, groups - 1), (0, 1)]

    def bundle_columns(value, bundle, core):
        return [lax.dynamic_slice_in_dim(value, k_rows * (f ^ m) + k_half * core, k_half, 1) for m in bundle]

    def chip_blocks(bundle, got):
        size = 2 * k_half
        blocks = []
        for r in range(zs):
            row = slice_row(first_row(z ^ r))
            blocks.append(sum_low(*[lax.dynamic_slice(v, (row, bundle * size), (most, size)) for v in (main_sum, got)]))
        return blocks

    middle = width // 2
    order_m = bundles[0] + bundles[1]
    extra_sum = lax.dot_general(d_extra, normed_all, contract, preferred_element_type=F32).astype(BF16)
    extra_sum = with_layout_constraint(extra_sum, Layout((0, 1)))
    halves_e = [jnp.stack(bundle_columns(extra_sum, range(groups), core)) for core in (c, 1 - c)]
    extra_theirs = swap(halves_e[1], "dp", 1)
    partial = matmul(then(d_main, halves_e[1]), w_main, "nn", more=(d_extra, w_extra))
    partial, extra_theirs = together(partial, extra_theirs)
    d_normed = lax.psum_scatter(partial, "fsdp", scatter_dimension=0, tiled=True).astype(F32)
    both = halves_e[0].astype(F32) + extra_theirs.astype(F32)
    total, both_low = both[0], both.astype(BF16)
    arriving = [swap(both_low[m], "fsdp", m) for m in range(1, groups)]
    chosen = [2 * (f ^ m) + core for core in (1 - c, c) for m in order_m]
    sum_theirs, main_sum = matmul_blocks(then(d_main, both_low, branch), normed_all, k_half, chosen)
    sum_theirs, *arriving = together(sum_theirs, *arriving)
    got = swap(sum_theirs, "dp", 1)
    for other in arriving:
        total = total + other.astype(F32)
    total = total.astype(BF16)
    got, total = together(got, total)
    blocks_a, blocks_b = chip_blocks(0, got), chip_blocks(1, got)
    near, far = z_masks[-1], z_masks[0]
    sent_a = jnp.stack([blocks_a[near], blocks_a[near | far]])
    sent_b = jnp.stack([blocks_b[far], blocks_b[near | far]])
    got_a, got_b, got_e = together(
        swap(sent_a, "dp", 2 * near), swap(sent_b, "dp", 2 * far), swap(total, "dp", 2 * near)
    )
    total = sum_low(total, got_e)
    keep_a, sent_a = sum_low(blocks_a[0], got_a[0]), sum_low(blocks_a[far], got_a[1])
    keep_b, sent_b = sum_low(blocks_b[0], got_b[0]), sum_low(blocks_b[near], got_b[1])
    got_a, got_b, got_e = together(
        swap(sent_a, "dp", 2 * far), swap(sent_b, "dp", 2 * near), swap(total, "dp", 2 * far)
    )
    total = sum_low(total, got_e)
    done_a, done_b = sum_low(keep_a, got_a), sum_low(keep_b, got_b)
    recv = [None] * groups
    for block, bundle in ((done_a, bundles[0]), (done_b, bundles[1])):
        for i, m in enumerate(bundle):
            piece = block[:, i * k_half : (i + 1) * k_half]
            recv[m] = piece if m == 0 else swap(piece, "fsdp", m)
    recv = together(*recv)
    sent_b = recv[-1]

    hidden = then(tokens[0], sent_b).astype(F32)
    live = (jnp.arange(length, dtype=jnp.int32) < valid_len[0]).astype(F32)[:, None]
    scale = lax.rsqrt(jnp.mean(hidden * hidden, axis=-1, keepdims=True) + EPSILON)
    weighted = norm_full * d_normed
    average = jnp.mean(hidden * weighted, axis=-1, keepdims=True)
    grad_tokens = cotangent[0].astype(F32) + scale * weighted - hidden * (scale * scale * scale * average)
    s_norm = jnp.sum(hidden * scale * d_normed, axis=0)
    own = then(out_own, sent_b)
    out_rows = [lax.dynamic_slice_in_dim(own, unit * (f ^ m), unit, 0) for m in range(groups)]
    out_parts = jnp.stack(out_rows[:1] + [swap(out_rows[m], "fsdp", m) for m in range(1, groups)])
    s_gain, s_cw, s_cb, s_cwbc, s_cbbc, s_shift, s_logd, s_skip = [
        then(v, sent_b).sum(axis=0) for v in sums
    ]
    grad_out = jnp.concatenate(
        [lax.dynamic_index_in_dim(out_parts, f ^ g, 0, keepdims=False) for g in range(groups)]
    ).astype(F32)
    blocks = jnp.concatenate([*recv, total])
    grad_chip = lax.dot_general(blocks, picks(rank + moved), contract, preferred_element_type=F32).astype(BF16)
    left, right = grad_chip[:, :per_dev], grad_chip[:, per_dev:]
    own = jnp.where(c == 0, left, right)
    got = swap(jnp.where(c == 0, right, left), "dp", 1)
    grad_in = jnp.concatenate([jnp.where(c == 0, own, got), jnp.where(c == 0, got, own)]).astype(F32)

    out_tokens = (hidden + branch.astype(F32) * live).astype(BF16)

    small_sums = (
        s_norm[None],
        all_channels(s_gain),
        jnp.concatenate([all_channels(s_cw), s_cwbc], axis=1),
        jnp.concatenate([all_channels(s_cb), s_cbbc], axis=1),
        all_channels(s_shift.T),
        all_channels(s_logd.T),
        all_channels(s_skip.reshape(1, -1, HP).sum(axis=2)),
    )
    flat = jnp.concatenate(
        [jnp.moveaxis(s.reshape(s.shape[0], groups, -1), 1, 0).reshape(groups, -1) for s in small_sums], axis=1
    )
    mine = lax.dynamic_index_in_dim(flat, f, 0, keepdims=True)
    for m in range(1, groups):
        mine = mine + swap(lax.dynamic_index_in_dim(flat, f ^ m, 0, keepdims=True), "fsdp", m)
    for mask in bits_of(dp):
        mine = mine + swap(mine, "dp", mask)
    return out_tokens, grad_tokens, (grad_in, grad_out) + split_small(mine[0], small)


def split_small(flat, small):
    result, at = [], 0
    for v in small:
        result.append(flat[at : at + v.size].reshape(v.shape))
        at += v.size
    return tuple(result)


def alone(tokens, cotangent, doc_starts, valid_len, weights, firsts, seconds):
    w_in, w_out = weights[:2]
    small = weights[2:]
    length = tokens.shape[1]
    hidden = tokens[0].astype(F32)
    upstream = cotangent[0].astype(F32)
    flat = jnp.concatenate([v.astype(BF16).reshape(-1) for v in small])
    every = lax.all_gather(flat, "fsdp", axis=0, tiled=False)
    full, at = [], 0
    for v in small:
        piece = every[:, at : at + v.size].astype(F32)
        at += v.size
        if v.ndim == 1:
            full.append(piece.reshape(1, -1))
        else:
            full.append(jnp.moveaxis(piece.reshape((-1,) + v.shape), 0, 1).reshape(v.shape[0], -1))
    norm_full, gate_full, convw_full, convb_full, shift_full, logd_full, skip_full = full
    in_full = lax.all_gather(
        lax.all_gather(w_in.astype(BF16), "dp", axis=1, tiled=True), "fsdp", axis=0, tiled=True
    )
    out_full = lax.all_gather(
        lax.all_gather(w_out.astype(BF16), "dp", axis=1, tiled=True), "fsdp", axis=0, tiled=True
    )
    scale = lax.rsqrt(jnp.mean(hidden * hidden, axis=-1, keepdims=True) + EPSILON)
    normed = (hidden * scale * norm_full).astype(BF16)
    projected = dot(normed, in_full)
    extra = projected[:, MAIN:]
    common = (
        projected[:, :MAIN], extra, extra[:, 2 * NS :].T, convw_full[:, :DI], convb_full[:, :DI],
        convw_full[:, DI:], convb_full[:, DI:], shift_full.T, logd_full.T, jnp.repeat(skip_full, HP, axis=1),
    )
    gated, y, states, squares = mix_forward(0, length, doc_starts, *common)
    q = lax.rsqrt(squares * (1.0 / DI) + EPSILON)
    mixed = (gated * q * gate_full).astype(BF16)
    live = (jnp.arange(length, dtype=jnp.int32) < valid_len[0]).astype(F32)[:, None]
    d_branch = (upstream * live).astype(BF16)
    out_tokens = (hidden + dot(mixed, out_full) * live).astype(BF16)
    d_mixed = dot_nt(d_branch, out_full)
    mean = q * q * jnp.sum(mixed.astype(F32) * d_mixed, axis=1, keepdims=True) * (1.0 / DI)
    d_main, d_bc_in, d_dt, *sums = mix_backward(
        0, 1, length, None, doc_starts, *common, gate_full, y, states, q, mean, d_mixed
    )
    s_gain, s_cw, s_cb, s_cwbc, s_cbbc, s_shift, s_logd, s_skip = [v[0] for v in sums]
    d_low = jnp.concatenate([d_main, d_bc_in, d_dt.T.astype(BF16)], axis=1)
    d_normed = dot_nt(d_low, in_full)
    weighted = norm_full * d_normed
    average = jnp.mean(hidden * weighted, axis=-1, keepdims=True)
    grad_tokens = upstream + scale * weighted - hidden * (scale * scale * scale * average)
    s_norm = jnp.sum(hidden * scale * d_normed, axis=0)
    contract = (((0,), (0,)), ((), ()))
    out_sum = lax.dot_general(mixed, d_branch, contract, preferred_element_type=F32).astype(BF16)
    in_sum = lax.dot_general(normed, d_low, contract, preferred_element_type=F32).astype(BF16)
    grads = []
    for total in (in_sum, out_sum):
        total = lax.psum_scatter(total, "fsdp", scatter_dimension=0, tiled=True)
        grads.append(lax.psum_scatter(total, "dp", scatter_dimension=1, tiled=True).astype(F32))
    sums = (
        s_norm[None],
        s_gain,
        jnp.concatenate([s_cw, s_cwbc], axis=1),
        jnp.concatenate([s_cb, s_cbbc], axis=1),
        s_shift.T,
        s_logd.T,
        s_skip.reshape(1, NH, HP).sum(axis=2),
    )
    parts = lax.axis_size("fsdp")
    flat = jnp.concatenate(
        [jnp.moveaxis(s.reshape(s.shape[0], parts, -1), 1, 0).reshape(parts, -1) for s in sums], axis=1
    )
    total = lax.psum(flat, ("dp", "fsdp"))
    mine = lax.dynamic_index_in_dim(total, lax.axis_index("fsdp"), 0, keepdims=False)
    return out_tokens, grad_tokens, tuple(grads) + split_small(mine, small)


def regular(w_in, dp, groups):
    zs = dp // 2
    if dp % 2 or zs & (zs - 1) or zs < 4 or groups & (groups - 1) or DI % (groups * groups * 128):
        return False
    local = DI // groups
    per_chip = 2 * w_in.shape[1]
    edges = [
        static_count(g, min(per_chip * zz, MAIN), local // groups, local) for zz in range(zs + 1) for g in range(groups)
    ]
    return local % BC == 0 and groups == 4 and zs == 4 and all(e % 16 == 0 for e in edges) and w_in.shape[0] % 256 == 0


def shards(tokens, cotangent, doc_starts, valid_len, *rest):
    weights, moments = rest[:9], rest[9:]
    firsts, seconds = moments[0::2], moments[1::2]
    dp, groups = lax.axis_size("dp"), lax.axis_size("fsdp")
    plan = grouped if regular(weights[0], dp, groups) else alone
    out_tokens, grad_tokens, grads = plan(tokens, cotangent, doc_starts, valid_len, weights, firsts, seconds)
    factor = 1.0 / math.sqrt(tokens.shape[0] * tokens.shape[1] * dp * groups)
    decay_flags = (True, True, False, False, True, True, False, False, False)
    results = []
    for i, (weight, gradient, first, second) in enumerate(zip(weights, grads, firsts, seconds)):
        direction, first_new, second_new = adam_direction(weight, gradient * factor, first, second, decay_flags[i])
        if i < 2:
            direction = weight - LEARN_RATE * direction
        results.extend((direction, first_new, second_new))
    return (out_tokens[None], grad_tokens[None]) + tuple(results)


def solution(mesh):
    rows3 = P(("dp", "fsdp"), None, None)
    both, split, last = P("fsdp", "dp"), P("fsdp"), P(None, "fsdp")
    small = (split, split, last, split, split, split, split)
    placed = (rows3, rows3, P(("dp", "fsdp"), None), P(("dp", "fsdp")), both, both) + small
    placed = placed + (both,) * 4 + tuple(s for s in small for _ in range(2))
    out = (rows3, rows3) + (both,) * 6 + tuple(s for s in small for _ in range(3))
    return jax.shard_map(shards, mesh=mesh, in_specs=placed, out_specs=out, check_vma=False)
```

```python
import functools
import math

import jax
import jax.numpy as jnp
from jax import lax
from jax.experimental import pallas as pl
from jax.experimental.layout import Layout, with_layout_constraint
from jax.experimental.pallas import tpu as pltpu
from jax.sharding import PartitionSpec as P

NH = 64
HP = 64
NS = 128
CONVW = 4
DI = 4096
CONV = 4352

EPSILON = 1e-05
BETA_ONE = 0.9
BETA_TWO = 0.95
ADAM_EPS = 1e-08
LEARN_RATE = 0.01
DECAY_RATE = 0.1
adam_step = 10
highest = lax.Precision.HIGHEST

Q = 128
BC = 512
HB = BC // HP
PAIRS = BC // 128
F32 = jnp.float32
BF16 = jnp.bfloat16


def dot(a, b):
    return jnp.dot(a, b, preferred_element_type=F32)


def dot_nt(a, b):
    return lax.dot_general(a, b, (((1,), (1,)), ((), ())), preferred_element_type=F32)


def sigmoid(v):
    return 1.0 / (1.0 + jnp.exp(-v))


def segment_of(starts_ref, position):
    row = pl.program_id(0)
    count = jnp.zeros_like(position)
    for k in range(starts_ref.shape[1]):
        count = count + (starts_ref[row, k] <= position).astype(jnp.int32)
    return count


def conv_forward(values, weights, bias, same_ref):
    total = values * weights[CONVW - 1 : CONVW] + bias
    for lag in range(1, CONVW):
        moved = pltpu.roll(values, lag, 0) * same_ref[lag - 1]
        total = total + moved * weights[CONVW - 1 - lag : CONVW - lag]
    return total


def conv_backward(d_conv, values, weights, same_ref):
    length = values.shape[0]
    d_in = d_conv * weights[CONVW - 1 : CONVW]
    sums = [jnp.sum(d_conv * values, axis=0, keepdims=True)]
    for lag in range(1, CONVW):
        masked = d_conv * same_ref[lag - 1]
        sums.append(jnp.sum(masked * pltpu.roll(values, lag, 0), axis=0, keepdims=True))
        d_in = d_in + pltpu.roll(masked, length - lag, 0) * weights[CONVW - 1 - lag : CONVW - lag]
    return d_in, jnp.concatenate(sums[::-1], axis=0), jnp.sum(d_conv, axis=0, keepdims=True)


def prepare_masks(starts_ref, length, same_ref, enter_ref, last_ref):
    col = lax.broadcasted_iota(jnp.int32, (length, 128), 0)
    seg = segment_of(starts_ref, col)
    for lag in range(1, CONVW):
        same_ref[lag - 1] = (segment_of(starts_ref, col - lag) == seg).astype(F32)
    begin = col - lax.rem(col, Q)
    enter_ref[...] = ((segment_of(starts_ref, begin - 1) == seg) & (begin > 0)).astype(F32)
    last_ref[...] = (segment_of(starts_ref, begin + (Q - 1)) == seg).astype(F32)


def keep_mask(starts_ref, chunk):
    rows = lax.broadcasted_iota(jnp.int32, (Q, Q), 0) + chunk * Q
    cols = lax.broadcasted_iota(jnp.int32, (Q, Q), 1) + chunk * Q
    return (rows >= cols) & (segment_of(starts_ref, rows) == segment_of(starts_ref, cols))


def step_rows(dt_ref, shift_ref, logd_ref):
    pre = dt_ref[...] + shift_ref[...]
    step = jnp.maximum(pre, 0.0) + jnp.log1p(jnp.exp(-jnp.abs(pre)))
    decay = jnp.exp(logd_ref[...])
    return pre, step, -step * decay, decay


def cumulate(rate, chunks):
    rows = lax.broadcasted_iota(jnp.int32, (Q, Q), 0)
    cols = lax.broadcasted_iota(jnp.int32, (Q, Q), 1)
    upper = (rows <= cols).astype(F32)
    parts = [
        jnp.dot(rate[:, c * Q : (c + 1) * Q], upper, precision=highest, preferred_element_type=F32)
        for c in range(chunks)
    ]
    return jnp.concatenate(parts, axis=1)


def halves(lo, pair):
    zero = jnp.zeros_like(pair)
    return jnp.concatenate([jnp.where(lo, pair, zero), jnp.where(lo, zero, pair)], axis=0)


def forward_kernel(
    starts_ref, gate_ref, xin_ref, bc_ref, dt_ref, cw_ref, cb_ref, cwbc_ref, cbbc_ref,
    shift_ref, logd_ref, skip_ref,
    gated_ref, y_ref, state_ref, total_ref,
    same_ref, enter_ref, last_ref, cmat_ref, bt_ref, score_ref, square_ref,
    x_ref, carry_ref, step_ref, cum_ref, cumt_ref, tailed_ref, decay_ref,
):
    j = pl.program_id(1)
    length = gate_ref.shape[0]
    chunks = length // Q
    lo = lax.broadcasted_iota(jnp.int32, (Q, 128), 1) < HP

    @pl.when(j == 0)
    def _():
        prepare_masks(starts_ref, length, same_ref, enter_ref, last_ref)
        square_ref[...] = jnp.zeros_like(square_ref)
        both = []
        for part in range(2):
            cols = slice(part * NS, (part + 1) * NS)
            conv = conv_forward(bc_ref[:, cols].astype(F32), cwbc_ref[:, cols], cbbc_ref[:, cols], same_ref)
            both.append(conv * sigmoid(conv))
        bmat, cmat = both
        cmat_ref[...] = cmat.astype(BF16)
        bt = bmat.T
        bt_ref[...] = bt.astype(BF16)
        for c in range(chunks):
            rows = slice(c * Q, (c + 1) * Q)
            score = jnp.dot(cmat[rows].astype(BF16), bt[:, rows].astype(BF16), preferred_element_type=F32)
            score_ref[c] = jnp.where(keep_mask(starts_ref, c), score, 0.0)

    _, step, rate, _ = step_rows(dt_ref, shift_ref, logd_ref)
    cum = cumulate(rate, chunks)
    cumt_ref[...] = cum
    cum_ref[...] = cum.T
    step_ref[...] = step.T
    carry_ref[...] = jnp.zeros_like(carry_ref)
    for p in range(PAIRS):
        cols = slice(p * 128, (p + 1) * 128)
        conv = conv_forward(xin_ref[:, cols].astype(F32), cw_ref[:, cols], cb_ref[:, cols], same_ref)
        x_ref[:, cols] = conv * sigmoid(conv)
    for c in range(chunks):
        rows = slice(c * Q, (c + 1) * Q)
        entering_state = carry_ref[...].astype(BF16)
        state_ref[0, c] = entering_state
        if c > 0:
            outside = dot(cmat_ref[rows, :], entering_state)
        score = score_ref[c]
        for p in range(PAIRS):
            cols = slice(p * 128, (p + 1) * 128)
            cum_a = jnp.broadcast_to(cum_ref[rows, 2 * p : 2 * p + 1], (Q, Q))
            cum_b = jnp.broadcast_to(cum_ref[rows, 2 * p + 1 : 2 * p + 2], (Q, Q))
            low_a = (score * jnp.exp(jnp.minimum(cum_a - cumt_ref[2 * p : 2 * p + 1, rows], 0.0))).astype(BF16)
            low_b = (score * jnp.exp(jnp.minimum(cum_b - cumt_ref[2 * p + 1 : 2 * p + 2, rows], 0.0))).astype(BF16)
            cum_x = jnp.where(lo, cum_a, cum_b)
            step_x = jnp.where(lo, step_ref[rows, 2 * p : 2 * p + 1], step_ref[rows, 2 * p + 1 : 2 * p + 2])
            x = x_ref[rows, cols]
            xs = (x * step_x).astype(BF16)
            y = dot(jnp.concatenate([low_a, low_b], axis=1), halves(lo, xs))
            reach = jnp.exp(cum_x) * enter_ref[rows]
            if c > 0:
                y = y + reach * outside[:, cols]
            if c < chunks - 1:
                tail = jnp.exp(cum_x[Q - 1 : Q] - cum_x) * last_ref[rows]
                tailed_ref[:, cols] = (xs.astype(F32) * tail).astype(BF16)
                decay_ref[0:1, cols] = reach[Q - 1 : Q]
            y_ref[rows, cols] = y
            gate = gate_ref[rows, cols].astype(F32)
            gated = (y + skip_ref[:, cols] * x) * (gate * sigmoid(gate))
            square_ref[rows, :] += gated * gated
            gated_ref[rows, cols] = gated
        if c < chunks - 1:
            carry_ref[...] = decay_ref[0:1, :] * carry_ref[...] + dot(bt_ref[:, rows], tailed_ref[...])

    @pl.when(j == pl.num_programs(1) - 1)
    def _():
        total_ref[...] = jnp.sum(square_ref[...], axis=1, keepdims=True)


def backward_body(
    starts_ref, gate_ref, xin_ref, bc_ref, dt_ref, cw_ref, cb_ref, cwbc_ref, cbbc_ref,
    shift_ref, logd_ref, skip_ref, gain_ref, y_ref, state_ref, q_ref, mean_ref, dm_ref,
    before_ref, dgate_ref, dbc_ref, ddt_ref, sgain_ref, scw_ref, scb_ref, scwbc_ref, scbbc_ref,
    sshift_ref, slogd_ref, sskip_ref,
    same_ref, enter_ref, last_ref, bmat_ref, cmat_ref, ct_ref, score_ref, scoret_ref,
    x_ref, slope_ref, dy_ref, dxs_ref, carry_ref, step_ref, cum_ref, cumt_ref,
    dscore_ref, db_ref, dc_ref, v1_ref, v2_ref, v3_ref, v4_ref, tailed_ref, reached_ref, decay_ref, held_ref,
):
    j = pl.program_id(2)
    length = gate_ref.shape[0]
    chunks = length // Q
    lo = lax.broadcasted_iota(jnp.int32, (Q, 128), 1) < HP

    def activate_bc(part):
        cols = slice(part * NS, (part + 1) * NS)
        return conv_forward(bc_ref[:, cols].astype(F32), cwbc_ref[:, cols], cbbc_ref[:, cols], same_ref)

    @pl.when(j == 0)
    def _():
        prepare_masks(starts_ref, length, same_ref, enter_ref, last_ref)
        both = []
        for part in range(2):
            conv = activate_bc(part)
            both.append(conv * sigmoid(conv))
        bmat, cmat = both
        bmat_ref[...] = bmat.astype(BF16)
        cmat_ref[...] = cmat.astype(BF16)
        bt = bmat.T
        ct_ref[...] = cmat.T.astype(BF16)
        for c in range(chunks):
            rows = slice(c * Q, (c + 1) * Q)
            score = jnp.dot(cmat[rows].astype(BF16), bt[:, rows].astype(BF16), preferred_element_type=F32)
            score = jnp.where(keep_mask(starts_ref, c), score, 0.0)
            score_ref[c] = score
            scoret_ref[c] = score.T
        dscore_ref[...] = jnp.zeros_like(dscore_ref)
        db_ref[...] = jnp.zeros_like(db_ref)
        dc_ref[...] = jnp.zeros_like(dc_ref)

    pre, step, rate, decay = step_rows(dt_ref, shift_ref, logd_ref)
    cum = cumulate(rate, chunks)
    cumt_ref[...] = cum
    cum_ref[...] = cum.T
    step_ref[...] = step.T
    carry_ref[...] = jnp.zeros_like(carry_ref)
    q = q_ref[...]
    mean = mean_ref[...]
    for p in range(PAIRS):
        cols = slice(p * 128, (p + 1) * 128)
        conv = conv_forward(xin_ref[:, cols].astype(F32), cw_ref[:, cols], cb_ref[:, cols], same_ref)
        sig = sigmoid(conv)
        x = conv * sig
        x_ref[:, cols] = x
        slope_ref[:, cols] = sig * (1.0 + conv - x)
        gate = gate_ref[:, cols].astype(F32)
        gsig = sigmoid(gate)
        silu = gate * gsig
        scanned = y_ref[:, cols] + skip_ref[:, cols] * x
        gated = scanned * silu
        scaled = dm_ref[:, cols].astype(F32) * q
        sgain_ref[0, :, cols] = jnp.sum(gated * scaled, axis=0, keepdims=True)
        d_gated = scaled * gain_ref[:, cols] - gated * mean
        dgate_ref[:, cols] = (d_gated * scanned * (gsig * (1.0 + gate - silu))).astype(dgate_ref.dtype)
        d_scanned = d_gated * silu
        dy_ref[:, cols] = d_scanned
        sskip_ref[0, :, cols] = jnp.sum(d_scanned * x, axis=0, keepdims=True)

    for c in reversed(range(chunks)):
        rows = slice(c * Q, (c + 1) * Q)
        score = score_ref[c]
        scoret = scoret_ref[c]
        d_state = carry_ref[...]
        d_state_low = d_state.astype(BF16)
        if c < chunks - 1:
            from_state = dot(bmat_ref[rows, :], d_state_low)
        d_score = dscore_ref[c]
        for p in range(PAIRS):
            cols = slice(p * 128, (p + 1) * 128)
            cum_a = jnp.broadcast_to(cum_ref[rows, 2 * p : 2 * p + 1], (Q, Q))
            cum_b = jnp.broadcast_to(cum_ref[rows, 2 * p + 1 : 2 * p + 2], (Q, Q))
            row_a = cumt_ref[2 * p : 2 * p + 1, rows]
            row_b = cumt_ref[2 * p + 1 : 2 * p + 2, rows]
            cum_x = jnp.where(lo, cum_a, cum_b)
            step_x = jnp.where(lo, step_ref[rows, 2 * p : 2 * p + 1], step_ref[rows, 2 * p + 1 : 2 * p + 2])
            x = x_ref[rows, cols]
            xs = (x * step_x).astype(BF16)
            xs_wide = xs.astype(F32)
            d_y = dy_ref[rows, cols]
            d_y_low = d_y.astype(BF16)
            pair = dot_nt(d_y_low, halves(lo, xs))
            d_score = d_score + pair[:, :Q] * jnp.exp(jnp.minimum(cum_a - row_a, 0.0))
            d_score = d_score + pair[:, Q:] * jnp.exp(jnp.minimum(cum_b - row_b, 0.0))
            up_a = (scoret * jnp.exp(jnp.minimum(row_a - cum_a, 0.0))).astype(BF16)
            up_b = (scoret * jnp.exp(jnp.minimum(row_b - cum_b, 0.0))).astype(BF16)
            d_xs = dot(jnp.concatenate([up_a, up_b], axis=1), halves(lo, d_y_low))
            v1_ref[rows, cols] = d_y_low.astype(F32) * y_ref[rows, cols] - xs_wide * d_xs
            reach = jnp.exp(cum_x) * enter_ref[rows]
            if c < chunks - 1:
                tail = jnp.exp(cum_x[Q - 1 : Q] - cum_x) * last_ref[rows]
                d_tail = tail * from_state[:, cols]
                v3_ref[rows, cols] = xs_wide * d_tail
                d_xs = d_xs + d_tail
                tailed_ref[:, cols] = (xs_wide * tail).astype(BF16)
                entered = state_ref[0, c, :, cols]
                v4_ref[c : c + 1, cols] = reach[Q - 1 : Q] * jnp.sum(
                    d_state[:, cols] * entered.astype(F32), axis=0, keepdims=True
                )
            else:
                v3_ref[rows, cols] = jnp.zeros((Q, 128), F32)
                v4_ref[c : c + 1, cols] = jnp.zeros((1, 128), F32)
            if c > 0:
                reached_ref[:, cols] = (reach * d_y).astype(BF16)
                decay_ref[0:1, cols] = reach[Q - 1 : Q]
            v2_ref[rows, cols] = x * d_xs
            dxs_ref[rows, cols] = step_x * d_xs + skip_ref[:, cols] * d_y
        dscore_ref[c] = d_score
        if c < chunks - 1:
            db_ref[rows, :] += dot_nt(tailed_ref[...], d_state_low)
        if c > 0:
            reached = reached_ref[...]
            dc_ref[rows, :] += dot_nt(reached, state_ref[0, c])
            carry_ref[...] = decay_ref[0:1, :] * d_state + dot(ct_ref[:, rows], reached)

    head = lax.broadcasted_iota(jnp.int32, (HB, BC), 0)
    lane = lax.broadcasted_iota(jnp.int32, (HB, BC), 1)
    pick = ((lane >= head * HP) & (lane < (head + 1) * HP)).astype(BF16)

    def by_head(values):
        high = values.astype(BF16)
        rest = (values - high.astype(F32)).astype(BF16)
        return dot_nt(pick, high) + dot_nt(pick, rest)

    h1 = by_head(v1_ref[...])
    h2 = by_head(v2_ref[...])
    h3 = by_head(v3_ref[...])
    h4 = by_head(v4_ref[...])
    rows_i = lax.broadcasted_iota(jnp.int32, (Q, Q), 0)
    cols_i = lax.broadcasted_iota(jnp.int32, (Q, Q), 1)
    suffix = (rows_i >= cols_i).astype(F32)
    prefix = (rows_i < cols_i).astype(F32)
    parts = []
    for c in range(chunks):
        rows = slice(c * Q, (c + 1) * Q)
        parts.append(
            jnp.dot(h1[:, rows], suffix, precision=highest, preferred_element_type=F32)
            + jnp.dot(h3[:, rows], prefix, precision=highest, preferred_element_type=F32)
            + h4[:, c : c + 1]
        )
    d_rate = jnp.concatenate(parts, axis=1)
    d_step = h2 - d_rate * decay
    d_raw = d_step * sigmoid(pre)
    ddt_ref[...] = d_raw
    sshift_ref[0] = jnp.sum(d_raw, axis=1, keepdims=True)
    slogd_ref[0] = jnp.sum(d_rate * rate, axis=1, keepdims=True)

    for p in range(PAIRS):
        cols = slice(p * 128, (p + 1) * 128)
        d_conv = dxs_ref[:, cols] * slope_ref[:, cols]
        d_in, s_w, s_b = conv_backward(d_conv, xin_ref[:, cols].astype(F32), cw_ref[:, cols], same_ref)
        held_ref[j, :, cols] = d_in.astype(BF16)
        scw_ref[0, :, cols] = s_w
        scb_ref[0, :, cols] = s_b

    @pl.when(j == pl.num_programs(2) - 1)
    def _():
        for c in range(chunks):
            rows = slice(c * Q, (c + 1) * Q)
            masked = jnp.where(keep_mask(starts_ref, c), dscore_ref[c], 0.0)
            dc_ref[rows, :] += dot(masked.astype(BF16), bmat_ref[rows, :])
            db_ref[rows, :] += dot(masked.T.astype(BF16), cmat_ref[rows, :])
        for part, grad_ref in ((0, db_ref), (1, dc_ref)):
            cols = slice(part * NS, (part + 1) * NS)
            conv = activate_bc(part)
            sig = sigmoid(conv)
            d_conv = grad_ref[...] * (sig * (1.0 + conv - conv * sig))
            d_in, s_w, s_b = conv_backward(d_conv, bc_ref[:, cols].astype(F32), cwbc_ref[:, cols], same_ref)
            dbc_ref[:, cols] = d_in.astype(dbc_ref.dtype)
            scwbc_ref[0, :, cols] = s_w
            scbbc_ref[0, :, cols] = s_b


def backward_kernel(*refs):
    outputs_at = 18

    @pl.when(pl.program_id(1) == 0)
    def _():
        backward_body(*refs)

    @pl.when(pl.program_id(1) == 1)
    def _():
        refs[outputs_at + 1][...] = refs[-1][pl.program_id(2)]


def backward_first(*refs):
    backward_kernel(*refs[:18], None, *refs[18:])


def forward_index(first, rows):
    return lambda r, j: (first + r, r, j)


def backward_index(first, rows):
    def index(r, s, j):
        r = jnp.minimum(r + s, rows - 1)
        return first + r, r, j * (1 - s)

    return index


def common_specs(index, length, channels):
    def at(shape, where):
        return pl.BlockSpec(shape, lambda *g: where(*index(*g)))

    blocks = channels // BC
    heads = at((HB, 1), lambda a, r, j: (j, 0))
    return at, [
        pl.BlockSpec(memory_space=pltpu.SMEM),
        at((length, BC), lambda a, r, j: (a, j)),
        at((length, BC), lambda a, r, j: (a, j + blocks)),
        at((length, 2 * NS), lambda a, r, j: (a, 0)),
        at((HB, length), lambda a, r, j: (j, a)),
        at((CONVW, BC), lambda a, r, j: (0, j)),
        at((1, BC), lambda a, r, j: (0, j)),
        at((CONVW, 2 * NS), lambda a, r, j: (0, 0)),
        at((1, 2 * NS), lambda a, r, j: (0, 0)),
        heads,
        heads,
        at((1, BC), lambda a, r, j: (0, j)),
    ]


def row_cost(size, weight):
    return pl.CostEstimate(flops=1000 * weight * size, bytes_accessed=12 * size, transcendentals=0)


def mix_forward(first, length, starts, main, extra, dt_rows, conv_w, conv_b, cw_bc, cb_bc, shift, logd, skip_cols):
    rows = starts.shape[0]
    channels = main.shape[1] // 2
    chunks = length // Q
    vmem = pltpu.VMEM
    _, in_specs = common_specs(forward_index(first, rows), length, channels)
    return pl.pallas_call(
        forward_kernel,
        grid=(rows, channels // BC),
        in_specs=in_specs,
        out_specs=[
            pl.BlockSpec((length, BC), lambda r, j: (r, j)),
            pl.BlockSpec((length, BC), lambda r, j: (r, j)),
            pl.BlockSpec((1, chunks, NS, BC), lambda r, j: (r, 0, 0, j)),
            pl.BlockSpec((length, 1), lambda r, j: (r, 0)),
        ],
        out_shape=[
            jax.ShapeDtypeStruct((rows * length, channels), F32),
            jax.ShapeDtypeStruct((rows * length, channels), F32),
            jax.ShapeDtypeStruct((rows, chunks, NS, channels), BF16),
            jax.ShapeDtypeStruct((rows * length, 1), F32),
        ],
        scratch_shapes=[
            vmem((CONVW - 1, length, 128), F32),
            vmem((length, 128), F32),
            vmem((length, 128), F32),
            vmem((length, NS), BF16),
            vmem((NS, length), BF16),
            vmem((chunks, Q, Q), F32),
            vmem((length, 128), F32),
            vmem((length, BC), F32),
            vmem((NS, BC), F32),
            vmem((length, HB), F32),
            vmem((length, HB), F32),
            vmem((HB, length), F32),
            vmem((Q, BC), BF16),
            vmem((8, BC), F32),
        ],
        compiler_params=pltpu.CompilerParams(vmem_limit_bytes=48 * 1024 * 1024),
        cost_estimate=row_cost(rows * length * channels, 18),
        name="mix_forward",
    )(starts, main, main, extra, dt_rows, conv_w, conv_b, cw_bc, cb_bc, shift, logd, skip_cols)


def mix_backward(
    first, total, length, before, starts, main, extra, dt_rows, conv_w, conv_b, cw_bc, cb_bc, shift, logd, skip_cols,
    gain, y, states, q, mean, d_mixed,
):
    rows = starts.shape[0]
    channels = main.shape[1] // 2
    heads = channels // HP
    blocks = channels // BC
    chunks = length // Q
    vmem = pltpu.VMEM
    at, in_specs = common_specs(backward_index(first, rows), length, channels)
    col = at((length, 1), lambda a, r, j: (a, 0))

    def result(shape, where):
        return pl.BlockSpec(shape, lambda r, s, j: where(r, jnp.maximum(j, s * (blocks - 1))))

    def row_sums(count):
        return result((1, count, BC), lambda r, j: (r, 0, j))

    per_head = result((1, HB, 1), lambda r, j: (r, j, 0))
    shape = jax.ShapeDtypeStruct
    operands = (
        starts, main, main, extra, dt_rows, conv_w, conv_b, cw_bc, cb_bc, shift, logd, skip_cols,
        gain, y, states, q, mean, d_mixed,
    )
    in_specs = in_specs + [
        at((1, BC), lambda a, r, j: (0, j)),
        at((length, BC), lambda a, r, j: (r, j)),
        at((1, chunks, NS, BC), lambda a, r, j: (r, 0, 0, j)),
        col,
        col,
        at((length, BC), lambda a, r, j: (a, j)),
    ]
    aliases = {}
    if before is not None:
        aliases = {len(operands): 0}
        operands = operands + (before,)
        in_specs = in_specs + [pl.BlockSpec(memory_space=pl.ANY)]
    return pl.pallas_call(
        backward_first if before is None else backward_kernel,
        grid=(rows, 2, blocks),
        in_specs=in_specs,
        out_specs=[
            pl.BlockSpec((length, BC), lambda r, s, j: (first + r, j + blocks * s)),
            result((length, 2 * NS), lambda r, j: (r, 0)),
            result((HB, length), lambda r, j: (j, r)),
            row_sums(1),
            row_sums(CONVW),
            row_sums(1),
            result((1, CONVW, 2 * NS), lambda r, j: (r, 0, 0)),
            result((1, 1, 2 * NS), lambda r, j: (r, 0, 0)),
            per_head,
            per_head,
            row_sums(1),
        ],
        out_shape=[
            shape((total * length, 2 * channels), BF16),
            shape((rows * length, 2 * NS), BF16),
            shape((heads, rows * length), F32),
            shape((rows, 1, channels), F32),
            shape((rows, CONVW, channels), F32),
            shape((rows, 1, channels), F32),
            shape((rows, CONVW, 2 * NS), F32),
            shape((rows, 1, 2 * NS), F32),
            shape((rows, heads, 1), F32),
            shape((rows, heads, 1), F32),
            shape((rows, 1, channels), F32),
        ],
        scratch_shapes=[
            vmem((CONVW - 1, length, 128), F32),
            vmem((length, 128), F32),
            vmem((length, 128), F32),
            vmem((length, NS), BF16),
            vmem((length, NS), BF16),
            vmem((NS, length), BF16),
            vmem((chunks, Q, Q), F32),
            vmem((chunks, Q, Q), F32),
            vmem((length, BC), F32),
            vmem((length, BC), F32),
            vmem((length, BC), F32),
            vmem((length, BC), F32),
            vmem((NS, BC), F32),
            vmem((length, HB), F32),
            vmem((length, HB), F32),
            vmem((HB, length), F32),
            vmem((chunks, Q, Q), F32),
            vmem((length, NS), F32),
            vmem((length, NS), F32),
            vmem((length, BC), F32),
            vmem((length, BC), F32),
            vmem((length, BC), F32),
            vmem((8, BC), F32),
            vmem((Q, BC), BF16),
            vmem((Q, BC), BF16),
            vmem((8, BC), F32),
            vmem((blocks, length, BC), BF16),
        ],
        input_output_aliases=aliases,
        compiler_params=pltpu.CompilerParams(vmem_limit_bytes=48 * 1024 * 1024),
        cost_estimate=row_cost(rows * length * channels, 42),
        name="mix_backward",
    )(*operands)


MAIN = 2 * DI
EXTRA = 2 * NS + NH


def adam_direction(weight, gradient, first, second, decayed):
    first_new = BETA_ONE * first + (1.0 - BETA_ONE) * gradient
    second_new = BETA_TWO * second + (1.0 - BETA_TWO) * gradient * gradient
    first_hat = first_new / (1.0 - BETA_ONE**adam_step)
    second_hat = second_new / (1.0 - BETA_TWO**adam_step)
    direction = first_hat / (jnp.sqrt(second_hat) + ADAM_EPS)
    if decayed:
        direction = direction + DECAY_RATE * weight
    return (direction, first_new, second_new)


def swap(value, axis, mask):
    size = lax.axis_size(axis)
    return lax.ppermute(value, axis, [(i, i ^ mask) for i in range(size)])


def bits_of(size):
    return [1 << b for b in reversed(range(size.bit_length() - 1))]


def place(buffer, shape, block, at, items):
    arrays, copies, table = [], [], [at[0], at[1]]
    for array, lead, row, col, valid, cuts in items:
        if not any(array is a for a in arrays):
            arrays.append(array)
        source = [array is a for a in arrays].index(True)
        for start, end in zip(cuts[:-1], cuts[1:]):
            copies.append((source, lead, start, end - start))
            table.extend([row, col, valid])
    table = jnp.stack([jnp.asarray(v, jnp.int32) for v in table])
    operands = [table] + arrays + ([] if buffer is None else [buffer])

    def kernel(table_ref, *refs):
        out_ref = refs[-1]
        for i, (source, lead, start, size) in enumerate(copies):
            piece = refs[source]
            row = pl.multiple_of(table_ref[3 * i + 2] + start, 16)
            col = pl.multiple_of(table_ref[3 * i + 3], 128)

            @pl.when(table_ref[3 * i + 4] > start)
            def _():
                rows = pl.ds(start, size)
                value = piece[rows, :] if lead is None else piece[lead, rows, :]
                out_ref[pl.ds(row, size), pl.ds(col, value.shape[1])] = value

    def all_of(a):
        return pl.BlockSpec(a.shape, lambda i, t: (0,) * a.ndim)

    return pl.pallas_call(
        kernel,
        grid_spec=pltpu.PrefetchScalarGridSpec(
            num_scalar_prefetch=1,
            grid=(1,),
            in_specs=[all_of(a) for a in arrays] + ([] if buffer is None else [pl.BlockSpec(memory_space=pl.ANY)]),
            out_specs=pl.BlockSpec(block, lambda i, t: (t[0], t[1])),
        ),
        out_shape=jax.ShapeDtypeStruct(shape, BF16),
        input_output_aliases={} if buffer is None else {len(operands) - 1: 0},
        compiler_params=pltpu.CompilerParams(vmem_limit_bytes=60 * 1024 * 1024),
        name="place",
    )(*operands)


def place_blocks(buffer, shape, arrays, size, order, columns, first_rows, counts, cuts):
    width, steps = arrays[0].shape[2], len(columns)
    pieces = [(a, n) for a, array in enumerate(arrays) for n in range(array.shape[0])]
    table = [jnp.asarray(v, jnp.int32) for v in columns]
    for rel in order:
        table.extend([first_rows(rel), counts(rel)])
    operands = [jnp.stack(table)] + list(arrays) + ([] if buffer is None else [buffer])

    def kernel(table_ref, *refs):
        for i, (a, n) in enumerate(pieces):
            begin = pl.multiple_of(table_ref[steps + 2 * i], 16)
            for start, end in zip(cuts[:-1], cuts[1:]):

                @pl.when(table_ref[steps + 2 * i + 1] > start)
                def _():
                    refs[-1][pl.ds(pl.multiple_of(begin + start, 16), end - start), :] = refs[a][n, start:end, :]

    return pl.pallas_call(
        kernel,
        grid_spec=pltpu.PrefetchScalarGridSpec(
            num_scalar_prefetch=1,
            grid=(steps,),
            in_specs=[pl.BlockSpec((a.shape[0], size, width), lambda i, t: (0, i, 0)) for a in arrays]
            + ([] if buffer is None else [pl.BlockSpec(memory_space=pl.ANY)]),
            out_specs=pl.BlockSpec((shape[0], width), lambda i, t: (0, t[i])),
        ),
        out_shape=jax.ShapeDtypeStruct(shape, BF16),
        input_output_aliases={} if buffer is None else {len(operands) - 1: 0},
        compiler_params=pltpu.CompilerParams(vmem_limit_bytes=60 * 1024 * 1024),
        name="place_blocks",
    )(*operands)


def matmul(a, b, kind, out_dtype=BF16, scale=None, more=None):
    m = a.shape[1] if kind == "tn" else a.shape[0]
    k = a.shape[0] if kind == "tn" else a.shape[1]
    n = b.shape[0] if kind == "nt" else b.shape[1]
    tm, tn = min(m, 1024), min(n, 512)
    dims = {"nn": ((1,), (0,)), "nt": ((1,), (1,)), "tn": ((0,), (0,))}[kind]

    def kernel(*refs):
        first = refs[0][...]
        if scale is not None:
            first = first * refs[2][...]
        total = lax.dot_general(first, refs[1][...], (dims, ((), ())), preferred_element_type=F32)
        if more is not None:
            total = total + dot(refs[2][...], refs[3][...])
        refs[-1][...] = total.astype(out_dtype)

    in_specs = [
        pl.BlockSpec((k, tm), lambda i, j: (0, i)) if kind == "tn" else pl.BlockSpec((tm, k), lambda i, j: (i, 0)),
        pl.BlockSpec((tn, k), lambda i, j: (j, 0)) if kind == "nt" else pl.BlockSpec((k, tn), lambda i, j: (0, j)),
    ]
    operands = [a, b]
    if more is not None:
        inner = more[0].shape[1]
        in_specs += [pl.BlockSpec((tm, inner), lambda i, j: (i, 0)), pl.BlockSpec((inner, tn), lambda i, j: (0, j))]
        operands += list(more)
    if scale is not None:
        in_specs.append(pl.BlockSpec((k, 1), lambda i, j: (0, 0)))
        operands.append(scale)
    return pl.pallas_call(
        kernel,
        grid=(m // tm, n // tn),
        in_specs=in_specs,
        out_specs=pl.BlockSpec((tm, tn), lambda i, j: (i, j)),
        out_shape=jax.ShapeDtypeStruct((m, n), out_dtype),
        compiler_params=pltpu.CompilerParams(vmem_limit_bytes=56 * 1024 * 1024),
        cost_estimate=pl.CostEstimate(flops=2 * m * n * k, bytes_accessed=2 * (m * k + n * k + m * n), transcendentals=0),
        name="matmul_" + kind,
    )(*operands)


def matmul_blocks(a, b, size, chosen):
    k, m = a.shape
    tm, count = min(m, 2048), len(chosen) // 2

    def kernel(chosen_ref, a_ref, b_ref, first_ref, second_ref):
        total = lax.dot_general(a_ref[...], b_ref[...], (((0,), (0,)), ((), ())), preferred_element_type=F32)

        @pl.when(pl.program_id(1) < count)
        def _():
            first_ref[...] = total.astype(BF16)

        @pl.when(pl.program_id(1) >= count)
        def _():
            second_ref[...] = total.astype(BF16)

    return pl.pallas_call(
        kernel,
        grid_spec=pltpu.PrefetchScalarGridSpec(
            num_scalar_prefetch=1,
            grid=(m // tm, 2 * count),
            in_specs=[
                pl.BlockSpec((k, tm), lambda i, j, t: (0, i)),
                pl.BlockSpec((k, size), lambda i, j, t: (0, t[j])),
            ],
            out_specs=[
                pl.BlockSpec((tm, size), lambda i, j, t: (i, jnp.minimum(j, count - 1))),
                pl.BlockSpec((tm, size), lambda i, j, t: (i, jnp.maximum(j - count, 0))),
            ],
        ),
        out_shape=[jax.ShapeDtypeStruct((m, size * count), BF16)] * 2,
        compiler_params=pltpu.CompilerParams(vmem_limit_bytes=56 * 1024 * 1024),
        name="matmul_blocks",
    )(jnp.stack([jnp.asarray(v, jnp.int32) for v in chosen]), a, b)


def mixed_gradient(upstream, weights, live, mixed):
    rows, width = upstream.shape
    local = weights.shape[0]
    tm, tn = min(rows, 1024), min(local, 512)

    def kernel(up_ref, w_ref, live_ref, mixed_ref, out_ref, inner_ref):
        total = (dot_nt(up_ref[...], w_ref[...]) * live_ref[...]).astype(BF16)
        out_ref[...] = total
        part = jnp.sum(total.astype(F32) * mixed_ref[...].astype(F32), axis=1, keepdims=True)

        @pl.when(pl.program_id(1) == 0)
        def _():
            inner_ref[...] = part

        @pl.when(pl.program_id(1) > 0)
        def _():
            inner_ref[...] += part

    return pl.pallas_call(
        kernel,
        grid=(rows // tm, local // tn),
        in_specs=[
            pl.BlockSpec((tm, width), lambda i, j: (i, 0)),
            pl.BlockSpec((tn, width), lambda i, j: (j, 0)),
            pl.BlockSpec((tm, 1), lambda i, j: (i, 0)),
            pl.BlockSpec((tm, tn), lambda i, j: (i, j)),
        ],
        out_specs=[pl.BlockSpec((tm, tn), lambda i, j: (i, j)), pl.BlockSpec((tm, 1), lambda i, j: (i, 0))],
        out_shape=[jax.ShapeDtypeStruct((rows, local), BF16), jax.ShapeDtypeStruct((rows, 1), F32)],
        compiler_params=pltpu.CompilerParams(vmem_limit_bytes=56 * 1024 * 1024),
        name="mixed_gradient",
    )(upstream, weights, live, mixed)


def rows_into(buffer, row, rows, length, pieces, gain=None):
    tile = 256
    counts = [p.shape[0] // tile for p in pieces]
    starts = [sum(counts[:i]) for i in range(len(counts) + 1)]
    width = pieces[0].shape[1]
    operands = list(pieces) + ([] if gain is None else [gain]) + ([] if buffer is None else [buffer])

    def kernel(*refs):
        step = pl.program_id(0)
        for i in range(len(pieces)):

            @pl.when((step >= starts[i]) & (step < starts[i + 1]))
            def _():
                value = refs[i][...]
                if gain is not None:
                    value = value.astype(F32)
                    mean = jnp.mean(value * value, axis=1, keepdims=True)
                    value = (value * lax.rsqrt(mean + EPSILON) * refs[len(pieces)][...]).astype(BF16)
                refs[-1][...] = value

    def piece_spec(i):
        return pl.BlockSpec((tile, width), lambda s: (jnp.clip(s - starts[i], 0, counts[i] - 1), 0))

    specs = [piece_spec(i) for i in range(len(pieces))]
    if gain is not None:
        specs.append(pl.BlockSpec(gain.shape, lambda s: (0, 0)))
    if buffer is not None:
        specs.append(pl.BlockSpec(memory_space=pl.ANY))
    return pl.pallas_call(
        kernel,
        grid=(starts[-1],),
        in_specs=specs,
        out_specs=pl.BlockSpec((tile, width), lambda s: (row * length // tile + s, 0)),
        out_shape=jax.ShapeDtypeStruct((rows * length, width), BF16),
        input_output_aliases={} if buffer is None else {len(operands) - 1: 0},
        compiler_params=pltpu.CompilerParams(vmem_limit_bytes=60 * 1024 * 1024),
        name="rows_into",
    )(*operands)


def prefix_count(g, n, unit, period):
    return (n // period) * unit + jnp.clip(n % period - g * unit, 0, unit)


def static_count(g, n, unit, period):
    return (n // period) * unit + min(max(n % period - g * unit, 0), unit)


def together(*values):
    return lax.optimization_barrier(values)


def then(value, *earlier):
    return lax.optimization_barrier((value,) + earlier)[0]


def spread_z(bundle, masks, late=()):
    have, order = bundle[None], [0]
    for i, mask in enumerate(masks):
        if i > 0:
            have = then(have, *late)
        have = jnp.concatenate([have, swap(have, "dp", 2 * mask)])
        order = order + [rel ^ mask for rel in order]
    return have, order


def grouped(tokens, cotangent, doc_starts, valid_len, weights, firsts, seconds):
    w_in, w_out, norm_gain, gate_gain, conv_w, conv_b, dt_bias, a_log, d_skip = weights
    small = weights[2:]
    dp, groups = lax.axis_size("dp"), lax.axis_size("fsdp")
    zs = dp // 2
    d, f = lax.axis_index("dp"), lax.axis_index("fsdp")
    z, c = d // 2, d % 2
    z_masks = bits_of(zs)
    length, width = tokens.shape[1], tokens.shape[2]
    local = DI // groups
    unit = local // groups
    k_rows, per_dev = w_in.shape
    k_half = k_rows // 2
    per_chip = 2 * per_dev
    out_cols = w_out.shape[1]
    sizes = {
        (zz, g): static_count(g, min(per_chip * (zz + 1), MAIN), unit, local)
        - static_count(g, min(per_chip * zz, MAIN), unit, local)
        for zz in range(zs)
        for g in range(groups)
    }
    cuts = [0] + sorted(set(sizes.values()) - {0})
    most = cuts[-1]

    def first_row(zz):
        return prefix_count(f, jnp.minimum(per_chip * zz, MAIN), unit, local)

    def rows_valid(zz):
        return first_row(zz + 1) - first_row(zz)

    def slice_row(row):
        return jnp.minimum(row, 2 * local - most)

    low = w_in.astype(BF16)
    mine = lax.dynamic_slice_in_dim(low, k_half * c, k_half, 0)
    other = swap(lax.dynamic_slice_in_dim(low, k_half * (1 - c), k_half, 0), "dp", 1)
    chip = jnp.concatenate([jnp.where(c == 0, mine, other), jnp.where(c == 0, other, mine)], axis=1)
    column = per_chip * z + jnp.arange(per_chip, dtype=jnp.int32)
    owner = (column // unit) % groups
    begin = prefix_count(owner, per_chip * z, unit, local)
    rank = prefix_count(owner, column, unit, local) - begin
    moved = begin - slice_row(begin)
    extra_key = groups * most + column - MAIN
    places = jnp.arange(groups * most + EXTRA, dtype=jnp.int32)[:, None]

    def picks(ranks):
        key = jnp.where(column < MAIN, (owner ^ f) * most + ranks, extra_key)
        return (places == key[None, :]).astype(BF16)

    parts = dot_nt(picks(rank), chip).astype(BF16)

    def own_channels(v):
        v = v.reshape(v.shape[0], groups, groups, -1)
        return lax.dynamic_index_in_dim(v, f, 2, keepdims=False).reshape(v.shape[0], -1)

    out_low = w_out.astype(BF16).reshape(groups, unit, out_cols)
    out_blocks = [lax.dynamic_index_in_dim(out_low, f ^ m, 0, keepdims=False) for m in range(groups)]
    blocks = [parts[m * most : (m + 1) * most] for m in range(groups)]
    blocks = blocks[:1] + [swap(blocks[m], "fsdp", m) for m in range(1, groups)]
    first = jnp.concatenate([blocks[0], parts[groups * most :]])[None]
    marks = jnp.concatenate([doc_starts[0], valid_len])
    marks = jnp.concatenate([(marks // 32).astype(BF16), (marks % 32).astype(BF16)])
    flat = then(jnp.concatenate([marks] + [v.astype(BF16).reshape(-1) for v in small])[None], mine)
    rel_small = jnp.concatenate([flat] + [swap(flat, "fsdp", m) for m in range(1, groups)])
    order = jnp.arange(groups, dtype=jnp.int32) ^ f
    every = jnp.sum(
        jnp.where((order[None, :] == jnp.arange(groups)[:, None])[:, :, None], rel_small[None], 0), axis=1
    ).astype(F32)
    count = marks.shape[0] // 2
    marks = every[:, : 2 * count].astype(jnp.int32)
    marks = marks[:, :count] * 32 + marks[:, count:]
    every = every[:, 2 * count :]
    second = then(jnp.concatenate(blocks[1:])[None], rel_small)
    token_rows = lax.all_gather(tokens[0], "fsdp", axis=0, tiled=True)
    upstream_all = lax.all_gather(cotangent[0], "fsdp", axis=0, tiled=True)
    got = swap(first, "dp", 2 * z_masks[0])
    first_2 = jnp.concatenate([first, got])
    sent_a = then(first_2, second)
    sent_b = then(second, first_2)
    got_a = swap(sent_a, "dp", 2 * z_masks[1])
    got_b = swap(sent_b, "dp", 2 * z_masks[0])
    full, at = [], 0
    for v in small:
        piece = every[:, at : at + v.size]
        at += v.size
        if v.ndim == 1:
            full.append(piece.reshape(1, -1))
        else:
            full.append(jnp.moveaxis(piece.reshape((-1,) + v.shape), 0, 1).reshape(v.shape[0], -1))
    norm_full, gate_full, convw_full, convb_full, shift_full, logd_full, skip_full = full

    hidden = tokens[0].astype(F32)
    upstream = cotangent[0].astype(F32)
    live = (jnp.arange(length, dtype=jnp.int32) < valid_len[0]).astype(F32)[:, None]
    starts = marks[:, :-1]
    live_all = jnp.concatenate([(jnp.arange(length) < marks[r, -1]).astype(F32)[:, None] for r in range(groups)])

    out_blocks = [then(v, sent_b) for v in out_blocks]
    out_cat = jnp.stack(out_blocks[:1] + [swap(out_blocks[m], "fsdp", m) for m in range(1, groups)])
    out_cat = jnp.concatenate([lax.dynamic_index_in_dim(out_cat, f ^ m, 0, keepdims=False) for m in range(groups)])
    second_2, got_a, out_cat = together(jnp.concatenate([second, got_b]), got_a, out_cat)
    got_b2 = swap(second_2, "dp", 2 * z_masks[1])
    spread_a = jnp.concatenate([first_2, got_a])
    order_z = [0, z_masks[0]] + [z_masks[1], z_masks[0] ^ z_masks[1]]
    sibling_a = swap(then(spread_a, second_2), "dp", 1)
    sibling_b = swap(second_2, "dp", 1)
    extra_at = jnp.stack([jnp.int32(r) for r in order_z]) == (z ^ (zs - 1))
    extra_at = jnp.sum(jnp.where(extra_at, jnp.arange(zs, dtype=jnp.int32), 0))
    extra_own = lax.dynamic_index_in_dim(then(spread_a, second_2), extra_at, 0, keepdims=False)[most:]
    extra_got = jnp.stack([extra_own] + [swap(extra_own, "fsdp", m) for m in range(1, groups)])
    w_shape = (2 * local, width)

    def place_main(buffer, arrays, ms, rc):
        where = [2 * (f ^ m) + (c ^ rc) for m in ms]
        return place_blocks(
            buffer, w_shape, arrays, most, order_z, where, lambda r: first_row(z ^ r), lambda r: rows_valid(z ^ r), cuts
        )

    w_main = place_main(None, [spread_a], [0], 0)
    w_main = place_main(w_main, [sibling_a], [0], 1)
    normed_all = rows_into(None, 0, groups, length, [then(token_rows, w_main)], norm_full)
    extra_got = then(extra_got, w_main)
    extra_pair = [extra_got, swap(extra_got, "dp", 1)]
    extra_pair[1] = then(extra_pair[1], normed_all)
    extra_items = []
    for m in range(groups):
        for rc in range(2):
            extra_items.append((extra_pair[rc], m, 0, k_rows * (f ^ m) + k_half * (c ^ rc), EXTRA, (0, EXTRA)))
    w_extra = place(None, (EXTRA, width), (EXTRA, width), (0, 0), extra_items)
    w_dt = w_extra[2 * NS :].reshape(groups, groups, -1, width)
    w_dt = lax.dynamic_index_in_dim(w_dt, f, 1, keepdims=False).reshape(-1, width)
    w_own = jnp.concatenate([w_extra[: 2 * NS], w_dt, jnp.zeros((128 - w_dt.shape[0], width), BF16)])
    extra = matmul(normed_all, w_own, "nt", F32)
    dt_rows = extra[:, 2 * NS : 2 * NS + w_dt.shape[0]].T
    got_b2 = then(got_b2, normed_all, w_main, extra)
    sibling_b2 = swap(got_b2, "dp", 1)
    others = range(1, groups)
    w_main = place_main(w_main, [second_2, got_b2], others, 0)
    w_main = place_main(w_main, [sibling_b, sibling_b2], others, 1)
    out_1 = then(out_cat[None], got_b2)
    out_got = swap(out_1, "dp", 2 * z_masks[0])

    main = matmul(then(normed_all, extra), w_main, "nt", F32)
    common = (
        main, extra, dt_rows,
        own_channels(convw_full[:, :DI]), own_channels(convb_full[:, :DI]), convw_full[:, DI:], convb_full[:, DI:],
        own_channels(shift_full).T, own_channels(logd_full).T, own_channels(jnp.repeat(skip_full, HP, axis=1)),
    )
    half_rows = groups // 2
    out_2 = jnp.concatenate([out_1, then(out_got, main)])
    out_got = swap(out_2, "dp", 2 * z_masks[1])
    results = [mix_forward(0, length, then(starts[:half_rows], out_2), *common)]
    out_4 = jnp.concatenate([out_2, then(out_got, results[0][3])])
    out_sibling = swap(out_4, "dp", 1)
    results.append(mix_forward(half_rows, length, then(starts[half_rows:], out_4), *common))
    out_sibling = then(out_sibling, results[1][3])
    gated, y, states, squares = zip(*results)
    out_items = []
    for rc, array in enumerate((out_4, out_sibling)):
        for i, rel in enumerate(order_z):
            out_items.append((array, i, 0, out_cols * (2 * (z ^ rel) + (c ^ rc)), local, (0, local)))
    w_out_own = place(None, (local, width), (local, width), (0, 0), out_items)
    gain = own_channels(gate_full)

    def group_sum(v):
        return v, [swap(v, "fsdp", m) for m in range(1, groups)]

    def summed(parts, *late):
        v, got = parts
        for other in got:
            v = v + then(other, *late)
        return v

    squares = group_sum(jnp.concatenate(squares).reshape(groups, length))
    squares = summed(squares, w_out_own)
    q = lax.rsqrt(squares.reshape(-1, 1) * (1.0 / DI) + EPSILON)
    mixed = jnp.concatenate(
        [(g * q[i * half_rows * length : (i + 1) * half_rows * length] * gain).astype(BF16) for i, g in enumerate(gated)]
    )
    d_mixed, inner = mixed_gradient(upstream_all, w_out_own, live_all, mixed)
    inner = group_sum(inner.reshape(groups, length))
    out_full = matmul(then(mixed, inner[0]), upstream_all, "tn", scale=live_all.astype(BF16))
    branch = matmul(then(mixed, out_full), w_out_own, "nn")
    mean = q * q * summed(inner, out_full).reshape(-1, 1) * (1.0 / DI)

    def sum_low(a, b):
        return (a.astype(F32) + b.astype(F32)).astype(BF16)

    contract = (((0,), (0,)), ((), ()))


    out_own = lax.psum_scatter(out_full, "dp", scatter_dimension=1, tiled=True)
    d_mixed = then(d_mixed, branch)
    branch = lax.psum_scatter(branch, "fsdp", scatter_dimension=0, tiled=True)
    d_main, backs = None, []
    for i in range(2):
        begin = starts[i * half_rows : (i + 1) * half_rows]
        d_main, *result = mix_backward(
            i * half_rows, groups, length, d_main, begin, *common, gain, y[i], states[i], q, mean, d_mixed
        )
        backs.append(result)
    d_bc_in = jnp.concatenate([b[0] for b in backs])
    d_dt = jnp.concatenate([b[1] for b in backs], axis=1)
    sums = [jnp.concatenate(v) for v in list(zip(*backs))[2:]]
    here = (jnp.arange(groups, dtype=jnp.int32) == f).astype(F32)

    def all_channels(v):
        v = v.reshape(v.shape[0], groups, 1, -1)
        return (v * here[None, None, :, None]).reshape(v.shape[0], -1)

    d_extra = jnp.concatenate([d_bc_in, all_channels(d_dt.T).astype(BF16)], axis=1)

    bundles = [(groups - 2, groups - 1), (0, 1)]

    def bundle_columns(value, bundle, core):
        return [lax.dynamic_slice_in_dim(value, k_rows * (f ^ m) + k_half * core, k_half, 1) for m in bundle]

    def chip_blocks(bundle, got):
        size = 2 * k_half
        blocks = []
        for r in range(zs):
            row = slice_row(first_row(z ^ r))
            blocks.append(sum_low(*[lax.dynamic_slice(v, (row, bundle * size), (most, size)) for v in (main_sum, got)]))
        return blocks

    middle = width // 2
    order_m = bundles[0] + bundles[1]
    extra_sum = lax.dot_general(d_extra, normed_all, contract, preferred_element_type=F32).astype(BF16)
    extra_sum = with_layout_constraint(extra_sum, Layout((0, 1)))
    halves_e = [jnp.stack(bundle_columns(extra_sum, range(groups), core)) for core in (c, 1 - c)]
    extra_theirs = swap(halves_e[1], "dp", 1)
    partial = matmul(then(d_main, halves_e[1]), w_main, "nn", more=(d_extra, w_extra))
    partial, extra_theirs = together(partial, extra_theirs)
    d_normed = lax.psum_scatter(partial, "fsdp", scatter_dimension=0, tiled=True).astype(F32)
    both = halves_e[0].astype(F32) + extra_theirs.astype(F32)
    total, both_low = both[0], both.astype(BF16)
    arriving = [swap(both_low[m], "fsdp", m) for m in range(1, groups)]
    chosen = [2 * (f ^ m) + core for core in (1 - c, c) for m in order_m]
    sum_theirs, main_sum = matmul_blocks(then(d_main, both_low, branch), normed_all, k_half, chosen)
    sum_theirs, *arriving = together(sum_theirs, *arriving)
    got = swap(sum_theirs, "dp", 1)
    for other in arriving:
        total = total + other.astype(F32)
    total = total.astype(BF16)
    got, total = together(got, total)
    blocks_a, blocks_b = chip_blocks(0, got), chip_blocks(1, got)
    near, far = z_masks[-1], z_masks[0]
    sent_a = jnp.stack([blocks_a[near], blocks_a[near | far]])
    sent_b = jnp.stack([blocks_b[far], blocks_b[near | far]])
    got_a, got_b, got_e = together(
        swap(sent_a, "dp", 2 * near), swap(sent_b, "dp", 2 * far), swap(total, "dp", 2 * near)
    )
    total = sum_low(total, got_e)
    keep_a, sent_a = sum_low(blocks_a[0], got_a[0]), sum_low(blocks_a[far], got_a[1])
    keep_b, sent_b = sum_low(blocks_b[0], got_b[0]), sum_low(blocks_b[near], got_b[1])
    got_a, got_b, got_e = together(
        swap(sent_a, "dp", 2 * far), swap(sent_b, "dp", 2 * near), swap(total, "dp", 2 * far)
    )
    total = sum_low(total, got_e)
    done_a, done_b = sum_low(keep_a, got_a), sum_low(keep_b, got_b)
    recv = [None] * groups
    for block, bundle in ((done_a, bundles[0]), (done_b, bundles[1])):
        for i, m in enumerate(bundle):
            piece = block[:, i * k_half : (i + 1) * k_half]
            recv[m] = piece if m == 0 else swap(piece, "fsdp", m)
    recv = together(*recv)
    sent_b = recv[-1]

    hidden = then(tokens[0], sent_b).astype(F32)
    live = (jnp.arange(length, dtype=jnp.int32) < valid_len[0]).astype(F32)[:, None]
    scale = lax.rsqrt(jnp.mean(hidden * hidden, axis=-1, keepdims=True) + EPSILON)
    weighted = norm_full * d_normed
    average = jnp.mean(hidden * weighted, axis=-1, keepdims=True)
    grad_tokens = cotangent[0].astype(F32) + scale * weighted - hidden * (scale * scale * scale * average)
    s_norm = jnp.sum(hidden * scale * d_normed, axis=0)
    own = then(out_own, sent_b)
    out_rows = [lax.dynamic_slice_in_dim(own, unit * (f ^ m), unit, 0) for m in range(groups)]
    out_parts = jnp.stack(out_rows[:1] + [swap(out_rows[m], "fsdp", m) for m in range(1, groups)])
    s_gain, s_cw, s_cb, s_cwbc, s_cbbc, s_shift, s_logd, s_skip = [
        then(v, sent_b).sum(axis=0) for v in sums
    ]
    grad_out = jnp.concatenate(
        [lax.dynamic_index_in_dim(out_parts, f ^ g, 0, keepdims=False) for g in range(groups)]
    ).astype(F32)
    blocks = jnp.concatenate([*recv, total])
    grad_chip = lax.dot_general(blocks, picks(rank + moved), contract, preferred_element_type=F32).astype(BF16)
    left, right = grad_chip[:, :per_dev], grad_chip[:, per_dev:]
    own = jnp.where(c == 0, left, right)
    got = swap(jnp.where(c == 0, right, left), "dp", 1)
    grad_in = jnp.concatenate([jnp.where(c == 0, own, got), jnp.where(c == 0, got, own)]).astype(F32)

    out_tokens = (hidden + branch.astype(F32) * live).astype(BF16)

    small_sums = (
        s_norm[None],
        all_channels(s_gain),
        jnp.concatenate([all_channels(s_cw), s_cwbc], axis=1),
        jnp.concatenate([all_channels(s_cb), s_cbbc], axis=1),
        all_channels(s_shift.T),
        all_channels(s_logd.T),
        all_channels(s_skip.reshape(1, -1, HP).sum(axis=2)),
    )
    flat = jnp.concatenate(
        [jnp.moveaxis(s.reshape(s.shape[0], groups, -1), 1, 0).reshape(groups, -1) for s in small_sums], axis=1
    )
    mine = lax.dynamic_index_in_dim(flat, f, 0, keepdims=True)
    for m in range(1, groups):
        mine = mine + swap(lax.dynamic_index_in_dim(flat, f ^ m, 0, keepdims=True), "fsdp", m)
    for mask in bits_of(dp):
        mine = mine + swap(mine, "dp", mask)
    return out_tokens, grad_tokens, (grad_in, grad_out) + split_small(mine[0], small)


def split_small(flat, small):
    result, at = [], 0
    for v in small:
        result.append(flat[at : at + v.size].reshape(v.shape))
        at += v.size
    return tuple(result)


def alone(tokens, cotangent, doc_starts, valid_len, weights, firsts, seconds):
    w_in, w_out = weights[:2]
    small = weights[2:]
    length = tokens.shape[1]
    hidden = tokens[0].astype(F32)
    upstream = cotangent[0].astype(F32)
    flat = jnp.concatenate([v.astype(BF16).reshape(-1) for v in small])
    every = lax.all_gather(flat, "fsdp", axis=0, tiled=False)
    full, at = [], 0
    for v in small:
        piece = every[:, at : at + v.size].astype(F32)
        at += v.size
        if v.ndim == 1:
            full.append(piece.reshape(1, -1))
        else:
            full.append(jnp.moveaxis(piece.reshape((-1,) + v.shape), 0, 1).reshape(v.shape[0], -1))
    norm_full, gate_full, convw_full, convb_full, shift_full, logd_full, skip_full = full
    in_full = lax.all_gather(
        lax.all_gather(w_in.astype(BF16), "dp", axis=1, tiled=True), "fsdp", axis=0, tiled=True
    )
    out_full = lax.all_gather(
        lax.all_gather(w_out.astype(BF16), "dp", axis=1, tiled=True), "fsdp", axis=0, tiled=True
    )
    scale = lax.rsqrt(jnp.mean(hidden * hidden, axis=-1, keepdims=True) + EPSILON)
    normed = (hidden * scale * norm_full).astype(BF16)
    projected = dot(normed, in_full)
    extra = projected[:, MAIN:]
    common = (
        projected[:, :MAIN], extra, extra[:, 2 * NS :].T, convw_full[:, :DI], convb_full[:, :DI],
        convw_full[:, DI:], convb_full[:, DI:], shift_full.T, logd_full.T, jnp.repeat(skip_full, HP, axis=1),
    )
    gated, y, states, squares = mix_forward(0, length, doc_starts, *common)
    q = lax.rsqrt(squares * (1.0 / DI) + EPSILON)
    mixed = (gated * q * gate_full).astype(BF16)
    live = (jnp.arange(length, dtype=jnp.int32) < valid_len[0]).astype(F32)[:, None]
    d_branch = (upstream * live).astype(BF16)
    out_tokens = (hidden + dot(mixed, out_full) * live).astype(BF16)
    d_mixed = dot_nt(d_branch, out_full)
    mean = q * q * jnp.sum(mixed.astype(F32) * d_mixed, axis=1, keepdims=True) * (1.0 / DI)
    d_main, d_bc_in, d_dt, *sums = mix_backward(
        0, 1, length, None, doc_starts, *common, gate_full, y, states, q, mean, d_mixed
    )
    s_gain, s_cw, s_cb, s_cwbc, s_cbbc, s_shift, s_logd, s_skip = [v[0] for v in sums]
    d_low = jnp.concatenate([d_main, d_bc_in, d_dt.T.astype(BF16)], axis=1)
    d_normed = dot_nt(d_low, in_full)
    weighted = norm_full * d_normed
    average = jnp.mean(hidden * weighted, axis=-1, keepdims=True)
    grad_tokens = upstream + scale * weighted - hidden * (scale * scale * scale * average)
    s_norm = jnp.sum(hidden * scale * d_normed, axis=0)
    contract = (((0,), (0,)), ((), ()))
    out_sum = lax.dot_general(mixed, d_branch, contract, preferred_element_type=F32).astype(BF16)
    in_sum = lax.dot_general(normed, d_low, contract, preferred_element_type=F32).astype(BF16)
    grads = []
    for total in (in_sum, out_sum):
        total = lax.psum_scatter(total, "fsdp", scatter_dimension=0, tiled=True)
        grads.append(lax.psum_scatter(total, "dp", scatter_dimension=1, tiled=True).astype(F32))
    sums = (
        s_norm[None],
        s_gain,
        jnp.concatenate([s_cw, s_cwbc], axis=1),
        jnp.concatenate([s_cb, s_cbbc], axis=1),
        s_shift.T,
        s_logd.T,
        s_skip.reshape(1, NH, HP).sum(axis=2),
    )
    parts = lax.axis_size("fsdp")
    flat = jnp.concatenate(
        [jnp.moveaxis(s.reshape(s.shape[0], parts, -1), 1, 0).reshape(parts, -1) for s in sums], axis=1
    )
    total = lax.psum(flat, ("dp", "fsdp"))
    mine = lax.dynamic_index_in_dim(total, lax.axis_index("fsdp"), 0, keepdims=False)
    return out_tokens, grad_tokens, tuple(grads) + split_small(mine, small)


def regular(w_in, dp, groups):
    zs = dp // 2
    if dp % 2 or zs & (zs - 1) or zs < 4 or groups & (groups - 1) or DI % (groups * groups * 128):
        return False
    local = DI // groups
    per_chip = 2 * w_in.shape[1]
    edges = [
        static_count(g, min(per_chip * zz, MAIN), local // groups, local) for zz in range(zs + 1) for g in range(groups)
    ]
    return local % BC == 0 and groups == 4 and zs == 4 and all(e % 16 == 0 for e in edges) and w_in.shape[0] % 256 == 0


def shards(tokens, cotangent, doc_starts, valid_len, *rest):
    weights, moments = rest[:9], rest[9:]
    firsts, seconds = moments[0::2], moments[1::2]
    dp, groups = lax.axis_size("dp"), lax.axis_size("fsdp")
    plan = grouped if regular(weights[0], dp, groups) else alone
    out_tokens, grad_tokens, grads = plan(tokens, cotangent, doc_starts, valid_len, weights, firsts, seconds)
    factor = 1.0 / math.sqrt(tokens.shape[0] * tokens.shape[1] * dp * groups)
    decay_flags = (True, True, False, False, True, True, False, False, False)
    results = []
    for i, (weight, gradient, first, second) in enumerate(zip(weights, grads, firsts, seconds)):
        direction, first_new, second_new = adam_direction(weight, gradient * factor, first, second, decay_flags[i])
        if i < 2:
            direction = weight - LEARN_RATE * direction
        results.extend((direction, first_new, second_new))
    return (out_tokens[None], grad_tokens[None]) + tuple(results)


def solution(mesh):
    rows3 = P(("dp", "fsdp"), None, None)
    both, split, last = P("fsdp", "dp"), P("fsdp"), P(None, "fsdp")
    small = (split, split, last, split, split, split, split)
    placed = (rows3, rows3, P(("dp", "fsdp"), None), P(("dp", "fsdp")), both, both) + small
    placed = placed + (both,) * 4 + tuple(s for s in small for _ in range(2))
    out = (rows3, rows3) + (both,) * 6 + tuple(s for s in small for _ in range(3))
    return jax.shard_map(shards, mesh=mesh, in_specs=placed, out_specs=out, check_vma=False)
```
